32 devices in a mesh: gx: 4 (over y, x), gy: 2 (over core), gz: 4 (over z).
Axes of the slice: x: 2, y: 2, z: 4, core: 2. Of those that a mesh axis runs over, the one named last changes fastest.
Arguments:
- tokens: bfloat16 [128, 328, 384], P(('gx', 'gy', 'gz')), may hold values from -6 to 6
- cotangent: bfloat16 [128, 328, 384], P(('gx', 'gy', 'gz')), may hold values from -6 to 6
- groups: int32 [128], P(('gx', 'gy', 'gz')), may hold values from 0 to 2
- keep_mask: int32 [128, 328], P(('gx', 'gy', 'gz')), may hold values from 0 to 1, as said below
- params: float32 [2015330], replicated, as said below
- momentum: float32 [2015330], replicated, as said below
- average: float32 [2015330], replicated, as said below
Outputs:
- mixed: bfloat16 [128, 328, 384], P(('gx', 'gy', 'gz'))
- input_gradient: bfloat16 [128, 328, 384], P(('gx', 'gy', 'gz'))
- ratio_loss: float32 [], replicated
- new_params: float32 [2015330], replicated
- new_momentum: float32 [2015330], replicated
- new_average: float32 [2015330], replicated
- block_vector_grads: float32 [4608], replicated
The draws below stay inside these ranges and needn't reach their ends.
Inputs may be any that keep to these rules, and one draw needn't show every extreme that they name: `groups`: an image of group 0, 1 or 2 holds 101, 197 or 325 tokens, the first its class token, padded up to 328. `keep_mask`: 1 keeps a patch token, 0 drops it; position 0 and positions past an image's tokens are not read. `params`: float32 values in the layout of the steps. `momentum`: float32 values in the layout of the steps. `average`: float32 values in the layout of the steps.
All inputs are finite; a program needn't handle non-finite values.
Results may differ from the reference program's by a relative error of at most 0.012.
Values sent between devices are 32-bit elements; how exact they have to be, the bound alone decides.
A program may use at most 192 MiB of HBM per device.

```python
import math
import jax
import jax.numpy as jnp
from jax import lax

D = 384
HEADS = 6
MLP = 1536
IMG_DEV = 4
SLOT = 328
LEN_A = 101
LEN_B = 197
LEN_C = 325
IMAGES = 128
TOKENS_ALL = 41984
NPARAM = 2015330
N_GX = 4
N_GY = 2
N_GZ = 4


def section_kinds():
    halfway = D // 2
    quarter = D // 4
    return [(D * D, D ** (-0.5), 0.0, 0), (D * halfway, D ** (-0.5), 0.0, 0), (halfway * quarter, halfway ** (-0.5), 0.0, 0), (quarter * 2, quarter ** (-0.5), 0.0, 0), (3 * D * D, D ** (-0.5), 0.0, 1), (D * D, 6.0 * D ** (-0.5), 0.0, 1), (D * MLP, D ** (-0.5), 0.0, 1), (MLP * D, MLP ** (-0.5), 0.0, 1), (D, 0.15, 1.0, 0), (D, 0.2, 0.0, 0), (D, 0.2, 0.0, 0), (halfway, 0.2, 0.0, 0), (quarter, 0.2, 0.0, 0), (2, 0.2, 0.0, 0), (D, 0.15, 1.0, 1), (D, 0.2, 0.0, 1), (D, 0.2, 0.0, 1), (D, 0.2, 0.0, 1), (D, 0.2, 0.0, 1), (D, 0.15, 1.0, 1), (D, 0.2, 0.0, 1), (MLP, 0.2, 0.0, 1), (D, 0.2, 0.0, 1)]


def layout_factors(gradient_size):
    scale_parts = []
    offset_parts = []
    for amount, scale_value, offset_value, owner in section_kinds():
        if gradient_size > 0.0:
            scale_value = gradient_size * (0.4 if owner == 1 else 0.05)
            offset_value = 0.0
        scale_parts.append(jnp.full((amount,), scale_value, jnp.float32))
        offset_parts.append(jnp.full((amount,), offset_value, jnp.float32))
    return (jnp.concatenate(scale_parts), jnp.concatenate(offset_parts))


def draw_params(key, part):
    key = jax.random.fold_in(key, 11)
    unit_noise = jax.random.normal(key, (NPARAM,), jnp.float32)
    scales, offsets = layout_factors(0.0)
    return offsets + scales * unit_noise


def draw_average(key, part):
    key = jax.random.fold_in(key, 12)
    unit_noise = jax.random.normal(key, (NPARAM,), jnp.float32)
    scales, offsets = layout_factors(0.0)
    return offsets + scales * unit_noise


def draw_momentum(key, part):
    key = jax.random.fold_in(key, 13)
    unit_noise = jax.random.normal(key, (NPARAM,), jnp.float32)
    scales, offsets = layout_factors(math.sqrt(TOKENS_ALL))
    return offsets + scales * unit_noise


def draw_keep_mask(key, part):
    key = jax.random.fold_in(key, 21)
    span_x = max(N_GX - 1, 1)
    span_y = max(N_GY - 1, 1)
    span_z = max(N_GZ - 1, 1)
    device = jnp.arange(IMAGES, dtype=jnp.int32) // IMG_DEV
    coord_x = device // (N_GY * N_GZ)
    coord_y = device // N_GZ % N_GY
    coord_z = device % N_GZ
    permille = 950 * (span_x + 2 * coord_x) * (span_y + 2 * coord_y) * (span_z + 2 * coord_z) // (27 * span_x * span_y * span_z)
    rolled = jax.random.randint(key, (IMAGES, SLOT), 0, 1000, dtype=jnp.int32)
    return (rolled < permille[:, None]).astype(jnp.int32)


def set_ends(values, key, least, largest):
    longest = values.shape.index(max(values.shape))
    spots = []
    for shift in (0, 1):
        where = [jax.random.randint(jax.random.fold_in(key, axis), (), 0, length) for axis, length in enumerate(values.shape)]
        where[longest] = (where[longest] + shift) % values.shape[longest]
        spots.append(tuple(where))
    return values.at[spots[0]].set(least).at[spots[1]].set(largest)


def levels(own_key, dims, cuts, smallest, top_value):
    factor_of = 1.0
    for dim, shards_of in cuts:
        heights = jax.random.uniform(jax.random.fold_in(jax.random.fold_in(own_key, 6), dim), (shards_of,), jnp.float32, smallest / len(cuts), top_value / len(cuts))
        factor_of = factor_of * jnp.repeat(jnp.exp(heights), dims[dim] // shards_of).reshape((-1,) + (1,) * (len(dims) - 1 - dim))
    return factor_of


def gaussian(stream_key, dims, scale, reach, shards=(), held_as=jnp.bfloat16):
    entries = jax.random.normal(stream_key, dims, jnp.float32) * scale
    if len(shards) > 0:
        entries = levels(stream_key, dims, shards, -0.22, 0.18) * entries
    return jnp.clip(entries, min=-reach, max=reach).astype(held_as)


def setup_inputs(seed: int = 0) -> dict:
    arg_keys = jax.random.split(jax.random.key(seed), 8)
    tokens = gaussian(arg_keys[0], (IMAGES, SLOT, D), 1.0, 6.0, ((0, 32),))
    cotangent = gaussian(arg_keys[1], (IMAGES, SLOT, D), 1.0, 6.0, ((0, 32),))
    groups = set_ends(jax.random.randint(arg_keys[2], (IMAGES,), 0, 3), jax.random.fold_in(arg_keys[2], 1), 0, 2).astype(jnp.int32)
    keep_mask = draw_keep_mask(jax.random.fold_in(arg_keys[7], 71), 0)
    params = draw_params(jax.random.fold_in(arg_keys[7], 71), 0)
    momentum = draw_momentum(jax.random.fold_in(arg_keys[7], 71), 0)
    average = draw_average(jax.random.fold_in(arg_keys[7], 71), 0)
    return dict(tokens=tokens, cotangent=cotangent, groups=groups, keep_mask=keep_mask, params=params, momentum=momentum, average=average)


NORM_EPS = 1e-06
RATIO_WEIGHT = 2.0
KEEP_TARGET = 0.7
MOMENTUM_DECAY = 0.5
AVERAGE_DECAY = 0.5
LEARN_RATE = 0.0001

@jax.custom_vjp
def low(v):
    return lax.optimization_barrier(v.astype(jnp.bfloat16)).astype(jnp.float32)

@jax.custom_vjp
def low_back(v):
    return v

def low_keep(v):
    return (low(v), None)

def low_pass(kept, grad):
    return (grad,)

def back_keep(v):
    return (v, None)

def back_low(kept, grad):
    return (low(grad),)
low.defvjp(low_keep, low_pass)
low_back.defvjp(back_keep, back_low)

def sections():
    halfway = D // 2
    quarter = D // 4
    return [('pred_in', (D, D)), ('pred_mid', (D, halfway)), ('pred_low', (halfway, quarter)), ('pred_out', (quarter, 2)), ('attn_in', (D, 3 * D)), ('attn_out', (D, D)), ('mlp_up', (D, MLP)), ('mlp_down', (MLP, D)), ('pred_gain', (D,)), ('pred_shift', (D,)), ('pred_in_bias', (D,)), ('pred_mid_bias', (halfway,)), ('pred_low_bias', (quarter,)), ('pred_out_bias', (2,)), ('norm_one_gain', (D,)), ('norm_one_shift', (D,)), ('query_bias', (D,)), ('value_bias', (D,)), ('attn_out_bias', (D,)), ('norm_two_gain', (D,)), ('norm_two_shift', (D,)), ('mlp_up_bias', (MLP,)), ('mlp_down_bias', (D,))]

def unpack(flat_vector):
    weight_table = {}
    offset = 0
    for section_name, section_shape in sections():
        amount = math.prod(section_shape)
        weight_table[section_name] = flat_vector[offset:offset + amount].reshape(section_shape)
        offset = offset + amount
    return weight_table

def highest_dot(operand, matrix):
    return jnp.einsum('...k,kn->...n', operand, matrix, precision=lax.Precision.HIGHEST)

def smooth(values):
    return jax.nn.gelu(values, approximate=False)

def layer_norm(values, norm_gain, norm_shift):
    centered = values - lax.optimization_barrier(jnp.mean(values, -1, keepdims=True))
    spread = lax.optimization_barrier(jnp.mean(centered * centered, -1, keepdims=True))
    return centered * lax.rsqrt(spread + NORM_EPS) * norm_gain + norm_shift

def predictor(hidden, weight_table, spatial):
    halfway = D // 2
    normed = low(layer_norm(hidden, weight_table['pred_gain'], weight_table['pred_shift']))
    activated = smooth(low_back(highest_dot(normed, low(weight_table['pred_in'])) + weight_table['pred_in_bias']))
    spatial_total = lax.optimization_barrier(jnp.sum(spatial, 1))[:, None, None]
    global_mean = lax.optimization_barrier(jnp.sum(activated[..., halfway:] * spatial[..., None], axis=1, keepdims=True)) / spatial_total
    joined = low(jnp.concatenate([activated[..., :halfway], jnp.broadcast_to(global_mean, activated[..., halfway:].shape)], -1))
    middle = low(smooth(low_back(highest_dot(joined, low(weight_table['pred_mid'])) + weight_table['pred_mid_bias'])))
    lower = low(smooth(low_back(highest_dot(middle, low(weight_table['pred_low'])) + weight_table['pred_low_bias'])))
    logits = low_back(highest_dot(lower, low(weight_table['pred_out'])) + weight_table['pred_out_bias'])
    return jnp.exp(jax.nn.log_softmax(logits, -1)[..., 0])

def vit_block(hidden, weight_table, policy, valid_mask):
    head_dim = D // HEADS
    normed = low(layer_norm(hidden, weight_table['norm_one_gain'], weight_table['norm_one_shift']))
    projected = highest_dot(normed, low(weight_table['attn_in']))
    head_shape = hidden.shape[:2] + (HEADS, head_dim)
    queries = low(low_back(projected[..., :D] + weight_table['query_bias'])).reshape(head_shape)
    keys_all = low(low_back(projected[..., D:2 * D])).reshape(head_shape)
    values_all = low(low_back(projected[..., 2 * D:] + weight_table['value_bias'])).reshape(head_shape)
    scores = low_back(jnp.einsum('bihd,bjhd->bhij', queries, keys_all, precision=lax.Precision.HIGHEST) * head_dim ** (-0.5))
    diagonal = jnp.eye(SLOT, dtype=jnp.float32)
    key_weight = policy[:, None, None, :] + (1.0 - policy)[:, None, None, :] * diagonal
    row_max = lax.optimization_barrier(jnp.max(scores, -1, keepdims=True))
    weighted = jnp.exp(scores - row_max) * key_weight
    attention = weighted / lax.optimization_barrier(jnp.sum(weighted, -1, keepdims=True))
    heads_out = low(low_back(jnp.einsum('bhij,bjhd->bihd', low(attention), values_all, precision=lax.Precision.HIGHEST)))
    joined = heads_out.reshape(hidden.shape)
    after_attn = hidden + low_back(highest_dot(joined, low(weight_table['attn_out'])) + weight_table['attn_out_bias'])
    normed_two = low(layer_norm(after_attn, weight_table['norm_two_gain'], weight_table['norm_two_shift']))
    upper = smooth(low_back(highest_dot(normed_two, low(weight_table['mlp_up'])) + weight_table['mlp_up_bias']))
    after_mlp = after_attn + low_back(highest_dot(low(upper), low(weight_table['mlp_down'])) + weight_table['mlp_down_bias'])
    return after_mlp * valid_mask[..., None]

def reference(tokens, cotangent, groups, keep_mask, params, momentum, average):
    position = jnp.arange(SLOT, dtype=jnp.int32)[None, :]
    lengths = jnp.where(groups == 0, LEN_A, jnp.where(groups == 1, LEN_B, LEN_C)).astype(jnp.int32)
    valid_mask = (position < lengths[:, None]).astype(jnp.float32)
    spatial = valid_mask * (position > 0).astype(jnp.float32)
    first_token = jnp.broadcast_to((position == 0).astype(jnp.float32), valid_mask.shape)
    hard_keep = keep_mask.astype(jnp.float32)
    block_count = IMAGES // IMG_DEV

    def split_blocks(values):
        return values.reshape((block_count, IMG_DEV) + values.shape[1:])
    hidden_in = tokens.astype(jnp.float32)
    fixed_table = unpack(params)
    scanned = (split_blocks(hidden_in), split_blocks(hard_keep), split_blocks(valid_mask), split_blocks(spatial), split_blocks(first_token))

    def whole(hidden_all, flat_params):
        weight_table = unpack(flat_params)
        blocks_hidden = split_blocks(hidden_all)

        def run_block(carried, block_item):
            block_hidden, held_hidden, block_hard, block_valid, block_spatial, block_first = block_item
            keep_prob = predictor(block_hidden, weight_table, block_spatial)
            held_prob = predictor(held_hidden, fixed_table, block_spatial)
            policy = block_first + block_spatial * (block_hard + keep_prob - held_prob)
            output = vit_block(block_hidden, weight_table, policy, block_valid)
            return (carried, (output, jnp.sum(block_spatial * policy)))
        _, (outputs, kept) = lax.scan(jax.checkpoint(run_block), jnp.zeros((), jnp.float32), (blocks_hidden,) + scanned)
        total_kept = jnp.sum(kept)
        total_valid = jnp.sum(spatial)
        excess = total_kept / total_valid - KEEP_TARGET
        loss_value = RATIO_WEIGHT * total_valid * excess * excess
        return (outputs.reshape(IMAGES, SLOT, D), loss_value)
    (mixed, loss_value), pullback = jax.vjp(whole, hidden_in, params)
    grad_hidden, grad_params = pullback((cotangent.astype(jnp.float32), jnp.ones_like(loss_value)))
    new_momentum = MOMENTUM_DECAY * momentum + grad_params
    new_params = params - LEARN_RATE * (grad_params + MOMENTUM_DECAY * new_momentum)
    new_average = AVERAGE_DECAY * average + (1.0 - AVERAGE_DECAY) * new_params
    block_vector_grads = grad_params[NPARAM - (8 * D + MLP):]
    return (mixed.astype(jnp.bfloat16), grad_hidden.astype(jnp.bfloat16), loss_value, new_params, new_momentum, new_average, block_vector_grads)
```

```python
import functools
import math

import jax
import jax.numpy as jnp
from jax import lax
from jax.experimental import pallas as pl
from jax.experimental.pallas import tpu as pltpu
from jax.sharding import PartitionSpec as P

MESH = pl.DeviceIdType.MESH
F32 = jnp.float32
BF16 = jnp.bfloat16

D = 384
HEADS = 6
PAIRS = 3
MLP = 1536
LEN_A, LEN_B, LEN_C = 101, 197, 325
IMG = 4
SLOT = 328
ROWS = 336
WIDE = 384
ALL = IMG * ROWS
NPARAM = 2015330
NORM_EPS = 1e-06
RATIO_WEIGHT = 2.0
KEEP_TARGET = 0.7
MOMENTUM_DECAY = 0.5
AVERAGE_DECAY = 0.5
LEARN_RATE = 0.0001

ROW_MID = 1152
ROW_LOW = 1728
ROW_OUT = 1872
ROW_QKV = 1874
ROW_PROJ = 5330
ROW_UP = 6482
ROW_DOWN = 11090
ROW_VEC = 15698
ROW_BLOCK = 15710
EARLY_BASE = 5328
EARLY_ROWS = 10376
FLAT_ROWS = 15752


def dot_nn(a, b):
    return lax.dot_general(a, b, (((1,), (0,)), ((), ())), preferred_element_type=F32)


def dot_nt(a, b):
    return lax.dot_general(a, b, (((1,), (1,)), ((), ())), preferred_element_type=F32)


def dot_tn(a, b):
    return lax.dot_general(a, b, (((0,), (0,)), ((), ())), preferred_element_type=F32)


def iota(shape, axis):
    return lax.broadcasted_iota(jnp.int32, shape, axis)


def gelu_pair(v):
    gauss = jnp.exp(v * v * -0.5)
    t = 1.0 / (1.0 + 0.2316418882663604 * jnp.abs(v))
    poly = 0.5 * 1.061405429
    for coefficient in (-1.453152027, 1.421413741, -0.284496736, 0.254829592):
        poly = poly * t + 0.5 * coefficient
    tail = poly * t * gauss
    cdf = jnp.where(v >= 0.0, 1.0 - tail, tail)
    return v * cdf, cdf + v * gauss * 0.3989422804014327


def normalise(x):
    mean = jnp.sum(x, -1, keepdims=True) * (1.0 / D)
    centered = x - mean
    spread = jnp.sum(centered * centered, -1, keepdims=True) * (1.0 / D)
    rstd = lax.rsqrt(spread + NORM_EPS)
    return centered * rstd, rstd


def normalise_back(grad, gain, xhat, rstd):
    scaled = grad * gain
    first = jnp.sum(scaled, -1, keepdims=True) * (1.0 / D)
    second = jnp.sum(scaled * xhat, -1, keepdims=True) * (1.0 / D)
    return rstd * (scaled - first - xhat * second)


def column_sum(x):
    return jnp.sum(x, 0, keepdims=True)


def load_padded(ref, b):
    x = ref[b].astype(F32)
    return jnp.concatenate([x, jnp.zeros((ROWS - SLOT, D), F32)], 0)


def length_of(groups, b):
    g = groups[b]
    return jnp.where(g == 0, LEN_A, jnp.where(g == 1, LEN_B, LEN_C))


def policy_lanes(keep, length, b):
    row = keep[pl.ds(b, 1), :].astype(F32)
    row = jnp.concatenate([row, jnp.zeros((1, WIDE - SLOT), F32)], 1)
    kept = jnp.broadcast_to(row, (128, WIDE)).T[:ROWS]
    position = iota((ROWS, 128), 0)
    return jnp.where(position == 0, 1.0, jnp.where(position < length, kept, 0.0))


def split_heads(tile):
    left = iota(tile.shape, 1) < 64
    zero = jnp.zeros_like(tile)
    return jnp.concatenate([jnp.where(left, tile, zero), jnp.where(left, zero, tile)], 0)


def diagonal_blocks(x):
    return jnp.concatenate([x[:64, :128], x[64:, 128:]], 0)


def put(ref, base, stride, value):
    rows, columns = value.shape
    for c in range(columns // 128):
        ref[pl.ds(base + c, rows, stride=stride), :] = value[:, c * 128 : (c + 1) * 128]


def put_row(ref, base, value):
    for c in range(value.shape[1] // 128):
        ref[base + c : base + c + 1, :] = value[:, c * 128 : (c + 1) * 128]


def row_of(ref, base, count):
    return jnp.concatenate([ref[base + c : base + c + 1, :] for c in range(count)], 1)


def shifted(ref, base, rows, stride):
    first = ref[pl.ds(base, rows, stride=stride), :]
    second = ref[pl.ds(base + 1, rows, stride=stride), :]
    low = iota((rows, 128), 1) < 64
    return pltpu.roll(jnp.where(low, second, first), 64, 1)


def forward_kernel(
    groups, tokens, cotangent, keep, flat,
    mixed, q_out, k_out, v_out, do_out, dx_out, lse_out, qkv_w_out, in_w_out, small_out, vec_out, early, early_vec,
    flat_one, flat_two, w_qkv, w_proj, w_up, w_down, vecs, v_turned, o_turned, weight, n2_all, gd_all, up_all, gup_all,
    acc_proj, acc_vec, sem,
):
    copy = pltpu.make_async_copy(flat, flat_one, sem)
    copy.start()
    copy.wait()

    def spread(i, _):
        flat_two[pl.ds(pl.multiple_of(i * 384, 384), 384), :] = flat_one[
            pl.ds(pl.multiple_of(i * 49152, 49152), 49152)
        ].reshape(384, 128)
        return 0

    lax.fori_loop(0, 41, spread, 0)
    flat_two[15744:15745, 0:98] = flat_one[pl.ds(15744 * 128, 98)].reshape(1, 98)

    for c in range(3):
        in_w_out[:, c * 128 : (c + 1) * 128] = flat_two[pl.ds(c, D, stride=3), :].astype(BF16)
    for c in range(9):
        tile = shifted(flat_two, ROW_QKV - 1 + c, D, 9).astype(BF16)
        w_qkv[:, c * 128 : (c + 1) * 128] = tile
        qkv_w_out[:, c * 128 : (c + 1) * 128] = tile
    for c in range(3):
        w_proj[:, c * 128 : (c + 1) * 128] = shifted(flat_two, ROW_PROJ - 1 + c, D, 3).astype(BF16)
    for n in range(4):
        for c in range(3):
            w_up[n, :, c * 128 : (c + 1) * 128] = shifted(flat_two, ROW_UP - 1 + 3 * n + c, D, 12).astype(BF16)
            w_down[n, :, c * 128 : (c + 1) * 128] = shifted(flat_two, ROW_DOWN - 1 + 1152 * n + c, D, 3).astype(BF16)
    small_out[0 : ROW_OUT - ROW_MID + 8, :] = flat_two[ROW_MID : ROW_OUT + 8, :]
    lane = iota((16, 128), 1)
    vec_out[0:16, :] = pltpu.roll(
        jnp.where(lane < 64, flat_two[15698:15714, :], flat_two[15697:15713, :]), 64, 1
    )
    lane = iota((36, 128), 1)
    vec_out[16:52, :] = pltpu.roll(
        jnp.where(lane < 98, flat_two[15709:15745, :], flat_two[15708:15744, :]), 30, 1
    )
    for r in range(12):
        vecs[r : r + 1, :] = row_of(vec_out, 16 + 3 * r, 3)

    def vec(r):
        return vecs[r : r + 1, :]

    acc_proj[...] = jnp.zeros_like(acc_proj)
    acc_vec[...] = jnp.zeros_like(acc_vec)

    def image(b, _):
        length = length_of(groups, b)
        x = load_padded(tokens, b)
        xhat, _ = normalise(x)
        n1 = (xhat * vec(0) + vec(1)).astype(BF16)
        zeros = jnp.zeros((WIDE - ROWS, 128), BF16)
        q = (dot_nn(n1, w_qkv[:, 0:D]) + vec(2)).astype(BF16) * jnp.array(0.125, BF16)
        for p in range(PAIRS):
            q_out[b, p] = jnp.concatenate([q[:, p * 128 : (p + 1) * 128], zeros], 0)
        k = dot_nn(n1, w_qkv[:, D : 2 * D]).astype(BF16)
        for p in range(PAIRS):
            k_out[b, p] = k[:, p * 128 : (p + 1) * 128]
        v = dot_nn(n1, w_qkv[:, 2 * D : 3 * D]) + vec(3)
        for p in range(PAIRS):
            v_pair = v[:, p * 128 : (p + 1) * 128]
            v_out[b, p] = v_pair.astype(BF16)
            v_turned[p] = v_pair.T.astype(BF16)

        policy = policy_lanes(keep, length, b)
        row_id = iota((ROWS, 128), 0)
        lane_id = iota((ROWS, 128), 1)
        for t in range(3):
            weight[t] = jnp.where(row_id == lane_id + 128 * t, 1.0, policy)

        def pair(p, _):
            k_pair = k_out[b, p]
            vt = v_turned[p]
            for t in range(3):
                q_two = split_heads(q_out[b, p, 128 * t : 128 * (t + 1), :])
                s = dot_nt(k_pair, q_two)
                top = jnp.max(s, 0, keepdims=True)
                w = weight[t]
                e = jnp.exp(s - top) * jnp.concatenate([w, w], 1)
                z = jnp.sum(e, 0, keepdims=True)
                lse_out[b, p, t, 0:1, :] = top + jnp.log(z)
                prob = (e * (1.0 / z)).astype(BF16)
                o = diagonal_blocks(dot_nn(vt, prob)).astype(BF16)
                o_turned[pl.ds(pl.multiple_of(p * 128, 128), 128), 128 * t : 128 * (t + 1)] = o
            return 0

        lax.fori_loop(0, PAIRS, pair, 0)

        x1 = x + dot_tn(o_turned[...], w_proj[...])[:ROWS] + vec(4)
        xhat2, rstd2 = normalise(x1)
        n2 = (xhat2 * vec(5) + vec(6)).astype(BF16)
        rows = pl.ds(pl.multiple_of(b * ROWS, 16), ROWS)
        n2_all[rows, :] = n2
        valid = (iota((ROWS, D), 0) < length).astype(F32)
        g = load_padded(cotangent, b) * valid
        g_d = g.astype(BF16)
        gd_all[rows, :] = g_d

        def part(n, carry):
            x2, dn2 = carry
            u_pre = dot_nn(n2, w_up[n]) + vecs[pl.ds(7 + n, 1), :]
            du = dot_nt(g_d, w_down[n])
            u, slope = gelu_pair(u_pre)
            u = u.astype(BF16)
            gu = (slope * du).astype(BF16)
            up_all[n, rows, :] = u
            gup_all[n, rows, :] = gu
            acc_vec[pl.ds(3 + n, 1), :] += column_sum(gu.astype(F32))
            return x2 + dot_nn(u, w_down[n]), dn2 + dot_nt(gu, w_up[n])

        x2, dn2 = lax.fori_loop(0, 4, part, (x1 + vec(11), jnp.zeros((ROWS, D), F32)))
        mixed[b] = (x2 * valid)[:SLOT].astype(BF16)
        acc_vec[7:8, :] += column_sum(g)
        acc_vec[1:2, :] += column_sum(dn2 * xhat2)
        acc_vec[2:3, :] += column_sum(dn2)
        dx1 = g + normalise_back(dn2, vec(5), xhat2, rstd2)
        dx_out[b] = dx1
        g_o = dx1.astype(BF16)
        acc_vec[0:1, :] += column_sum(g_o.astype(F32))
        acc_proj[...] += dot_nn(o_turned[...], jnp.concatenate([g_o, jnp.zeros((WIDE - ROWS, D), BF16)], 0))
        d_o = dot_nt(g_o, w_proj[...]).astype(BF16)
        for p in range(PAIRS):
            do_out[b, p] = jnp.concatenate([d_o[:, p * 128 : (p + 1) * 128], zeros], 0)
        return 0

    lax.fori_loop(0, IMG, image, 0)

    def finish(n, _):
        put(early, ROW_UP - EARLY_BASE + 3 * n, 12, dot_tn(n2_all[...], gup_all[n]))
        put(early, ROW_DOWN - EARLY_BASE + 1152 * n, 3, dot_tn(up_all[n], gd_all[...]))
        return 0

    lax.fori_loop(0, 4, finish, 0)
    put(early, ROW_PROJ - EARLY_BASE, 3, acc_proj[...])
    for r in range(8):
        put_row(early_vec, 3 * r, acc_vec[r : r + 1, :])


def forward(groups, tokens, cotangent, keep, flat):
    vmem = pl.BlockSpec(memory_space=pltpu.VMEM)
    shape = jax.ShapeDtypeStruct
    return pl.pallas_call(
        forward_kernel,
        out_shape=(
            shape((IMG, SLOT, D), BF16),
            shape((IMG, PAIRS, WIDE, 128), BF16),
            shape((IMG, PAIRS, ROWS, 128), BF16),
            shape((IMG, PAIRS, ROWS, 128), BF16),
            shape((IMG, PAIRS, WIDE, 128), BF16),
            shape((IMG, ROWS, D), F32),
            shape((IMG, PAIRS, 3, 8, 256), F32),
            shape((D, 3 * D), BF16),
            shape((D, D), BF16),
            shape((736, 128), F32),
            shape((56, 128), F32),
            shape((EARLY_ROWS, 128), F32),
            shape((24, 128), F32),
        ),
        in_specs=[pl.BlockSpec(memory_space=pltpu.SMEM), vmem, vmem, vmem, pl.BlockSpec(memory_space=pl.ANY)],
        out_specs=[vmem] * 13,
        scratch_shapes=[
            pltpu.VMEM((NPARAM,), F32),
            pltpu.VMEM((FLAT_ROWS, 128), F32),
            pltpu.VMEM((D, 3 * D), BF16),
            pltpu.VMEM((D, D), BF16),
            pltpu.VMEM((4, D, D), BF16),
            pltpu.VMEM((4, D, D), BF16),
            pltpu.VMEM((16, D), F32),
            pltpu.VMEM((PAIRS, 128, ROWS), BF16),
            pltpu.VMEM((D, WIDE), BF16),
            pltpu.VMEM((3, ROWS, 128), F32),
            pltpu.VMEM((ALL, D), BF16),
            pltpu.VMEM((ALL, D), BF16),
            pltpu.VMEM((4, ALL, D), BF16),
            pltpu.VMEM((4, ALL, D), BF16),
            pltpu.VMEM((D, D), F32),
            pltpu.VMEM((8, D), F32),
            pltpu.SemaphoreType.DMA,
        ],
        compiler_params=pltpu.CompilerParams(vmem_limit_bytes=60 << 20),
        name="forward",
    )(groups, tokens, cotangent, keep, flat)


def backward_kernel(
    groups, tokens, keep, counts, q_in, k_in, v_in, do_in, dx_in, lse_in, w_qkv, w_in, small, vec_in, early, early_vec,
    input_gradient, grads,
    w_mid, w_low, w_out, vecs, mid_one, mid_two, low_one, weight, away, acc_policy, n1_all, h0_all, ga_all, z_all,
    g1_all, m1_all, g2_all, m2_all, gl_all, dqkv_all, acc_vec, acc_small,
):
    lane = iota((192, 128), 1)
    a, b, c = (small[pl.ds(s, 192, stride=3), :] for s in range(3))
    zero = jnp.zeros((192, 128), F32)
    mid_one[pl.ds(0, 192, stride=2), :] = a
    mid_one[pl.ds(1, 192, stride=2), :] = pltpu.roll(jnp.where(lane < 64, c, b), 64, 1)
    mid_two[pl.ds(0, 192, stride=2), :] = jnp.where(lane < 64, b, zero)
    mid_two[pl.ds(1, 192, stride=2), :] = jnp.where(lane < 64, pltpu.roll(c, 64, 1), zero)
    w_mid[:, 0:128] = mid_one[...].astype(BF16)
    w_mid[:, 128:256] = mid_two[...].astype(BF16)
    lane = iota((48, 128), 1)
    base = ROW_LOW - ROW_MID
    a, b, c = (small[pl.ds(base + s, 48, stride=3), :] for s in range(3))
    zero = jnp.zeros((48, 128), F32)
    low_one[192:256, :] = jnp.zeros((64, 128), F32)
    for s, tile in enumerate(
        (
            a,
            jnp.where(lane < 32, pltpu.roll(a, 32, 1), pltpu.roll(b, 32, 1)),
            jnp.where(lane < 64, pltpu.roll(b, 64, 1), pltpu.roll(c, 64, 1)),
            pltpu.roll(c, 96, 1),
        )
    ):
        low_one[pl.ds(s, 48, stride=4), :] = jnp.where(lane < 96, tile, zero)
    w_low[...] = low_one[...].astype(BF16)
    base = ROW_OUT - ROW_MID
    head = jnp.concatenate([small[base : base + 1, :], small[base + 1 : base + 2, :]], 1)
    head = jnp.broadcast_to(head, (128, 256))
    lane = iota((128, 256), 1)
    chosen = (lane % 2 == iota((128, 256), 0)) & (lane < 192)
    doubled = (iota((128, 256), 1) // 2 == iota((128, 256), 0)).astype(F32).astype(BF16)
    w_out[...] = dot_nt(jnp.where(chosen, head, 0.0).astype(BF16), doubled).astype(BF16)
    for r in range(3):
        vecs[r : r + 1, :] = row_of(vec_in, 3 * r, 3)
    lane = iota((1, 128), 1)
    zero = jnp.zeros((1, 128), F32)
    r9, r10, r11 = (vec_in[r : r + 1, :] for r in (9, 10, 11))
    vecs[3:4, 0:128] = r9
    vecs[3:4, 128:256] = jnp.where(lane < 64, r10, zero)
    vecs[4:5, 0:128] = jnp.where(lane < 96, pltpu.roll(jnp.where(lane < 64, r11, r10), 64, 1), zero)
    vecs[5:6, 0:128] = jnp.where(lane < 2, pltpu.roll(r11, 96, 1), zero)
    vecs[6:7, :] = row_of(vec_in, 16, 3)
    vecs[7:8, :] = row_of(vec_in, 19, 3)
    coefficient = counts[2:3, 0:1]

    def vec(r, size=D):
        return vecs[r : r + 1, 0:size]

    acc_vec[...] = jnp.zeros_like(acc_vec)
    acc_small[...] = jnp.zeros_like(acc_small)
    grads[EARLY_BASE : EARLY_BASE + EARLY_ROWS, :] = early[...]

    def image(b, _):
        length = length_of(groups, b)
        rows = pl.ds(pl.multiple_of(b * ROWS, 16), ROWS)
        policy = policy_lanes(keep, length, b)
        row_id = iota((ROWS, 128), 0)
        lane_id = iota((ROWS, 128), 1)
        for t in range(3):
            same = row_id == lane_id + 128 * t
            weight[t] = jnp.where(same, 1.0, policy)
            away[t] = jnp.where(same, 0.0, 1.0)
        acc_policy[...] = jnp.zeros_like(acc_policy)

        def pair(p, _):
            k_pair = k_in[b, p]
            v_pair = v_in[b, p]
            kt = k_pair.T
            dk = jnp.zeros((ROWS, 128), F32)
            dv = jnp.zeros((ROWS, 128), F32)
            columns = pl.multiple_of(p * 128, 128)
            for t in range(3):
                q_two = split_heads(q_in[b, p, 128 * t : 128 * (t + 1), :])
                do_two = split_heads(do_in[b, p, 128 * t : 128 * (t + 1), :])
                s = dot_nt(k_pair, q_two)
                f = jnp.exp(s - lse_in[b, p, t, 0:1, :])
                w = weight[t]
                prob = f * jnp.concatenate([w, w], 1)
                dp = dot_nt(v_pair, do_two)
                centred = dp - jnp.sum(prob * dp, 0, keepdims=True)
                ds = (prob * centred).astype(BF16)
                dw = f * centred
                acc_policy[...] += (dw[:, :128] + dw[:, 128:]) * away[t]
                dv = dv + dot_nn(prob.astype(BF16), do_two)
                dk = dk + dot_nn(ds, q_two)
                dq = diagonal_blocks(dot_nn(kt, ds)).T * 0.125
                count = min(128, ROWS - 128 * t)
                first = pl.multiple_of(b * ROWS + 128 * t, 16)
                dqkv_all[pl.ds(first, count), pl.ds(columns, 128)] = dq[:count].astype(BF16)
            dqkv_all[rows, pl.ds(columns + D, 128)] = dk.astype(BF16)
            dqkv_all[rows, pl.ds(columns + 2 * D, 128)] = dv.astype(BF16)
            return 0

        lax.fori_loop(0, PAIRS, pair, 0)
        dpolicy = jnp.sum(acc_policy[...], 1, keepdims=True)

        xhat, rstd = normalise(load_padded(tokens, b))
        n1_all[rows, :] = (xhat * vec(6) + vec(7)).astype(BF16)
        h0 = (xhat * vec(0) + vec(1)).astype(BF16)
        h0_all[rows, :] = h0
        position = iota((ROWS, 1), 0)
        spatial = jnp.where((position > 0) & (position < length), 1.0, 0.0)
        share = 1.0 / (length - 1).astype(F32)
        act, act_slope = gelu_pair(dot_nn(h0, w_in[...]) + vec(2))
        pooled = column_sum(act * spatial) * share
        local = iota((ROWS, D), 1) < D // 2
        z = jnp.where(local, act, pooled).astype(BF16)
        z_all[rows, :] = z
        m1, m1_slope = gelu_pair(dot_nn(z, w_mid[...]) + vec(3, 256))
        m1 = m1.astype(BF16)
        m1_all[rows, :] = m1
        m2, m2_slope = gelu_pair(dot_nn(m1, w_low[...]) + vec(4, 128))
        m2 = m2.astype(BF16)
        m2_all[rows, :] = m2
        logits = dot_nt(m2, w_out[...]) + vec(5, 128)
        keep_prob = 1.0 / (1.0 + jnp.exp(logits[:, 1:2] - logits[:, 0:1]))
        drop_prob = 1.0 / (1.0 + jnp.exp(logits[:, 0:1] - logits[:, 1:2]))
        dlog = spatial * (dpolicy + coefficient * spatial) * keep_prob * drop_prob
        lane = iota((ROWS, 128), 1)
        g_l = jnp.where(lane == 0, dlog, jnp.where(lane == 1, -dlog, 0.0)).astype(BF16)
        gl_all[rows, :] = g_l
        g_2 = (m2_slope * dot_nn(g_l, w_out[...])).astype(BF16)
        g2_all[rows, :] = g_2
        g_1 = (m1_slope * dot_nt(g_2, w_low[...])).astype(BF16)
        g1_all[rows, :] = g_1
        dz = dot_nt(g_1, w_mid[...])
        da = jnp.where(local, dz, spatial * share * column_sum(dz))
        g_a = (act_slope * da).astype(BF16)
        ga_all[rows, :] = g_a
        dh0 = dot_nt(g_a, w_in[...])
        acc_vec[0:1, :] += column_sum(dh0 * xhat)
        acc_vec[1:2, :] += column_sum(dh0)
        acc_vec[2:3, :] += column_sum(g_a.astype(F32))
        acc_small[0:1, :] += column_sum(g_1.astype(F32))
        acc_small[1:2, 0:128] += column_sum(g_2.astype(F32))
        acc_small[2:3, 0:128] += column_sum(g_l.astype(F32))
        dqkv = dqkv_all[rows, :]
        acc_vec[5:6, :] += column_sum(dqkv[:, 0:D].astype(F32))
        acc_vec[6:7, :] += column_sum(dqkv[:, 2 * D : 3 * D].astype(F32))
        dn1 = dot_nt(dqkv, w_qkv[...])
        acc_vec[3:4, :] += column_sum(dn1 * xhat)
        acc_vec[4:5, :] += column_sum(dn1)
        total = (
            dx_in[b]
            + normalise_back(dn1, vec(6), xhat, rstd)
            + normalise_back(dh0, vec(0), xhat, rstd)
        )
        input_gradient[b] = total[:SLOT].astype(BF16)
        return 0

    lax.fori_loop(0, IMG, image, 0)

    for n in range(3):
        put(grads, ROW_QKV + 3 * n, 9, dot_tn(n1_all[...], dqkv_all[:, n * D : (n + 1) * D]))
    put(grads, 0, 3, dot_tn(h0_all[...], ga_all[...]))
    grad_mid = dot_tn(z_all[...], g1_all[...])
    mid_one[...] = grad_mid[:, 0:128]
    mid_two[...] = grad_mid[:, 128:256]
    lane = iota((192, 128), 1)
    odd = pltpu.roll(mid_one[pl.ds(1, 192, stride=2), :], 64, 1)
    grads[pl.ds(ROW_MID, 192, stride=3), :] = mid_one[pl.ds(0, 192, stride=2), :]
    grads[pl.ds(ROW_MID + 1, 192, stride=3), :] = jnp.where(lane < 64, mid_two[pl.ds(0, 192, stride=2), :], odd)
    grads[pl.ds(ROW_MID + 2, 192, stride=3), :] = jnp.where(
        lane < 64, odd, pltpu.roll(mid_two[pl.ds(1, 192, stride=2), :], 64, 1)
    )
    low_one[...] = dot_tn(m1_all[...], g2_all[...])
    lane = iota((48, 128), 1)
    r0, r1, r2, r3 = (low_one[pl.ds(s, 48, stride=4), :] for s in range(4))
    r1, r2, r3 = pltpu.roll(r1, 96, 1), pltpu.roll(r2, 64, 1), pltpu.roll(r3, 32, 1)
    grads[pl.ds(ROW_LOW, 48, stride=3), :] = jnp.where(lane < 96, r0, r1)
    grads[pl.ds(ROW_LOW + 1, 48, stride=3), :] = jnp.where(lane < 64, r1, r2)
    grads[pl.ds(ROW_LOW + 2, 48, stride=3), :] = jnp.where(lane < 32, r2, r3)
    m2_doubled = dot_nn(m2_all[...], doubled).astype(BF16)
    both = dot_tn(gl_all[...], m2_doubled)
    head = jnp.where(iota((1, 256), 1) % 2 == 0, both[0:1, :], both[1:2, :])
    lane = iota((1, 128), 1)
    grads[ROW_OUT : ROW_OUT + 1, :] = head[:, 0:128]
    grads[ROW_OUT + 1 : ROW_OUT + 2, :] = pltpu.roll(head[:, 128:256], 64, 1)
    for r in range(3):
        put_row(grads, ROW_VEC + 3 * r, acc_vec[r : r + 1, :])
    low_bias = pltpu.roll(acc_small[1:2, 0:128], 64, 1)
    out_bias = pltpu.roll(acc_small[2:3, 0:128], 32, 1)
    grads[ROW_VEC + 9 : ROW_VEC + 10, :] = acc_small[0:1, 0:128]
    grads[ROW_VEC + 10 : ROW_VEC + 11, :] = jnp.where(lane < 64, acc_small[0:1, 128:256], low_bias)
    grads[ROW_VEC + 11 : ROW_VEC + 12, :] = jnp.where(lane < 32, low_bias, out_bias)
    for r in range(4):
        put_row(grads, ROW_BLOCK + 3 * r, acc_vec[3 + r : 4 + r, :])
    grads[ROW_BLOCK + 12 : ROW_BLOCK + 36, :] = early_vec[...]
    first = ROW_BLOCK + 36
    grads[first:, :] = jnp.zeros((grads.shape[0] - first, 128), F32)


def backward(total_rows, *operands):
    vmem = pl.BlockSpec(memory_space=pltpu.VMEM)
    shape = jax.ShapeDtypeStruct
    return pl.pallas_call(
        backward_kernel,
        out_shape=(shape((IMG, SLOT, D), BF16), shape((total_rows, 128), F32)),
        in_specs=[pl.BlockSpec(memory_space=pltpu.SMEM)] + [vmem] * 15,
        out_specs=[vmem] * 2,
        scratch_shapes=[
            pltpu.VMEM((D, 256), BF16),
            pltpu.VMEM((256, 128), BF16),
            pltpu.VMEM((128, 128), BF16),
            pltpu.VMEM((8, D), F32),
            pltpu.VMEM((D, 128), F32),
            pltpu.VMEM((D, 128), F32),
            pltpu.VMEM((256, 128), F32),
            pltpu.VMEM((3, ROWS, 128), F32),
            pltpu.VMEM((3, ROWS, 128), F32),
            pltpu.VMEM((ROWS, 128), F32),
            pltpu.VMEM((ALL, D), BF16),
            pltpu.VMEM((ALL, D), BF16),
            pltpu.VMEM((ALL, D), BF16),
            pltpu.VMEM((ALL, D), BF16),
            pltpu.VMEM((ALL, 256), BF16),
            pltpu.VMEM((ALL, 256), BF16),
            pltpu.VMEM((ALL, 128), BF16),
            pltpu.VMEM((ALL, 128), BF16),
            pltpu.VMEM((ALL, 128), BF16),
            pltpu.VMEM((ALL, 3 * D), BF16),
            pltpu.VMEM((8, D), F32),
            pltpu.VMEM((8, 256), F32),
        ],
        compiler_params=pltpu.CompilerParams(vmem_limit_bytes=60 << 20),
        name="backward",
    )(*operands)


AXES = ("gx", "gy", "gz")


def peers_of(sizes, axis):
    me = lax.axis_index(axis)
    size = sizes[axis]
    found = []
    for k in range(1, size):
        other = lax.rem(me + k, size)
        found.append((tuple(other if a == axis else lax.axis_index(a) for a in AXES), k - 1, other))
    return found


def greet(sizes):
    barrier = pltpu.get_barrier_semaphore()
    total = 0
    for axis in AXES:
        for device, _, _ in peers_of(sizes, axis):
            pl.semaphore_signal(barrier, inc=1, device_id=device, device_id_type=MESH)
            total += 1
    if total:
        pl.semaphore_wait(barrier, total)


def count_kernel(sizes, groups, keep, out, held, landed, send, recv):
    greet(sizes)
    kept = jnp.zeros((1, 1), F32)
    valid = jnp.zeros((1, 1), F32)
    position = iota((1, SLOT), 1)
    for b in range(IMG):
        spatial = jnp.where((position > 0) & (position < length_of(groups, b)), 1.0, 0.0)
        kept += jnp.sum(spatial * keep[b : b + 1, :].astype(F32), keepdims=True)
        valid += jnp.sum(spatial, keepdims=True)
    row = iota((8, 128), 0)
    held[0] = jnp.where(row == 0, kept, jnp.where(row == 1, valid, 0.0))
    base = 0
    for stage, axis in enumerate(AXES):
        copies = []
        for device, slot, _ in peers_of(sizes, axis):
            copy = pltpu.make_async_remote_copy(
                held.at[stage], landed.at[base + slot], send.at[base + slot], recv.at[base + slot], device, MESH
            )
            copy.start()
            copies.append(copy)
        total = held[stage]
        for slot, copy in enumerate(copies):
            copy.wait()
            total = total + landed[base + slot]
        held[stage + 1] = total
        base += len(copies)
    total = held[len(AXES)]
    excess = total[0:1, :] / total[1:2, :] - KEEP_TARGET
    loss = RATIO_WEIGHT * total[1:2, :] * excess * excess
    out[...] = jnp.where(row == 2, 2.0 * RATIO_WEIGHT * excess, jnp.where(row == 3, loss, total))


def count(sizes, groups, keep):
    copies = max(sum(sizes[a] - 1 for a in AXES), 1)
    return pl.pallas_call(
        functools.partial(count_kernel, sizes),
        out_shape=jax.ShapeDtypeStruct((8, 128), F32),
        in_specs=[pl.BlockSpec(memory_space=pltpu.SMEM), pl.BlockSpec(memory_space=pltpu.VMEM)],
        out_specs=pl.BlockSpec(memory_space=pltpu.VMEM),
        scratch_shapes=[
            pltpu.VMEM((4, 8, 128), F32),
            pltpu.VMEM((copies, 8, 128), F32),
            pltpu.SemaphoreType.DMA((copies,)),
            pltpu.SemaphoreType.DMA((copies,)),
        ],
        compiler_params=pltpu.CompilerParams(collective_id=0, has_side_effects=True),
        name="counts",
    )(groups, keep)


PIECES = (("gy", "gz", "gx"), ("gy", "gx", "gz"), ("gy", "gx", "gz"), ("gy", "gx", "gz"))


def reduce_kernel(sizes, piece_rows, local, out, *scratch):
    held, landed, (rs_send, rs_recv, ag_send, ag_recv) = scratch[:3], scratch[3:6], scratch[6:]
    greet(sizes)

    def rows_after(piece, stage):
        rows = piece_rows
        for axis in PIECES[piece][:stage]:
            rows //= sizes[axis]
        return rows

    def add(target, sources, rows):
        step = math.gcd(rows, 64)

        def body(i, _):
            part = pl.ds(pl.multiple_of(i * step, 8), step)
            total = sources[0][part, :]
            for source in sources[1:]:
                total = total + source[part, :]
            target[part, :] = total
            return 0

        lax.fori_loop(0, rows // step, body, 0)

    def start_scatter(piece, stage):
        axis = PIECES[piece][stage]
        rows = rows_after(piece, stage + 1)
        copies = []
        for device, slot, other in peers_of(sizes, axis):
            begin = pl.multiple_of(other * rows, 8)
            if stage == 0:
                source = local.at[pl.ds(pl.multiple_of(begin + piece * piece_rows, 8), rows), :]
            else:
                source = held[stage - 1].at[piece, pl.ds(begin, rows), :]
            copy = pltpu.make_async_remote_copy(
                source,
                landed[stage].at[piece, slot, pl.ds(0, rows), :],
                rs_send.at[stage, piece, slot],
                rs_recv.at[stage, piece, slot],
                device,
                MESH,
            )
            copy.start()
            copies.append(copy)
        return copies

    def end_scatter(piece, stage, copies):
        axis = PIECES[piece][stage]
        rows = rows_after(piece, stage + 1)
        begin = pl.multiple_of(lax.axis_index(axis) * rows, 8)
        if stage == 0:
            own = local.at[pl.ds(pl.multiple_of(begin + piece * piece_rows, 8), rows), :]
        else:
            own = held[stage - 1].at[piece, pl.ds(begin, rows), :]
        for copy in copies:
            copy.wait()
        sources = [own] + [landed[stage].at[piece, k, pl.ds(0, rows), :] for k in range(len(copies))]
        if stage == 2:
            target = out.at[pl.ds(place(piece, 3), rows), :]
        else:
            target = held[stage].at[piece, pl.ds(0, rows), :]
        add(target, sources, rows)

    def place(piece, stage):
        begin = piece * piece_rows
        for s, axis in enumerate(PIECES[piece][:stage]):
            begin = begin + lax.axis_index(axis) * rows_after(piece, s + 1)
        return pl.multiple_of(begin, 8)

    def start_gather(piece, stage):
        axis = PIECES[piece][stage]
        rows = rows_after(piece, stage + 1)
        block = out.at[pl.ds(place(piece, stage + 1), rows), :]
        copies = []
        for device, slot, _ in peers_of(sizes, axis):
            copy = pltpu.make_async_remote_copy(
                block, block, ag_send.at[stage, piece, slot], ag_recv.at[stage, piece, slot], device, MESH
            )
            copy.start()
            copies.append(copy)
        return copies

    pieces = range(len(PIECES))
    flying = {p: start_scatter(p, 0) for p in pieces}
    for stage in range(3):
        for p in pieces:
            end_scatter(p, stage, flying[p])
            flying[p] = start_scatter(p, stage + 1) if stage < 2 else start_gather(p, 2)
    for stage in (2, 1, 0):
        for p in pieces:
            for copy in flying[p]:
                copy.wait()
            if stage:
                flying[p] = start_gather(p, stage - 1)


def reduce_all(sizes, piece_rows, grads):
    width = max(max(sizes[a] for a in AXES) - 1, 1)
    n = len(PIECES)
    first = piece_rows // sizes["gy"]
    second = first // min(sizes["gx"], sizes["gz"])
    third = first // (sizes["gx"] * sizes["gz"])
    return pl.pallas_call(
        functools.partial(reduce_kernel, sizes, piece_rows),
        out_shape=jax.ShapeDtypeStruct(grads.shape, F32),
        in_specs=[pl.BlockSpec(memory_space=pltpu.VMEM)],
        out_specs=pl.BlockSpec(memory_space=pltpu.VMEM),
        scratch_shapes=[
            pltpu.VMEM((n, first, 128), F32),
            pltpu.VMEM((n, second, 128), F32),
            pltpu.VMEM((n, third, 128), F32),
            pltpu.VMEM((n, max(sizes["gy"] - 1, 1), first, 128), F32),
            pltpu.VMEM((n, max(max(sizes["gx"], sizes["gz"]) - 1, 1), second, 128), F32),
            pltpu.VMEM((n, max(max(sizes["gx"], sizes["gz"]) - 1, 1), third, 128), F32),
            pltpu.SemaphoreType.DMA((3, n, width)),
            pltpu.SemaphoreType.DMA((3, n, width)),
            pltpu.SemaphoreType.DMA((3, n, width)),
            pltpu.SemaphoreType.DMA((3, n, width)),
        ],
        compiler_params=pltpu.CompilerParams(
            collective_id=1, has_side_effects=True, vmem_limit_bytes=60 << 20
        ),
        name="reduce",
    )(grads)


UPDATE_ROWS = 768


def update_kernel(grads, after, params, momentum, average, new_params, new_momentum, new_average, joined):
    i = pl.program_id(0)
    n = UPDATE_ROWS
    joined[0:n, :] = grads[...]
    joined[n : n + 8, :] = after[...]
    here = joined[0:n, :]
    row = iota((n, 128), 0) + i * n
    lane = iota((n, 128), 1)
    moved = pltpu.roll(jnp.where(lane < 64, joined[1 : n + 1, :], here), 64, 1)
    flat = jnp.where(row < ROW_QKV - 1, here, moved)
    joined[0:n, :] = flat

    @pl.when(i == pl.num_programs(0) - 1)
    def _():
        first = 15708 - (NPARAM // (n * 128)) * n
        lane = iota((40, 128), 1)
        one = grads[first + 1 : first + 41, :]
        two = grads[first + 2 : first + 42, :]
        tail = pltpu.roll(jnp.where(lane < 30, two, one), 98, 1)
        keep_old = (iota((40, 128), 0) == 0) & (lane < 98)
        joined[first : first + 40, :] = jnp.where(keep_old, joined[first : first + 40, :], tail)

    g = joined[0:n, :].reshape(n * 128)
    moment = MOMENTUM_DECAY * momentum[...] + g
    value = params[...] - LEARN_RATE * (g + MOMENTUM_DECAY * moment)
    new_momentum[...] = moment
    new_params[...] = value
    new_average[...] = AVERAGE_DECAY * average[...] + (1.0 - AVERAGE_DECAY) * value


def update(grads, params, momentum, average):
    n = UPDATE_ROWS
    flat = pl.BlockSpec((n * 128,), lambda i: (i,))
    out = jax.ShapeDtypeStruct((NPARAM,), F32)
    return pl.pallas_call(
        update_kernel,
        grid=(pl.cdiv(NPARAM, n * 128),),
        out_shape=(out, out, out),
        in_specs=[
            pl.BlockSpec((n, 128), lambda i: (i, 0)),
            pl.BlockSpec((8, 128), lambda i: ((i + 1) * (n // 8), 0)),
            flat,
            flat,
            flat,
        ],
        out_specs=[flat] * 3,
        scratch_shapes=[pltpu.VMEM((n + 8, 128), F32)],
        compiler_params=pltpu.CompilerParams(vmem_limit_bytes=40 << 20),
        name="update",
    )(grads, grads, params, momentum, average)


def solution(mesh):
    sizes = dict(mesh.shape)
    devices = mesh.size
    unit = devices * 8 * len(PIECES)
    total_rows = -(-16136 // unit) * unit

    def per_device(tokens, cotangent, groups, keep_mask, params, momentum, average):
        counts = count(sizes, groups, keep_mask)
        (
            mixed, q, k, v, d_o, dx, lse, w_qkv, w_in, small, vec, early, early_vec,
        ) = forward(groups, tokens, cotangent, keep_mask, params)
        input_gradient, grads = backward(
            total_rows, groups, tokens, keep_mask, counts, q, k, v, d_o, dx, lse, w_qkv, w_in, small, vec, early,
            early_vec,
        )
        grads = reduce_all(sizes, total_rows // len(PIECES), grads)
        new_params, new_momentum, new_average = update(grads, params, momentum, average)
        block = grads[ROW_BLOCK : ROW_BLOCK + 36].reshape(-1)
        return (mixed, input_gradient, counts[3, 0], new_params, new_momentum, new_average, block)

    split = P(("gx", "gy", "gz"))
    return jax.shard_map(
        per_device,
        mesh=mesh,
        in_specs=(split, split, split, split, P(), P(), P()),
        out_specs=(split, split, P(), P(), P(), P(), P()),
        check_vma=False,
    )
```

```python
import functools
import math

import jax
import jax.numpy as jnp
from jax import lax
from jax.experimental import pallas as pl
from jax.experimental.pallas import tpu as pltpu
from jax.sharding import PartitionSpec as P

MESH = pl.DeviceIdType.MESH
F32 = jnp.float32
BF16 = jnp.bfloat16

D = 384
HEADS = 6
PAIRS = 3
MLP = 1536
LEN_A, LEN_B, LEN_C = 101, 197, 325
IMG = 4
SLOT = 328
ROWS = 336
WIDE = 384
ALL = IMG * ROWS
NPARAM = 2015330
NORM_EPS = 1e-06
RATIO_WEIGHT = 2.0
KEEP_TARGET = 0.7
MOMENTUM_DECAY = 0.5
AVERAGE_DECAY = 0.5
LEARN_RATE = 0.0001

ROW_MID = 1152
ROW_LOW = 1728
ROW_OUT = 1872
ROW_QKV = 1874
ROW_PROJ = 5330
ROW_UP = 6482
ROW_DOWN = 11090
ROW_VEC = 15698
ROW_BLOCK = 15710
EARLY_BASE = 5328
EARLY_ROWS = 10376
FLAT_ROWS = 15752


def dot_nn(a, b):
    return lax.dot_general(a, b, (((1,), (0,)), ((), ())), preferred_element_type=F32)


def dot_nt(a, b):
    return lax.dot_general(a, b, (((1,), (1,)), ((), ())), preferred_element_type=F32)


def dot_tn(a, b):
    return lax.dot_general(a, b, (((0,), (0,)), ((), ())), preferred_element_type=F32)


def iota(shape, axis):
    return lax.broadcasted_iota(jnp.int32, shape, axis)


def gelu_pair(v):
    gauss = jnp.exp(v * v * -0.5)
    t = 1.0 / (1.0 + 0.2316418882663604 * jnp.abs(v))
    poly = 0.5 * 1.061405429
    for coefficient in (-1.453152027, 1.421413741, -0.284496736, 0.254829592):
        poly = poly * t + 0.5 * coefficient
    tail = poly * t * gauss
    cdf = jnp.where(v >= 0.0, 1.0 - tail, tail)
    return v * cdf, cdf + v * gauss * 0.3989422804014327


def normalise(x):
    mean = jnp.sum(x, -1, keepdims=True) * (1.0 / D)
    centered = x - mean
    spread = jnp.sum(centered * centered, -1, keepdims=True) * (1.0 / D)
    rstd = lax.rsqrt(spread + NORM_EPS)
    return centered * rstd, rstd


def normalise_back(grad, gain, xhat, rstd):
    scaled = grad * gain
    first = jnp.sum(scaled, -1, keepdims=True) * (1.0 / D)
    second = jnp.sum(scaled * xhat, -1, keepdims=True) * (1.0 / D)
    return rstd * (scaled - first - xhat * second)


def column_sum(x):
    return jnp.sum(x, 0, keepdims=True)


def load_padded(ref, b):
    x = ref[b].astype(F32)
    return jnp.concatenate([x, jnp.zeros((ROWS - SLOT, D), F32)], 0)


def length_of(groups, b):
    g = groups[b]
    return jnp.where(g == 0, LEN_A, jnp.where(g == 1, LEN_B, LEN_C))


def policy_lanes(keep, length, b):
    row = keep[pl.ds(b, 1), :].astype(F32)
    row = jnp.concatenate([row, jnp.zeros((1, WIDE - SLOT), F32)], 1)
    kept = jnp.broadcast_to(row, (128, WIDE)).T[:ROWS]
    position = iota((ROWS, 128), 0)
    return jnp.where(position == 0, 1.0, jnp.where(position < length, kept, 0.0))


def split_heads(tile):
    left = iota(tile.shape, 1) < 64
    zero = jnp.zeros_like(tile)
    return jnp.concatenate([jnp.where(left, tile, zero), jnp.where(left, zero, tile)], 0)


def diagonal_blocks(x):
    return jnp.concatenate([x[:64, :128], x[64:, 128:]], 0)


def put(ref, base, stride, value):
    rows, columns = value.shape
    for c in range(columns // 128):
        ref[pl.ds(base + c, rows, stride=stride), :] = value[:, c * 128 : (c + 1) * 128]


def put_row(ref, base, value):
    for c in range(value.shape[1] // 128):
        ref[base + c : base + c + 1, :] = value[:, c * 128 : (c + 1) * 128]


def row_of(ref, base, count):
    return jnp.concatenate([ref[base + c : base + c + 1, :] for c in range(count)], 1)


def shifted(ref, base, rows, stride):
    first = ref[pl.ds(base, rows, stride=stride), :]
    second = ref[pl.ds(base + 1, rows, stride=stride), :]
    low = iota((rows, 128), 1) < 64
    return pltpu.roll(jnp.where(low, second, first), 64, 1)


AXES = ("gx", "gy", "gz")


def digits(sizes, axis):
    size, stride, found = sizes[axis], 1, []
    while size > 1:
        base = 2 if size % 2 == 0 else size
        found.append((axis, stride, base))
        size //= base
        stride *= base
    return found


def whole(sizes, axis):
    return [(axis, 1, sizes[axis])] if sizes[axis] > 1 else []


def digit_of(stage):
    axis, stride, base = stage
    return lax.rem(lax.axis_index(axis) // stride, base)


def partners(stage):
    axis, stride, base = stage
    mine = digit_of(stage)
    found = []
    for k in range(1, base):
        other = lax.rem(mine + k, base)
        index = lax.axis_index(axis) + (other - mine) * stride
        found.append((tuple(index if a == axis else lax.axis_index(a) for a in AXES), k - 1, other))
    return found


def greet(sizes):
    barrier = pltpu.get_barrier_semaphore()
    total = 0
    for axis in AXES:
        for stage in whole(sizes, axis):
            for device, _, _ in partners(stage):
                pl.semaphore_signal(barrier, inc=1, device_id=device, device_id_type=MESH)
                total += 1
    return barrier, total


class Piece:
    def __init__(self, name, rows, base, stages):
        self.name, self.rows, self.base, self.stages = name, rows, base, stages
        self.copies = sum(s[2] - 1 for s in stages)

    def steps(self, buffer, landing, sems, free, first, first_stage):
        stages = self.stages
        rows_after = [self.rows]
        for stage in stages:
            rows_after.append(rows_after[-1] // stage[2])
        landing_at, sem_at = [self.base], [first]
        for s, stage in enumerate(stages):
            landing_at.append(landing_at[-1] + (stage[2] - 1) * rows_after[s + 1])
            sem_at.append(sem_at[-1] + stage[2] - 1)

        def place(s):
            begin = self.base
            for i in range(s):
                begin = begin + digit_of(stages[i]) * rows_after[i + 1]
            return begin

        def block(s, digit):
            return pl.ds(pl.multiple_of(place(s) + digit * rows_after[s + 1], 8), rows_after[s + 1])

        def scatter(s):
            found = []
            for device, slot, other in partners(stages[s]):
                found.append(
                    pltpu.make_async_remote_copy(
                        buffer.at[block(s, other), :],
                        landing.at[pl.ds(landing_at[s] + slot * rows_after[s + 1], rows_after[s + 1]), :],
                        sems.at[0, sem_at[s] + slot],
                        sems.at[1, sem_at[s] + slot],
                        device,
                        MESH,
                    )
                )
            return found

        def gather(s):
            found = []
            for device, slot, _ in partners(stages[s]):
                own = buffer.at[block(s, digit_of(stages[s])), :]
                found.append(
                    pltpu.make_async_remote_copy(
                        own, own, sems.at[2, sem_at[s] + slot], sems.at[3, sem_at[s] + slot], device, MESH
                    )
                )
            return found

        def start(copies):
            for copy in copies:
                copy.start()

        def end_scatter(s):
            for copy in scatter(s):
                copy.wait()
            for device, _, _ in partners(stages[s]):
                pl.semaphore_signal(free.at[first_stage + s], inc=1, device_id=device, device_id_type=MESH)
            rows = rows_after[s + 1]
            begin = place(s) + digit_of(stages[s]) * rows
            step = math.gcd(rows, 64)

            def body(i, _):
                own = pl.ds(pl.multiple_of(begin + i * step, 8), step)
                total = buffer[own, :]
                for slot in range(stages[s][2] - 1):
                    at = landing_at[s] + slot * rows
                    total = total + landing[pl.ds(pl.multiple_of(at + i * step, 8), step), :]
                buffer[own, :] = total
                return 0

            lax.fori_loop(0, rows // step, body, 0)

        def end_gather(s):
            for copy in gather(s):
                copy.wait()

        count = len(stages)
        found = []
        for s in range(count):

            def there(s=s):
                if s:
                    end_scatter(s - 1)
                start(scatter(s))

            found.append(there)
        for s in reversed(range(count)):

            def back(s=s):
                if s == count - 1:
                    end_scatter(s)
                else:
                    end_gather(s + 1)
                pl.semaphore_wait(free.at[first_stage + s], stages[s][2] - 1)
                start(gather(s))

            found.append(back)
        if count:
            found.append(lambda: end_gather(0))
        return found


def pieces_of(sizes):
    unit = 8 * math.prod(sizes.values())

    def whole_rows(rows):
        return -(-rows // unit) * unit

    core, x, z = digits(sizes, "gy"), digits(sizes, "gx"), digits(sizes, "gz")
    y = x[::-1]
    core_all, x_all, z_all = (whole(sizes, a) for a in ("gy", "gx", "gz"))
    found, base = [], 0
    for name, rows, stages in (
        ("mlp0", 3072, core + z + x),
        ("mlp1", 3072, core + x + z),
        ("mlp2", 3072, core + y + z),
        ("proj", 1152, core + x + z),
        ("qkv0", 1152, core + y + z),
        ("qkv1", 1152, core + x + z),
        ("qkv2", 1152, core_all + z_all + x_all),
        ("pred", 1874, core_all + x_all + z_all),
        ("vecs", 48, core_all + x_all + z_all),
    ):
        found.append(Piece(name, whole_rows(rows), base, stages))
        base += found[-1].rows
    return found, base


PART = 512
PARTS = MLP // PART
HALF = ALL // 2


def layer_kernel(
    sizes, pieces,
    groups, tokens, cotangent, keep, flat, flat_end,
    mixed, input_gradient, grads, counts,
    w_qkv, w_proj, w_up, w_down, w_in, w_mid, w_low, w_out, vecs, qkv_bias,
    q_all, k_all, v_all, do_all, lse_all, v_turned, o_turned, n1_all, dx_all, acc_vec, acc_small,
    buffer, landing, sems, free, held, landed, count_sems, sem,
):
    by_name = {p.name: p for p in pieces}
    plan, first, first_stage = {}, 0, 0
    for p in pieces:
        plan[p.name] = p.steps(buffer, landing, sems, free, first, first_stage)
        first += p.copies
        first_stage += len(p.stages)
    done = {p.name: 0 for p in pieces}

    def take(*names):
        found = []
        for name in names:
            if done[name] < len(plan[name]):
                found.append(plan[name][done[name]])
                done[name] += 1
        return found

    def run(steps):
        for step in steps:
            step()

    barrier, greetings = greet(sizes)
    count_steps = counting(sizes, groups, keep, counts, held, landed, count_sems)

    def weights(flat_one, flat_two):
        unpack(flat, flat_end, flat_one, flat_two, sem, w_qkv, w_proj, w_up, w_down, w_in, w_mid, w_low, w_out, vecs,
               qkv_bias)

    pl.run_scoped(weights, pltpu.VMEM((NPARAM // 1024 * 1024,), F32), pltpu.VMEM((FLAT_ROWS, 128), F32))
    if greetings:
        pl.semaphore_wait(barrier, greetings)
    run(count_steps[:1])

    def vec(r, size=D):
        return vecs[r : r + 1, 0:size]

    acc_vec[...] = jnp.zeros_like(acc_vec)
    acc_small[...] = jnp.zeros_like(acc_small)

    def rows_of(b):
        return pl.ds(pl.multiple_of(b * ROWS, 16), ROWS)

    def first_half(x1_all, x2_all, dn2_all, n2_all, gd_all, up_part, gup_part, go_all, weight):
        def attend(b, _):
            length = length_of(groups, b)
            x = load_padded(tokens, b)
            xhat, _ = normalise(x)
            n1 = (xhat * vec(V_ONE_GAIN) + vec(V_ONE_SHIFT)).astype(BF16)
            n1_all[rows_of(b), :] = n1
            zeros = jnp.zeros((WIDE - ROWS, 128), BF16)
            for p in range(PAIRS):
                part = dot_nn(n1, w_qkv[:, p * D : (p + 1) * D]) + qkv_bias[0:1, p * D : (p + 1) * D]
                q_all[b, p] = jnp.concatenate([part[:, 0:128].astype(BF16) * jnp.array(0.125, BF16), zeros], 0)
                k_all[b, p] = part[:, 128:256].astype(BF16)
                v_all[b, p] = part[:, 256:384].astype(BF16)
                v_turned[p] = part[:, 256:384].T.astype(BF16)

            policy = policy_lanes(keep, length, b)
            row_id = iota((ROWS, 128), 0)
            lane_id = iota((ROWS, 128), 1)
            for t in range(3):
                weight[t] = jnp.where(row_id == lane_id + 128 * t, 1.0, policy)

            def pair(p, _):
                k_pair = k_all[b, p]
                vt = v_turned[p]
                for t in range(3):
                    q_two = split_heads(q_all[b, p, 128 * t : 128 * (t + 1), :])
                    s = dot_nt(k_pair, q_two)
                    top = jnp.max(s, 0, keepdims=True)
                    w = weight[t]
                    e = jnp.exp(s - top) * jnp.concatenate([w, w], 1)
                    total = jnp.sum(e, 0, keepdims=True)
                    lse_all[b, p, t, 0:1, :] = top + jnp.log(total)
                    prob = (e * (1.0 / total)).astype(BF16)
                    o = diagonal_blocks(dot_nn(vt, prob)).astype(BF16)
                    o_turned[b, pl.ds(pl.multiple_of(p * 128, 128), 128), 128 * t : 128 * (t + 1)] = o
                return 0

            lax.fori_loop(0, PAIRS, pair, 0)
            x1 = x + dot_tn(o_turned[b], w_proj[...])[:ROWS] + vec(V_PROJ_BIAS)
            x1_all[rows_of(b), :] = x1
            x2_all[rows_of(b), :] = x1 + vec(V_DOWN_BIAS)
            dn2_all[rows_of(b), :] = jnp.zeros((ROWS, D), F32)
            xhat2, _ = normalise(x1)
            n2_all[rows_of(b), :] = (xhat2 * vec(V_TWO_GAIN) + vec(V_TWO_SHIFT)).astype(BF16)
            valid = (iota((ROWS, D), 0) < length).astype(F32)
            g = load_padded(cotangent, b) * valid
            gd_all[rows_of(b), :] = g.astype(BF16)
            acc_vec[A_DOWN_BIAS : A_DOWN_BIAS + 1, :] += column_sum(g)
            return 0

        lax.fori_loop(0, IMG, attend, 0)
        run(count_steps[1:2])

        for n in range(PARTS):
            columns = slice(n * PART, (n + 1) * PART)

            def mlp(h, _):
                rows = pl.ds(pl.multiple_of(h * HALF, 16), HALF)
                n2 = n2_all[rows, :]
                g_d = gd_all[rows, :]
                u, slope = gelu_pair(dot_nn(n2, w_up[:, columns]) + vecs[V_UP_BIAS : V_UP_BIAS + 1, columns])
                u = u.astype(BF16)
                gu = (slope * dot_nt(g_d, w_down[columns, :])).astype(BF16)
                up_part[rows, :] = u
                gup_part[rows, :] = gu
                acc_small[A_UP_BIAS : A_UP_BIAS + 1, columns] += column_sum(gu.astype(F32))
                x2_all[rows, :] += dot_nn(u, w_down[columns, :])
                dn2_all[rows, :] += dot_nt(gu, w_up[:, columns])
                return 0

            lax.fori_loop(0, 2, mlp, 0)
            base = by_name[f"mlp{n}"].base
            up = dot_tn(n2_all[...], gup_part[...])
            for c in range(PART // 128):
                buffer[base + c * D : base + (c + 1) * D, :] = up[:, c * 128 : (c + 1) * 128]
            put(buffer, base + 1536, 3, dot_tn(up_part[...], gd_all[...]))
            for step in TICKS["part"][n]:
                run(take(*step))

        run(count_steps[2:3])

        def descend(b, _):
            length = length_of(groups, b)
            valid = (iota((ROWS, D), 0) < length).astype(F32)
            mixed[b] = (x2_all[rows_of(b), :] * valid)[:SLOT].astype(BF16)
            xhat2, rstd2 = normalise(x1_all[rows_of(b), :])
            dn2 = dn2_all[rows_of(b), :]
            acc_vec[A_TWO_GAIN : A_TWO_GAIN + 1, :] += column_sum(dn2 * xhat2)
            acc_vec[A_TWO_SHIFT : A_TWO_SHIFT + 1, :] += column_sum(dn2)
            g = load_padded(cotangent, b) * valid
            dx1 = g + normalise_back(dn2, vec(V_TWO_GAIN), xhat2, rstd2)
            dx_all[rows_of(b), :] = dx1
            g_o = dx1.astype(BF16)
            acc_vec[A_PROJ_BIAS : A_PROJ_BIAS + 1, :] += column_sum(g_o.astype(F32))
            go_all[b] = jnp.concatenate([g_o, jnp.zeros((WIDE - ROWS, D), BF16)], 0)
            d_o = dot_nt(g_o, w_proj[...]).astype(BF16)
            zeros = jnp.zeros((WIDE - ROWS, 128), BF16)
            for p in range(PAIRS):
                do_all[b, p] = jnp.concatenate([d_o[:, p * 128 : (p + 1) * 128], zeros], 0)
            return 0

        lax.fori_loop(0, IMG, descend, 0)
        grad_proj = dot_nn(o_turned[0], go_all[0])
        for b in range(1, IMG):
            grad_proj = grad_proj + dot_nn(o_turned[b], go_all[b])
        put(buffer, by_name["proj"].base, 3, grad_proj)
        run(count_steps[3:])
        for step in TICKS["proj"]:
            run(take(*step))

    pl.run_scoped(
        first_half,
        pltpu.VMEM((ALL, D), F32),
        pltpu.VMEM((ALL, D), F32),
        pltpu.VMEM((ALL, D), F32),
        pltpu.VMEM((ALL, D), BF16),
        pltpu.VMEM((ALL, D), BF16),
        pltpu.VMEM((ALL, PART), BF16),
        pltpu.VMEM((ALL, PART), BF16),
        pltpu.VMEM((IMG, WIDE, D), BF16),
        pltpu.VMEM((3, ROWS, 128), F32),
    )
    coefficient = counts[2:3, 0:1]

    def second_half(acc_policy, h0_all, ga_all, z_all, g1_all, m1_all, g2_all, m2_all, gl_all, dqkv_all, mid_one,
                    mid_two, low_one):
        acc_policy[...] = jnp.zeros_like(acc_policy)
        row_id = iota((ROWS, 128), 0)
        lane_id = iota((ROWS, 128), 1)

        for p in range(PAIRS):
            ticks = [[take(*names) for names in step] for step in TICKS["pair"][p]]

            def attend(b, _):
                policy = policy_lanes(keep, length_of(groups, b), b)
                k_pair = k_all[b, p]
                v_pair = v_all[b, p]
                kt = k_pair.T
                dk = jnp.zeros((ROWS, 128), F32)
                dv = jnp.zeros((ROWS, 128), F32)
                for t in range(3):
                    q_two = split_heads(q_all[b, p, 128 * t : 128 * (t + 1), :])
                    do_two = split_heads(do_all[b, p, 128 * t : 128 * (t + 1), :])
                    f = jnp.exp(dot_nt(k_pair, q_two) - lse_all[b, p, t, 0:1, :])
                    same = row_id == lane_id + 128 * t
                    w = jnp.where(same, 1.0, policy)
                    prob = f * jnp.concatenate([w, w], 1)
                    dp = dot_nt(v_pair, do_two)
                    centred = dp - jnp.sum(prob * dp, 0, keepdims=True)
                    ds = (prob * centred).astype(BF16)
                    dw = f * centred
                    acc_policy[b] += jnp.where(same, 0.0, dw[:, :128] + dw[:, 128:])
                    dv = dv + dot_nn(prob.astype(BF16), do_two)
                    dk = dk + dot_nn(ds, q_two)
                    dq = diagonal_blocks(dot_nn(kt, ds)).T * 0.125
                    count = min(128, ROWS - 128 * t)
                    first = pl.multiple_of(b * ROWS + 128 * t, 16)
                    dqkv_all[pl.ds(first, count), p * D : p * D + 128] = dq[:count].astype(BF16)
                dqkv_all[rows_of(b), p * D + 128 : p * D + 256] = dk.astype(BF16)
                dqkv_all[rows_of(b), p * D + 256 : p * D + 384] = dv.astype(BF16)
                for i, steps in enumerate(ticks):
                    if any(steps):

                        @pl.when(b == i)
                        def _():
                            for step in steps:
                                run(step)

                return 0

            lax.fori_loop(0, IMG, attend, 0)
            dqkv = dqkv_all[:, p * D : (p + 1) * D]
            base = by_name[f"qkv{p}"].base
            grad = dot_tn(n1_all[...], dqkv)
            for c in range(3):
                buffer[base + c * D : base + (c + 1) * D, :] = grad[:, c * 128 : (c + 1) * 128]
            bias = column_sum(dqkv.astype(F32))
            acc_vec[A_QUERY_BIAS : A_QUERY_BIAS + 1, p * 128 : (p + 1) * 128] = bias[:, 0:128]
            acc_vec[A_VALUE_BIAS : A_VALUE_BIAS + 1, p * 128 : (p + 1) * 128] = bias[:, 256:384]
            for step in TICKS["qkv"][p]:
                run(take(*step))

        spatial_of, share_of = {}, {}

        def predict(b, _):
            length = length_of(groups, b)
            rows = rows_of(b)
            dpolicy = jnp.sum(acc_policy[b], 1, keepdims=True)
            xhat, _ = normalise(load_padded(tokens, b))
            h0 = (xhat * vec(V_PRED_GAIN) + vec(V_PRED_SHIFT)).astype(BF16)
            h0_all[rows, :] = h0
            position = iota((ROWS, 1), 0)
            spatial = jnp.where((position > 0) & (position < length), 1.0, 0.0)
            share = 1.0 / (length - 1).astype(F32)
            act, act_slope = gelu_pair(dot_nn(h0, w_in[...]) + vec(V_IN_BIAS))
            pooled = column_sum(act * spatial) * share
            local = iota((ROWS, D), 1) < D // 2
            z = jnp.where(local, act, pooled).astype(BF16)
            z_all[rows, :] = z
            m1, m1_slope = gelu_pair(dot_nn(z, w_mid[...]) + vec(V_MID_BIAS, 256))
            m1 = m1.astype(BF16)
            m1_all[rows, :] = m1
            m2, m2_slope = gelu_pair(dot_nn(m1, w_low[...]) + vec(V_LOW_BIAS, 128))
            m2 = m2.astype(BF16)
            m2_all[rows, :] = m2
            logits = dot_nt(m2, w_out[...]) + vec(V_OUT_BIAS, 128)
            keep_prob = 1.0 / (1.0 + jnp.exp(logits[:, 1:2] - logits[:, 0:1]))
            drop_prob = 1.0 / (1.0 + jnp.exp(logits[:, 0:1] - logits[:, 1:2]))
            dlog = spatial * (dpolicy + coefficient * spatial) * keep_prob * drop_prob
            lane = iota((ROWS, 128), 1)
            g_l = jnp.where(lane == 0, dlog, jnp.where(lane == 1, -dlog, 0.0)).astype(BF16)
            gl_all[rows, :] = g_l
            g_2 = (m2_slope * dot_nn(g_l, w_out[...])).astype(BF16)
            g2_all[rows, :] = g_2
            g_1 = (m1_slope * dot_nt(g_2, w_low[...])).astype(BF16)
            g1_all[rows, :] = g_1
            dz = dot_nt(g_1, w_mid[...])
            da = jnp.where(local, dz, spatial * share * column_sum(dz))
            g_a = (act_slope * da).astype(BF16)
            ga_all[rows, :] = g_a
            acc_vec[A_IN_BIAS : A_IN_BIAS + 1, :] += column_sum(g_a.astype(F32))
            acc_small[A_MID_BIAS : A_MID_BIAS + 1, 0:256] += column_sum(g_1.astype(F32))
            acc_small[A_LOW_BIAS : A_LOW_BIAS + 1, 0:128] += column_sum(g_2.astype(F32))
            acc_small[A_OUT_BIAS : A_OUT_BIAS + 1, 0:128] += column_sum(g_l.astype(F32))
            return 0

        lax.fori_loop(0, IMG, predict, 0)
        for step in TICKS["predict"]:
            run(take(*step))

        base = by_name["pred"].base
        put(buffer, base, 3, dot_tn(h0_all[...], ga_all[...]))
        grad_mid = dot_tn(z_all[...], g1_all[...])
        mid_one[...] = grad_mid[:, 0:128]
        mid_two[...] = grad_mid[:, 128:256]
        lane = iota((192, 128), 1)
        odd = pltpu.roll(mid_one[pl.ds(1, 192, stride=2), :], 64, 1)
        buffer[pl.ds(base + ROW_MID, 192, stride=3), :] = mid_one[pl.ds(0, 192, stride=2), :]
        buffer[pl.ds(base + ROW_MID + 1, 192, stride=3), :] = jnp.where(
            lane < 64, mid_two[pl.ds(0, 192, stride=2), :], odd
        )
        buffer[pl.ds(base + ROW_MID + 2, 192, stride=3), :] = jnp.where(
            lane < 64, odd, pltpu.roll(mid_two[pl.ds(1, 192, stride=2), :], 64, 1)
        )
        low_one[...] = dot_tn(m1_all[...], g2_all[...])
        lane = iota((48, 128), 1)
        r0, r1, r2, r3 = (low_one[pl.ds(s, 48, stride=4), :] for s in range(4))
        r1, r2, r3 = pltpu.roll(r1, 96, 1), pltpu.roll(r2, 64, 1), pltpu.roll(r3, 32, 1)
        buffer[pl.ds(base + ROW_LOW, 48, stride=3), :] = jnp.where(lane < 96, r0, r1)
        buffer[pl.ds(base + ROW_LOW + 1, 48, stride=3), :] = jnp.where(lane < 64, r1, r2)
        buffer[pl.ds(base + ROW_LOW + 2, 48, stride=3), :] = jnp.where(lane < 32, r2, r3)
        m2_doubled = dot_nn(m2_all[...], doubling()).astype(BF16)
        both = dot_tn(gl_all[...], m2_doubled)
        head = jnp.where(iota((1, 256), 1) % 2 == 0, both[0:1, :], both[1:2, :])
        buffer[base + ROW_OUT : base + ROW_OUT + 1, :] = head[:, 0:128]
        buffer[base + ROW_OUT + 1 : base + ROW_OUT + 2, :] = pltpu.roll(head[:, 128:256], 64, 1)
        for step in TICKS["pred"]:
            run(take(*step))

        def finish(b, _):
            rows = rows_of(b)
            xhat, rstd = normalise(load_padded(tokens, b))
            dh0 = dot_nt(ga_all[rows, :], w_in[...])
            acc_vec[A_PRED_GAIN : A_PRED_GAIN + 1, :] += column_sum(dh0 * xhat)
            acc_vec[A_PRED_SHIFT : A_PRED_SHIFT + 1, :] += column_sum(dh0)
            dn1 = dot_nt(dqkv_all[rows, :], w_qkv[...])
            acc_vec[A_ONE_GAIN : A_ONE_GAIN + 1, :] += column_sum(dn1 * xhat)
            acc_vec[A_ONE_SHIFT : A_ONE_SHIFT + 1, :] += column_sum(dn1)
            total = (
                dx_all[rows, :]
                + normalise_back(dn1, vec(V_ONE_GAIN), xhat, rstd)
                + normalise_back(dh0, vec(V_PRED_GAIN), xhat, rstd)
            )
            input_gradient[b] = total[:SLOT].astype(BF16)
            return 0

        lax.fori_loop(0, IMG, finish, 0)

    pl.run_scoped(
        second_half,
        pltpu.VMEM((IMG, ROWS, 128), F32),
        pltpu.VMEM((ALL, D), BF16),
        pltpu.VMEM((ALL, D), BF16),
        pltpu.VMEM((ALL, D), BF16),
        pltpu.VMEM((ALL, 256), BF16),
        pltpu.VMEM((ALL, 256), BF16),
        pltpu.VMEM((ALL, 128), BF16),
        pltpu.VMEM((ALL, 128), BF16),
        pltpu.VMEM((ALL, 128), BF16),
        pltpu.VMEM((ALL, 3 * D), BF16),
        pltpu.VMEM((D, 128), F32),
        pltpu.VMEM((D, 128), F32),
        pltpu.VMEM((256, 128), F32),
    )

    base = by_name["vecs"].base
    lane = iota((1, 128), 1)
    for r, a in enumerate((A_PRED_GAIN, A_PRED_SHIFT, A_IN_BIAS)):
        put_row(buffer, base + 3 * r, acc_vec[a : a + 1, :])
    mid_bias = acc_small[A_MID_BIAS : A_MID_BIAS + 1, 0:256]
    low_bias = pltpu.roll(acc_small[A_LOW_BIAS : A_LOW_BIAS + 1, 0:128], 64, 1)
    out_bias = pltpu.roll(acc_small[A_OUT_BIAS : A_OUT_BIAS + 1, 0:128], 32, 1)
    buffer[base + 9 : base + 10, :] = mid_bias[:, 0:128]
    buffer[base + 10 : base + 11, :] = jnp.where(lane < 64, mid_bias[:, 128:256], low_bias)
    buffer[base + 11 : base + 12, :] = jnp.where(lane < 32, low_bias, out_bias)
    for r, a in enumerate(
        (A_ONE_GAIN, A_ONE_SHIFT, A_QUERY_BIAS, A_VALUE_BIAS, A_PROJ_BIAS, A_TWO_GAIN, A_TWO_SHIFT)
    ):
        put_row(buffer, base + 12 + 3 * r, acc_vec[a : a + 1, :])
    put_row(buffer, base + 33, acc_small[A_UP_BIAS : A_UP_BIAS + 1, :])
    put_row(buffer, base + 45, acc_vec[A_DOWN_BIAS : A_DOWN_BIAS + 1, :])

    def settle(name, ordered):
        base = by_name[name].base
        if name.startswith("mlp"):
            n = int(name[3:])
            for c in range(4):
                ordered[pl.ds(ROW_UP + 4 * n + c, D, stride=12), :] = buffer[base + c * D : base + (c + 1) * D, :]
            ordered[ROW_DOWN + 1536 * n : ROW_DOWN + 1536 * (n + 1), :] = buffer[base + 1536 : base + 3072, :]
        elif name.startswith("qkv"):
            p = int(name[3:])
            for c in range(3):
                ordered[pl.ds(ROW_QKV + 3 * c + p, D, stride=9), :] = buffer[base + c * D : base + (c + 1) * D, :]
        else:
            first, rows = {"proj": (ROW_PROJ, 1152), "pred": (0, ROW_QKV), "vecs": (ROW_VEC, 48)}[name]
            ordered[first : first + rows, :] = buffer[base : base + rows, :]

    names = [p.name for p in pieces]
    while any(done[n] < len(plan[n]) for n in names):
        for n in names:
            if done[n] < len(plan[n]):
                run(take(n))

    def hand_over(ordered):
        for n in names:
            settle(n, ordered)
        copy = pltpu.make_async_copy(ordered, grads, sem)
        copy.start()
        copy.wait()

    pl.run_scoped(hand_over, pltpu.VMEM((GRAD_ROWS, 128), F32))


TICKS = {
    "part": [[["mlp0"]], [["mlp0", "mlp1"]], [["mlp0", "mlp1", "mlp2"]]],
    "proj": [["mlp0", "mlp1", "mlp2", "proj"]],
    "pair": [
        [[["mlp0"]], [["mlp1", "mlp2"]], [["mlp0", "proj"]], [["mlp1", "mlp2"]]],
        [[["mlp0", "proj"]], [["mlp1", "mlp2", "qkv0"]], [["mlp0", "proj"]], [["mlp1", "mlp2", "qkv0"]]],
        [[["mlp0", "proj"]], [["mlp1", "mlp2", "qkv0", "qkv1"]], [["mlp0", "proj"]], [["mlp1", "mlp2", "qkv0", "qkv1"]]],
    ],
    "qkv": [[["qkv0"]], [["qkv1", "proj"]], [["qkv2", "mlp0"]]],
    "predict": [["mlp1", "mlp2", "proj", "qkv0", "qkv1", "qkv2"]],
    "pred": [["pred", "mlp1", "mlp2", "proj", "qkv0", "qkv1", "qkv2"]],
}

(
    V_PRED_GAIN, V_PRED_SHIFT, V_IN_BIAS, V_MID_BIAS, V_LOW_BIAS, V_OUT_BIAS, V_ONE_GAIN, V_ONE_SHIFT, V_PROJ_BIAS,
    V_TWO_GAIN, V_TWO_SHIFT, V_UP_BIAS, V_DOWN_BIAS,
) = range(13)
(
    A_PRED_GAIN, A_PRED_SHIFT, A_IN_BIAS, A_ONE_GAIN, A_ONE_SHIFT, A_QUERY_BIAS, A_VALUE_BIAS, A_PROJ_BIAS, A_TWO_GAIN,
    A_TWO_SHIFT, A_DOWN_BIAS,
) = range(11)
A_UP_BIAS, A_MID_BIAS, A_LOW_BIAS, A_OUT_BIAS = range(4)


def doubling():
    return (iota((128, 256), 1) // 2 == iota((128, 256), 0)).astype(F32).astype(BF16)


def unpack(flat, flat_end, flat_one, flat_two, sem, w_qkv, w_proj, w_up, w_down, w_in, w_mid, w_low, w_out, vecs,
           qkv_bias):
    copy = pltpu.make_async_copy(flat.at[pl.ds(0, NPARAM // 1024 * 1024)], flat_one, sem)
    copy.start()
    copy.wait()

    def spread(i, _):
        flat_two[pl.ds(pl.multiple_of(i * 384, 384), 384), :] = flat_one[
            pl.ds(pl.multiple_of(i * 49152, 49152), 49152)
        ].reshape(384, 128)
        return 0

    lax.fori_loop(0, 41, spread, 0)
    flat_two[15744:15752, :] = flat_end[...].reshape(8, 128)

    for c in range(3):
        w_in[:, c * 128 : (c + 1) * 128] = flat_two[pl.ds(c, D, stride=3), :].astype(BF16)
        w_proj[:, c * 128 : (c + 1) * 128] = shifted(flat_two, ROW_PROJ - 1 + c, D, 3).astype(BF16)
        w_down[:, c * 128 : (c + 1) * 128] = shifted(flat_two, ROW_DOWN - 1 + c, MLP, 3).astype(BF16)
        for p in range(PAIRS):
            tile = shifted(flat_two, ROW_QKV - 1 + 3 * c + p, D, 9).astype(BF16)
            w_qkv[:, p * D + c * 128 : p * D + (c + 1) * 128] = tile
    for c in range(12):
        w_up[:, c * 128 : (c + 1) * 128] = shifted(flat_two, ROW_UP - 1 + c, D, 12).astype(BF16)

    a, b, c = (flat_two[pl.ds(ROW_MID + s, 192, stride=3), :] for s in range(3))
    lane = iota((192, 128), 1)
    zero = jnp.zeros((192, 128), F32)

    def interleave(tiles):
        count = len(tiles)
        rows = tiles[0].shape[0]
        for s, tile in enumerate(tiles):
            flat_two[pl.ds(s, rows, stride=count), :] = tile
        return flat_two[0 : rows * count, :].astype(BF16)

    w_mid[:, 0:128] = interleave((a, pltpu.roll(jnp.where(lane < 64, c, b), 64, 1)))
    w_mid[:, 128:256] = interleave(
        (jnp.where(lane < 64, b, zero), jnp.where(lane < 64, pltpu.roll(c, 64, 1), zero))
    )
    lane = iota((48, 128), 1)
    a, b, c = (flat_two[pl.ds(ROW_LOW + s, 48, stride=3), :] for s in range(3))
    low = (
        a,
        jnp.where(lane < 32, pltpu.roll(a, 32, 1), pltpu.roll(b, 32, 1)),
        jnp.where(lane < 64, pltpu.roll(b, 64, 1), pltpu.roll(c, 64, 1)),
        pltpu.roll(c, 96, 1),
    )
    w_low[0:192, :] = interleave([jnp.where(lane < 96, tile, 0.0) for tile in low])
    w_low[192:256, :] = jnp.zeros((64, 128), BF16)
    head = jnp.concatenate([flat_two[ROW_OUT : ROW_OUT + 1, :], flat_two[ROW_OUT + 1 : ROW_OUT + 2, :]], 1)
    head = jnp.broadcast_to(head, (128, 256))
    lane = iota((128, 256), 1)
    chosen = (lane % 2 == iota((128, 256), 0)) & (lane < 192)
    w_out[...] = dot_nt(jnp.where(chosen, head, 0.0).astype(BF16), doubling()).astype(BF16)

    lane = iota((16, 128), 1)
    flat_two[0:16, :] = pltpu.roll(jnp.where(lane < 64, flat_two[15698:15714, :], flat_two[15697:15713, :]), 64, 1)
    lane = iota((36, 128), 1)
    flat_two[16:52, :] = pltpu.roll(jnp.where(lane < 98, flat_two[15709:15745, :], flat_two[15708:15744, :]), 30, 1)
    for r, base in (
        (V_PRED_GAIN, 0), (V_PRED_SHIFT, 3), (V_IN_BIAS, 6), (V_ONE_GAIN, 16), (V_ONE_SHIFT, 19), (V_PROJ_BIAS, 28),
        (V_TWO_GAIN, 31), (V_TWO_SHIFT, 34), (V_DOWN_BIAS, 49),
    ):
        vecs[r : r + 1, 0:D] = row_of(flat_two, base, 3)
    vecs[V_UP_BIAS : V_UP_BIAS + 1, :] = row_of(flat_two, 37, 12)
    lane = iota((1, 128), 1)
    zero = jnp.zeros((1, 128), F32)
    r9, r10, r11 = (flat_two[r : r + 1, :] for r in (9, 10, 11))
    vecs[V_MID_BIAS : V_MID_BIAS + 1, 0:128] = r9
    vecs[V_MID_BIAS : V_MID_BIAS + 1, 128:256] = jnp.where(lane < 64, r10, zero)
    vecs[V_LOW_BIAS : V_LOW_BIAS + 1, 0:128] = jnp.where(
        lane < 96, pltpu.roll(jnp.where(lane < 64, r11, r10), 64, 1), zero
    )
    vecs[V_OUT_BIAS : V_OUT_BIAS + 1, 0:128] = jnp.where(lane < 2, pltpu.roll(r11, 96, 1), zero)
    for p in range(PAIRS):
        qkv_bias[0:1, p * D : p * D + 128] = flat_two[22 + p : 23 + p, :]
        qkv_bias[0:1, p * D + 128 : p * D + 256] = zero
        qkv_bias[0:1, p * D + 256 : p * D + 384] = flat_two[25 + p : 26 + p, :]


def counting(sizes, groups, keep, out, held, landed, sems):
    stages = [s for axis in ("gy", "gx", "gz") for s in whole(sizes, axis)]
    first = [0]
    for stage in stages:
        first.append(first[-1] + stage[2] - 1)

    def copies(s):
        return [
            pltpu.make_async_remote_copy(
                held.at[s], landed.at[first[s] + slot], sems.at[0, first[s] + slot], sems.at[1, first[s] + slot],
                device, MESH,
            )
            for device, slot, _ in partners(stages[s])
        ]

    def begin():
        kept = jnp.zeros((1, 1), F32)
        valid = jnp.zeros((1, 1), F32)
        position = iota((1, SLOT), 1)
        for b in range(IMG):
            spatial = jnp.where((position > 0) & (position < length_of(groups, b)), 1.0, 0.0)
            kept += jnp.sum(spatial * keep[b : b + 1, :].astype(F32), keepdims=True)
            valid += jnp.sum(spatial, keepdims=True)
        row = iota((8, 128), 0)
        held[0] = jnp.where(row == 0, kept, jnp.where(row == 1, valid, 0.0))

    def step(s):
        if s == 0:
            begin()
        else:
            total = held[s - 1]
            for slot, copy in enumerate(copies(s - 1)):
                copy.wait()
                total = total + landed[first[s - 1] + slot]
            held[s] = total
        if s < len(stages):
            for copy in copies(s):
                copy.start()
        else:
            total = held[s]
            row = iota((8, 128), 0)
            excess = total[0:1, :] / total[1:2, :] - KEEP_TARGET
            loss = RATIO_WEIGHT * total[1:2, :] * excess * excess
            out[...] = jnp.where(row == 2, 2.0 * RATIO_WEIGHT * excess, jnp.where(row == 3, loss, total))

    return [functools.partial(step, s) for s in range(len(stages) + 1)]


def layer(sizes, *operands):
    pieces, rows = pieces_of(sizes)
    copies = max(sum(p.copies for p in pieces), 1)
    small = max(sum(sizes[a] - 1 for a in AXES), 1)
    vmem = pl.BlockSpec(memory_space=pltpu.VMEM)
    smem = pl.BlockSpec(memory_space=pltpu.SMEM)
    shape = jax.ShapeDtypeStruct
    return pl.pallas_call(
        functools.partial(layer_kernel, sizes, pieces),
        grid=(1,),
        out_shape=(
            shape((IMG, SLOT, D), BF16),
            shape((IMG, SLOT, D), BF16),
            shape((GRAD_ROWS, 128), F32),
            shape((8, 128), F32),
        ),
        in_specs=[
            smem, vmem, vmem, vmem, pl.BlockSpec(memory_space=pl.ANY),
            pl.BlockSpec((1024,), lambda i: (NPARAM // 1024,)),
        ],
        out_specs=[vmem, vmem, pl.BlockSpec(memory_space=pl.ANY), vmem],
        scratch_shapes=[
            pltpu.VMEM((D, 3 * D), BF16),
            pltpu.VMEM((D, D), BF16),
            pltpu.VMEM((D, MLP), BF16),
            pltpu.VMEM((MLP, D), BF16),
            pltpu.VMEM((D, D), BF16),
            pltpu.VMEM((D, 256), BF16),
            pltpu.VMEM((256, 128), BF16),
            pltpu.VMEM((128, 128), BF16),
            pltpu.VMEM((16, MLP), F32),
            pltpu.VMEM((8, 3 * D), F32),
            pltpu.VMEM((IMG, PAIRS, WIDE, 128), BF16),
            pltpu.VMEM((IMG, PAIRS, ROWS, 128), BF16),
            pltpu.VMEM((IMG, PAIRS, ROWS, 128), BF16),
            pltpu.VMEM((IMG, PAIRS, WIDE, 128), BF16),
            pltpu.VMEM((IMG, PAIRS, 3, 8, 256), F32),
            pltpu.VMEM((PAIRS, 128, ROWS), BF16),
            pltpu.VMEM((IMG, D, WIDE), BF16),
            pltpu.VMEM((ALL, D), BF16),
            pltpu.VMEM((ALL, D), F32),
            pltpu.VMEM((16, D), F32),
            pltpu.VMEM((8, MLP), F32),
            pltpu.VMEM((rows, 128), F32),
            pltpu.VMEM((rows, 128), F32),
            pltpu.SemaphoreType.DMA((4, copies)),
            pltpu.SemaphoreType.REGULAR((max(sum(len(p.stages) for p in pieces), 1),)),
            pltpu.VMEM((4, 8, 128), F32),
            pltpu.VMEM((small, 8, 128), F32),
            pltpu.SemaphoreType.DMA((2, small)),
            pltpu.SemaphoreType.DMA,
        ],
        compiler_params=pltpu.CompilerParams(
            collective_id=0, has_side_effects=True, vmem_limit_bytes=62 << 20
        ),
        name="layer",
    )(*operands)


UPDATE_ROWS = 768


def update_kernel(grads, after, params, momentum, average, new_params, new_momentum, new_average, joined):
    i = pl.program_id(0)
    n = UPDATE_ROWS
    joined[0:n, :] = grads[...]
    joined[n : n + 8, :] = after[...]
    here = joined[0:n, :]
    row = iota((n, 128), 0) + i * n
    lane = iota((n, 128), 1)
    moved = pltpu.roll(jnp.where(lane < 64, joined[1 : n + 1, :], here), 64, 1)
    flat = jnp.where(row < ROW_QKV - 1, here, moved)
    joined[0:n, :] = flat

    @pl.when(i == pl.num_programs(0) - 1)
    def _():
        first = 15708 - (NPARAM // (n * 128)) * n
        lane = iota((40, 128), 1)
        one = grads[first + 1 : first + 41, :]
        two = grads[first + 2 : first + 42, :]
        tail = pltpu.roll(jnp.where(lane < 30, two, one), 98, 1)
        keep_old = (iota((40, 128), 0) == 0) & (lane < 98)
        joined[first : first + 40, :] = jnp.where(keep_old, joined[first : first + 40, :], tail)

    g = joined[0:n, :].reshape(n * 128)
    moment = MOMENTUM_DECAY * momentum[...] + g
    value = params[...] - LEARN_RATE * (g + MOMENTUM_DECAY * moment)
    new_momentum[...] = moment
    new_params[...] = value
    new_average[...] = AVERAGE_DECAY * average[...] + (1.0 - AVERAGE_DECAY) * value


def update(grads, params, momentum, average):
    n = UPDATE_ROWS
    flat = pl.BlockSpec((n * 128,), lambda i: (i,))
    out = jax.ShapeDtypeStruct((NPARAM,), F32)
    return pl.pallas_call(
        update_kernel,
        grid=(pl.cdiv(NPARAM, n * 128),),
        out_shape=(out, out, out),
        in_specs=[
            pl.BlockSpec((n, 128), lambda i: (i, 0)),
            pl.BlockSpec((8, 128), lambda i: ((i + 1) * (n // 8), 0)),
            flat,
            flat,
            flat,
        ],
        out_specs=[flat] * 3,
        scratch_shapes=[pltpu.VMEM((n + 8, 128), F32)],
        compiler_params=pltpu.CompilerParams(vmem_limit_bytes=40 << 20),
        name="update",
    )(grads, grads, params, momentum, average)


GRAD_ROWS = -(-(NPARAM // 128 + 40) // UPDATE_ROWS) * UPDATE_ROWS + 8


def solution(mesh):
    sizes = dict(mesh.shape)

    def per_device(tokens, cotangent, groups, keep_mask, params, momentum, average):
        mixed, input_gradient, grads, counts = layer(sizes, groups, tokens, cotangent, keep_mask, params, params)
        new_params, new_momentum, new_average = update(grads, params, momentum, average)
        block = grads[ROW_BLOCK : ROW_BLOCK + 36].reshape(-1)
        return (mixed, input_gradient, counts[3, 0], new_params, new_momentum, new_average, block)

    split = P(("gx", "gy", "gz"))
    return jax.shard_map(
        per_device,
        mesh=mesh,
        in_specs=(split, split, split, split, P(), P(), P()),
        out_specs=(split, split, P(), P(), P(), P(), P()),
        check_vma=False,
    )
```

```python
import functools
import math

import jax
import jax.numpy as jnp
from jax import lax
from jax.experimental import pallas as pl
from jax.experimental.pallas import tpu as pltpu
from jax.sharding import PartitionSpec as P

MESH = pl.DeviceIdType.MESH
F32 = jnp.float32
BF16 = jnp.bfloat16

D = 384
HEADS = 6
PAIRS = 3
MLP = 1536
LEN_A, LEN_B, LEN_C = 101, 197, 325
IMG = 4
SLOT = 328
ROWS = 336
WIDE = 384
ALL = IMG * ROWS
NPARAM = 2015330
NORM_EPS = 1e-06
RATIO_WEIGHT = 2.0
KEEP_TARGET = 0.7
MOMENTUM_DECAY = 0.5
AVERAGE_DECAY = 0.5
LEARN_RATE = 0.0001

ROW_MID = 1152
ROW_LOW = 1728
ROW_OUT = 1872
ROW_QKV = 1874
ROW_PROJ = 5330
ROW_UP = 6482
ROW_DOWN = 11090
ROW_VEC = 15698
ROW_BLOCK = 15710
EARLY_BASE = 5328
EARLY_ROWS = 10376
FLAT_ROWS = 15752


def dot_nn(a, b):
    return lax.dot_general(a, b, (((1,), (0,)), ((), ())), preferred_element_type=F32)


def dot_nt(a, b):
    return lax.dot_general(a, b, (((1,), (1,)), ((), ())), preferred_element_type=F32)


def dot_tn(a, b):
    return lax.dot_general(a, b, (((0,), (0,)), ((), ())), preferred_element_type=F32)


def iota(shape, axis):
    return lax.broadcasted_iota(jnp.int32, shape, axis)


def gelu_pair(v):
    cdf = 0.5 * lax.erf(v * 0.7071067811865476) + 0.5
    return v * cdf, cdf + v * jnp.exp(v * v * -0.5) * 0.3989422804014327


def normalise(x):
    mean = jnp.sum(x, -1, keepdims=True) * (1.0 / D)
    centered = x - mean
    spread = jnp.sum(centered * centered, -1, keepdims=True) * (1.0 / D)
    rstd = lax.rsqrt(spread + NORM_EPS)
    return centered * rstd, rstd


def normalise_back(grad, gain, xhat, rstd):
    scaled = grad * gain
    first = jnp.sum(scaled, -1, keepdims=True) * (1.0 / D)
    second = jnp.sum(scaled * xhat, -1, keepdims=True) * (1.0 / D)
    return rstd * (scaled - first - xhat * second)


def column_sum(x):
    return jnp.sum(x, 0, keepdims=True)


def load_padded(ref, b):
    x = ref[b].astype(F32)
    return jnp.concatenate([x, jnp.zeros((ROWS - SLOT, D), F32)], 0)


def length_of(groups, b):
    g = groups[b]
    return jnp.where(g == 0, LEN_A, jnp.where(g == 1, LEN_B, LEN_C))


def policy_lanes(keep, length, b):
    row = keep[pl.ds(b, 1), :].astype(F32)
    row = jnp.concatenate([row, jnp.zeros((1, WIDE - SLOT), F32)], 1)
    kept = jnp.broadcast_to(row, (128, WIDE)).T[:ROWS]
    position = iota((ROWS, 128), 0)
    return jnp.where(position == 0, 1.0, jnp.where(position < length, kept, 0.0))


def split_heads(tile):
    left = iota(tile.shape, 1) < 64
    zero = jnp.zeros_like(tile)
    return jnp.concatenate([jnp.where(left, tile, zero), jnp.where(left, zero, tile)], 0)


def diagonal_blocks(x):
    return jnp.concatenate([x[:64, :128], x[64:, 128:]], 0)


def put(ref, base, stride, value):
    rows, columns = value.shape
    for c in range(columns // 128):
        ref[pl.ds(base + c, rows, stride=stride), :] = value[:, c * 128 : (c + 1) * 128]


def put_row(ref, base, value):
    for c in range(value.shape[1] // 128):
        ref[base + c : base + c + 1, :] = value[:, c * 128 : (c + 1) * 128]


def row_of(ref, base, count):
    return jnp.concatenate([ref[base + c : base + c + 1, :] for c in range(count)], 1)


def shifted(ref, base, rows, stride):
    first = ref[pl.ds(base, rows, stride=stride), :]
    second = ref[pl.ds(base + 1, rows, stride=stride), :]
    low = iota((rows, 128), 1) < 64
    return pltpu.roll(jnp.where(low, second, first), 64, 1)


AXES = ("gx", "gy", "gz")


def digits(sizes, axis):
    size, stride, found = sizes[axis], 1, []
    while size > 1:
        base = 2 if size % 2 == 0 else size
        found.append((axis, stride, base))
        size //= base
        stride *= base
    return found


def whole(sizes, axis):
    return [(axis, 1, sizes[axis])] if sizes[axis] > 1 else []


def digit_of(stage):
    axis, stride, base = stage
    return lax.rem(lax.axis_index(axis) // stride, base)


def partners(stage):
    axis, stride, base = stage
    mine = digit_of(stage)
    found = []
    for k in range(1, base):
        other = lax.rem(mine + k, base)
        index = lax.axis_index(axis) + (other - mine) * stride
        found.append((tuple(index if a == axis else lax.axis_index(a) for a in AXES), k - 1, other))
    return found


def greet(sizes):
    barrier = pltpu.get_barrier_semaphore()
    total = 0
    for axis in AXES:
        for stage in whole(sizes, axis):
            for device, _, _ in partners(stage):
                pl.semaphore_signal(barrier, inc=1, device_id=device, device_id_type=MESH)
                total += 1
    return barrier, total


class Piece:
    def __init__(self, name, rows, base, stages):
        self.name, self.rows, self.base, self.stages = name, rows, base, stages
        self.copies = sum(s[2] - 1 for s in stages)

    def steps(self, buffer, landing, sems, free, first, first_stage):
        stages = self.stages
        rows_after = [self.rows]
        for stage in stages:
            rows_after.append(rows_after[-1] // stage[2])
        landing_at, sem_at = [self.base], [first]
        for s, stage in enumerate(stages):
            landing_at.append(landing_at[-1] + (stage[2] - 1) * rows_after[s + 1])
            sem_at.append(sem_at[-1] + stage[2] - 1)

        def place(s):
            begin = self.base
            for i in range(s):
                begin = begin + digit_of(stages[i]) * rows_after[i + 1]
            return begin

        def block(s, digit):
            return pl.ds(pl.multiple_of(place(s) + digit * rows_after[s + 1], 8), rows_after[s + 1])

        def scatter(s):
            found = []
            for device, slot, other in partners(stages[s]):
                found.append(
                    pltpu.make_async_remote_copy(
                        buffer.at[block(s, other), :],
                        landing.at[pl.ds(landing_at[s] + slot * rows_after[s + 1], rows_after[s + 1]), :],
                        sems.at[0, sem_at[s] + slot],
                        sems.at[1, sem_at[s] + slot],
                        device,
                        MESH,
                    )
                )
            return found

        def gather(s):
            found = []
            for device, slot, _ in partners(stages[s]):
                own = buffer.at[block(s, digit_of(stages[s])), :]
                found.append(
                    pltpu.make_async_remote_copy(
                        own, own, sems.at[2, sem_at[s] + slot], sems.at[3, sem_at[s] + slot], device, MESH
                    )
                )
            return found

        def start(copies):
            for copy in copies:
                copy.start()

        def end_scatter(s):
            for copy in scatter(s):
                copy.wait()
            for device, _, _ in partners(stages[s]):
                pl.semaphore_signal(free.at[first_stage + s], inc=1, device_id=device, device_id_type=MESH)
            rows = rows_after[s + 1]
            begin = place(s) + digit_of(stages[s]) * rows
            step = math.gcd(rows, 64)

            def body(i, _):
                own = pl.ds(pl.multiple_of(begin + i * step, 8), step)
                total = buffer[own, :]
                for slot in range(stages[s][2] - 1):
                    at = landing_at[s] + slot * rows
                    total = total + landing[pl.ds(pl.multiple_of(at + i * step, 8), step), :]
                buffer[own, :] = total
                return 0

            lax.fori_loop(0, rows // step, body, 0)

        def end_gather(s):
            for copy in gather(s):
                copy.wait()

        count = len(stages)
        found = []
        for s in range(count):

            def there(s=s):
                if s:
                    end_scatter(s - 1)
                start(scatter(s))

            found.append(there)
        for s in reversed(range(count)):

            def back(s=s):
                if s == count - 1:
                    end_scatter(s)
                else:
                    end_gather(s + 1)
                pl.semaphore_wait(free.at[first_stage + s], stages[s][2] - 1)
                start(gather(s))

            found.append(back)
        if count:
            found.append(lambda: end_gather(0))
        return found


SECTIONS = (
    ("m0", 3072, ((1024, "CGAB"), (1024, "CXHY"), (1024, "CHXY"),)),
    ("m1", 3072, ((3072, "CGH"),)),
    ("m2", 3072, ((3072, "CAXYB"),)),
    ("proj", 1152, ((1280, "CYXAB"),)),
    ("qkv0", 1152, ((1280, "CXAYB"),)),
    ("qkv1", 1152, ((1280, "CYXAB"),)),
    ("qkv2", 1152, ((512, "CAXYB"), (768, "CYXAB"),)),
    ("pred", 1874, ((1280, "CGH"), (768, "CGH"),)),
    ("vecs", 48, ((256, "CGH"),)),
)


def pieces_of(sizes):
    unit = 8 * math.prod(sizes.values())
    core, x, z = digits(sizes, "gy"), digits(sizes, "gx"), digits(sizes, "gz")
    ways = {
        "C": core, "X": x[:1], "Y": x[1:], "A": z[:1], "B": z[1:], "G": whole(sizes, "gx"), "H": whole(sizes, "gz"),
    }
    found, starts, base = [], {}, 0
    for name, rows, parts in SECTIONS:
        starts[name] = base
        if unit > 256 or len(parts) == 1:
            parts = ((rows, parts[0][1]),)
        for i, (part_rows, way) in enumerate(parts):
            stages = [stage for letter in way for stage in ways[letter]]
            part_rows = -(-part_rows // unit) * unit
            found.append(Piece(name + "abcd"[i] if len(parts) > 1 else name, part_rows, base, stages))
            base += part_rows
    return found, starts, base


PART = 512
PARTS = MLP // PART
HALF = ALL // 2


def layer_kernel(
    sizes, pieces, starts,
    groups, tokens, cotangent, keep, flat, flat_end,
    mixed, input_gradient, grads, counts,
    w_qkv, w_proj, w_up, w_down, w_in, w_mid, w_low, w_out, vecs, qkv_bias,
    q_all, k_all, v_all, do_all, lse_all, v_turned, o_turned, n1_all, dx_all, acc_vec, acc_small,
    buffer, landing, sems, free, held, landed, count_sems, sem,
):
    plan, first, first_stage = {}, 0, 0
    for p in pieces:
        plan[p.name] = p.steps(buffer, landing, sems, free, first, first_stage)
        first += p.copies
        first_stage += len(p.stages)
    done = {p.name: 0 for p in pieces}

    def take(*names):
        found = []
        for name in names:
            if name in plan and done[name] < len(plan[name]):
                found.append(plan[name][done[name]])
                done[name] += 1
        return found

    def run(steps):
        for step in steps:
            step()

    def tick(name):
        run(take(*TICKS.get(name, ())))

    barrier, greetings = greet(sizes)
    count_steps = counting(sizes, groups, keep, counts, held, landed, count_sems)

    def weights(flat_one, flat_two):
        unpack(flat, flat_end, flat_one, flat_two, sem, w_qkv, w_proj, w_up, w_down, w_in, w_mid, w_low, w_out, vecs,
               qkv_bias)

    pl.run_scoped(weights, pltpu.VMEM((NPARAM // 1024 * 1024,), F32), pltpu.VMEM((FLAT_ROWS, 128), F32))
    if greetings:
        pl.semaphore_wait(barrier, greetings)
    run(count_steps[:1])

    def vec(r, size=D):
        return vecs[r : r + 1, 0:size]

    acc_vec[...] = jnp.zeros_like(acc_vec)
    acc_small[...] = jnp.zeros_like(acc_small)

    def rows_of(b):
        if isinstance(b, int):
            return slice(b * ROWS, (b + 1) * ROWS)
        return pl.ds(pl.multiple_of(b * ROWS, 16), ROWS)

    def first_half(x1_all, x2_all, dn2_all, n2_all, gd_all, up_part, gup_part, go_all, weight):
        def attend(b, _):
            length = length_of(groups, b)
            x = load_padded(tokens, b)
            xhat, _ = normalise(x)
            n1 = (xhat * vec(V_ONE_GAIN) + vec(V_ONE_SHIFT)).astype(BF16)
            n1_all[rows_of(b), :] = n1
            zeros = jnp.zeros((WIDE - ROWS, 128), BF16)
            for p in range(PAIRS):
                part = dot_nn(n1, w_qkv[:, p * D : (p + 1) * D]) + qkv_bias[0:1, p * D : (p + 1) * D]
                q_all[b, p] = jnp.concatenate([part[:, 0:128].astype(BF16) * jnp.array(0.125, BF16), zeros], 0)
                k_all[b, p] = part[:, 128:256].astype(BF16)
                v_all[b, p] = part[:, 256:384].astype(BF16)
                v_turned[p] = part[:, 256:384].T.astype(BF16)

            policy = policy_lanes(keep, length, b)
            row_id = iota((ROWS, 128), 0)
            lane_id = iota((ROWS, 128), 1)
            for t in range(3):
                weight[t] = jnp.where(row_id == lane_id + 128 * t, 1.0, policy)

            def pair(p):
                k_pair = k_all[b, p]
                vt = v_turned[p]
                tiles = [slice(128 * t, 128 * (t + 1)) for t in range(3)]
                where = slice(p * 128, (p + 1) * 128)

                def soft(t, s):
                    top = jnp.max(s, 0, keepdims=True)
                    w = weight[t]
                    e = jnp.exp(s - top) * jnp.concatenate([w, w], 1)
                    total = jnp.sum(e, 0, keepdims=True)
                    lse_all[b, p, t, 0:1, :] = top + jnp.log(total)
                    return e.astype(BF16), 1.0 / total

                def score(t):
                    return dot_nt(k_pair, split_heads(q_all[b, p, tiles[t], :]))

                def mix(t, e, inverse):
                    o = diagonal_blocks(dot_nn(vt, e) * inverse).astype(BF16)
                    o_turned[b, where, tiles[t]] = o

                s0 = score(0)
                s1 = score(1)
                e0 = soft(0, s0)
                s2 = score(2)
                e1 = soft(1, s1)
                mix(0, *e0)
                e2 = soft(2, s2)
                mix(1, *e1)
                mix(2, *e2)

            for p in range(PAIRS):
                pair(p)
            x1 = x + dot_tn(o_turned[b], w_proj[...])[:ROWS] + vec(V_PROJ_BIAS)
            x1_all[rows_of(b), :] = x1
            x2_all[rows_of(b), :] = x1 + vec(V_DOWN_BIAS)
            dn2_all[rows_of(b), :] = jnp.zeros((ROWS, D), F32)
            xhat2, _ = normalise(x1)
            n2_all[rows_of(b), :] = (xhat2 * vec(V_TWO_GAIN) + vec(V_TWO_SHIFT)).astype(BF16)
            valid = (iota((ROWS, D), 0) < length).astype(F32)
            g = load_padded(cotangent, b) * valid
            gd_all[rows_of(b), :] = g.astype(BF16)
            acc_vec[A_DOWN_BIAS : A_DOWN_BIAS + 1, :] += column_sum(g)
            return 0

        lax.fori_loop(0, IMG, attend, 0)
        run(count_steps[1:2])

        for n in range(PARTS):
            columns = slice(n * PART, (n + 1) * PART)

            def mlp(h):
                rows = slice(h * HALF, (h + 1) * HALF)
                n2 = n2_all[rows, :]
                g_d = gd_all[rows, :]
                u, slope = gelu_pair(dot_nn(n2, w_up[:, columns]) + vecs[V_UP_BIAS : V_UP_BIAS + 1, columns])
                u = u.astype(BF16)
                gu = (slope * dot_nt(g_d, w_down[columns, :])).astype(BF16)
                up_part[rows, :] = u
                gup_part[rows, :] = gu
                acc_small[A_UP_BIAS : A_UP_BIAS + 1, columns] += column_sum(gu.astype(F32))
                x2_all[rows, :] += dot_nn(u, w_down[columns, :])
                dn2_all[rows, :] += dot_nt(gu, w_up[:, columns])

            for h in range(2):
                mlp(h)
                tick(f"part{n}.{h}")

            base = starts[f"m{n}"]
            up = dot_tn(n2_all[...], gup_part[...])
            for c in range(PART // 128):
                buffer[base + c * D : base + (c + 1) * D, :] = up[:, c * 128 : (c + 1) * 128]
            put(buffer, base + 1536, 3, dot_tn(up_part[...], gd_all[...]))
            tick(f"part{n}")

        run(count_steps[2:3])

        def descend(b):
            length = length_of(groups, b)
            valid = (iota((ROWS, D), 0) < length).astype(F32)
            mixed[b] = (x2_all[rows_of(b), :] * valid)[:SLOT].astype(BF16)
            xhat2, rstd2 = normalise(x1_all[rows_of(b), :])
            dn2 = dn2_all[rows_of(b), :]
            acc_vec[A_TWO_GAIN : A_TWO_GAIN + 1, :] += column_sum(dn2 * xhat2)
            acc_vec[A_TWO_SHIFT : A_TWO_SHIFT + 1, :] += column_sum(dn2)
            g = load_padded(cotangent, b) * valid
            dx1 = g + normalise_back(dn2, vec(V_TWO_GAIN), xhat2, rstd2)
            dx_all[rows_of(b), :] = dx1
            g_o = dx1.astype(BF16)
            acc_vec[A_PROJ_BIAS : A_PROJ_BIAS + 1, :] += column_sum(g_o.astype(F32))
            go_all[b] = jnp.concatenate([g_o, jnp.zeros((WIDE - ROWS, D), BF16)], 0)
            d_o = dot_nt(g_o, w_proj[...]).astype(BF16)
            zeros = jnp.zeros((WIDE - ROWS, 128), BF16)
            for p in range(PAIRS):
                do_all[b, p] = jnp.concatenate([d_o[:, p * 128 : (p + 1) * 128], zeros], 0)

        for b in range(IMG):
            descend(b)
            tick(f"descend{b}")

        grad_proj = dot_nn(o_turned[0], go_all[0])
        for b in range(1, IMG):
            grad_proj = grad_proj + dot_nn(o_turned[b], go_all[b])
        put(buffer, starts["proj"], 3, grad_proj)
        run(count_steps[3:])
        tick("proj")

    pl.run_scoped(
        first_half,
        pltpu.VMEM((ALL, D), F32),
        pltpu.VMEM((ALL, D), F32),
        pltpu.VMEM((ALL, D), F32),
        pltpu.VMEM((ALL, D), BF16),
        pltpu.VMEM((ALL, D), BF16),
        pltpu.VMEM((ALL, PART), BF16),
        pltpu.VMEM((ALL, PART), BF16),
        pltpu.VMEM((IMG, WIDE, D), BF16),
        pltpu.VMEM((3, ROWS, 128), F32),
    )
    coefficient = counts[2:3, 0:1]

    def second_half(acc_policy, h0_all, ga_all, z_all, g1_all, m1_all, g2_all, m2_all, gl_all, dqkv_all, mid_one,
                    mid_two, low_one):
        acc_policy[...] = jnp.zeros_like(acc_policy)
        row_id = iota((ROWS, 128), 0)
        lane_id = iota((ROWS, 128), 1)

        for p in range(PAIRS):
            def attend(b):
                policy = policy_lanes(keep, length_of(groups, b), b)
                k_pair = k_all[b, p]
                v_pair = v_all[b, p]
                kt = k_pair.T
                tiles = [slice(128 * t, 128 * (t + 1)) for t in range(3)]
                q_two = [split_heads(q_all[b, p, tile, :]) for tile in tiles]
                do_two = [split_heads(do_all[b, p, tile, :]) for tile in tiles]

                def score(t):
                    return dot_nt(k_pair, q_two[t]), dot_nt(v_pair, do_two[t])

                def soft(t, s, dp):
                    f = jnp.exp(s - lse_all[b, p, t, 0:1, :])
                    same = row_id == lane_id + 128 * t
                    w = jnp.where(same, 1.0, policy)
                    prob = f * jnp.concatenate([w, w], 1)
                    centred = dp - jnp.sum(prob * dp, 0, keepdims=True)
                    dw = f * centred
                    acc_policy[b] += jnp.where(same, 0.0, dw[:, :128] + dw[:, 128:])
                    return prob.astype(BF16), (prob * centred).astype(BF16)

                def query(t, ds):
                    dq = diagonal_blocks(dot_nn(kt, ds)).T * 0.125
                    count = min(128, ROWS - 128 * t)
                    first = b * ROWS + 128 * t
                    dqkv_all[pl.ds(first, count), p * D : p * D + 128] = dq[:count].astype(BF16)

                s0 = score(0)
                s1 = score(1)
                p0, d0 = soft(0, *s0)
                s2 = score(2)
                p1, d1 = soft(1, *s1)
                query(0, d0)
                p2, d2 = soft(2, *s2)
                query(1, d1)
                dv = dot_nn(jnp.concatenate([p0, p1, p2], 1), jnp.concatenate(do_two, 0))
                dk = dot_nn(jnp.concatenate([d0, d1, d2], 1), jnp.concatenate(q_two, 0))
                query(2, d2)
                dqkv_all[rows_of(b), p * D + 128 : p * D + 256] = dk.astype(BF16)
                dqkv_all[rows_of(b), p * D + 256 : p * D + 384] = dv.astype(BF16)

            for b in range(IMG):
                attend(b)
                tick(f"pair{p}.{b}")
            dqkv = dqkv_all[:, p * D : (p + 1) * D]
            base = starts[f"qkv{p}"]
            grad = dot_tn(n1_all[...], dqkv)
            for c in range(3):
                buffer[base + c * D : base + (c + 1) * D, :] = grad[:, c * 128 : (c + 1) * 128]
            bias = column_sum(dqkv.astype(F32))
            acc_vec[A_QUERY_BIAS : A_QUERY_BIAS + 1, p * 128 : (p + 1) * 128] = bias[:, 0:128]
            acc_vec[A_VALUE_BIAS : A_VALUE_BIAS + 1, p * 128 : (p + 1) * 128] = bias[:, 256:384]
            tick(f"qkv{p}")

        spatial_of, share_of = {}, {}

        def predict(b):
            length = length_of(groups, b)
            rows = rows_of(b)
            dpolicy = jnp.sum(acc_policy[b], 1, keepdims=True)
            xhat, _ = normalise(load_padded(tokens, b))
            h0 = (xhat * vec(V_PRED_GAIN) + vec(V_PRED_SHIFT)).astype(BF16)
            h0_all[rows, :] = h0
            position = iota((ROWS, 1), 0)
            spatial = jnp.where((position > 0) & (position < length), 1.0, 0.0)
            share = 1.0 / (length - 1).astype(F32)
            act, act_slope = gelu_pair(dot_nn(h0, w_in[...]) + vec(V_IN_BIAS))
            pooled = column_sum(act * spatial) * share
            local = iota((ROWS, D), 1) < D // 2
            z = jnp.where(local, act, pooled).astype(BF16)
            z_all[rows, :] = z
            m1, m1_slope = gelu_pair(dot_nn(z, w_mid[...]) + vec(V_MID_BIAS, 256))
            m1 = m1.astype(BF16)
            m1_all[rows, :] = m1
            m2, m2_slope = gelu_pair(dot_nn(m1, w_low[...]) + vec(V_LOW_BIAS, 128))
            m2 = m2.astype(BF16)
            m2_all[rows, :] = m2
            logits = dot_nt(m2, w_out[...]) + vec(V_OUT_BIAS, 128)
            keep_prob = 1.0 / (1.0 + jnp.exp(logits[:, 1:2] - logits[:, 0:1]))
            drop_prob = 1.0 / (1.0 + jnp.exp(logits[:, 0:1] - logits[:, 1:2]))
            dlog = spatial * (dpolicy + coefficient * spatial) * keep_prob * drop_prob
            lane = iota((ROWS, 128), 1)
            g_l = jnp.where(lane == 0, dlog, jnp.where(lane == 1, -dlog, 0.0)).astype(BF16)
            gl_all[rows, :] = g_l
            g_2 = (m2_slope * dot_nn(g_l, w_out[...])).astype(BF16)
            g2_all[rows, :] = g_2
            g_1 = (m1_slope * dot_nt(g_2, w_low[...])).astype(BF16)
            g1_all[rows, :] = g_1
            dz = dot_nt(g_1, w_mid[...])
            da = jnp.where(local, dz, spatial * share * column_sum(dz))
            g_a = (act_slope * da).astype(BF16)
            ga_all[rows, :] = g_a
            acc_vec[A_IN_BIAS : A_IN_BIAS + 1, :] += column_sum(g_a.astype(F32))
            acc_small[A_MID_BIAS : A_MID_BIAS + 1, 0:256] += column_sum(g_1.astype(F32))
            acc_small[A_LOW_BIAS : A_LOW_BIAS + 1, 0:128] += column_sum(g_2.astype(F32))
            acc_small[A_OUT_BIAS : A_OUT_BIAS + 1, 0:128] += column_sum(g_l.astype(F32))

        for b in range(IMG):
            predict(b)
            tick(f"predict{b}")


        base = starts["pred"]
        put(buffer, base, 3, dot_tn(h0_all[...], ga_all[...]))
        grad_mid = dot_tn(z_all[...], g1_all[...])
        mid_one[...] = grad_mid[:, 0:128]
        mid_two[...] = grad_mid[:, 128:256]
        lane = iota((192, 128), 1)
        odd = pltpu.roll(mid_one[pl.ds(1, 192, stride=2), :], 64, 1)
        buffer[pl.ds(base + ROW_MID, 192, stride=3), :] = mid_one[pl.ds(0, 192, stride=2), :]
        buffer[pl.ds(base + ROW_MID + 1, 192, stride=3), :] = jnp.where(
            lane < 64, mid_two[pl.ds(0, 192, stride=2), :], odd
        )
        buffer[pl.ds(base + ROW_MID + 2, 192, stride=3), :] = jnp.where(
            lane < 64, odd, pltpu.roll(mid_two[pl.ds(1, 192, stride=2), :], 64, 1)
        )
        low_one[...] = dot_tn(m1_all[...], g2_all[...])
        lane = iota((48, 128), 1)
        r0, r1, r2, r3 = (low_one[pl.ds(s, 48, stride=4), :] for s in range(4))
        r1, r2, r3 = pltpu.roll(r1, 96, 1), pltpu.roll(r2, 64, 1), pltpu.roll(r3, 32, 1)
        buffer[pl.ds(base + ROW_LOW, 48, stride=3), :] = jnp.where(lane < 96, r0, r1)
        buffer[pl.ds(base + ROW_LOW + 1, 48, stride=3), :] = jnp.where(lane < 64, r1, r2)
        buffer[pl.ds(base + ROW_LOW + 2, 48, stride=3), :] = jnp.where(lane < 32, r2, r3)
        m2_doubled = dot_nn(m2_all[...], doubling()).astype(BF16)
        both = dot_tn(gl_all[...], m2_doubled)
        head = jnp.where(iota((1, 256), 1) % 2 == 0, both[0:1, :], both[1:2, :])
        buffer[base + ROW_OUT : base + ROW_OUT + 1, :] = head[:, 0:128]
        buffer[base + ROW_OUT + 1 : base + ROW_OUT + 2, :] = pltpu.roll(head[:, 128:256], 64, 1)
        tick("pred")

        def finish(b):
            rows = rows_of(b)
            xhat, rstd = normalise(load_padded(tokens, b))
            dh0 = dot_nt(ga_all[rows, :], w_in[...])
            acc_vec[A_PRED_GAIN : A_PRED_GAIN + 1, :] += column_sum(dh0 * xhat)
            acc_vec[A_PRED_SHIFT : A_PRED_SHIFT + 1, :] += column_sum(dh0)
            dn1 = dot_nt(dqkv_all[rows, :], w_qkv[...])
            acc_vec[A_ONE_GAIN : A_ONE_GAIN + 1, :] += column_sum(dn1 * xhat)
            acc_vec[A_ONE_SHIFT : A_ONE_SHIFT + 1, :] += column_sum(dn1)
            total = (
                dx_all[rows, :]
                + normalise_back(dn1, vec(V_ONE_GAIN), xhat, rstd)
                + normalise_back(dh0, vec(V_PRED_GAIN), xhat, rstd)
            )
            input_gradient[b] = total[:SLOT].astype(BF16)

        for b in range(IMG):
            finish(b)
            tick(f"finish{b}")


    pl.run_scoped(
        second_half,
        pltpu.VMEM((IMG, ROWS, 128), F32),
        pltpu.VMEM((ALL, D), BF16),
        pltpu.VMEM((ALL, D), BF16),
        pltpu.VMEM((ALL, D), BF16),
        pltpu.VMEM((ALL, 256), BF16),
        pltpu.VMEM((ALL, 256), BF16),
        pltpu.VMEM((ALL, 128), BF16),
        pltpu.VMEM((ALL, 128), BF16),
        pltpu.VMEM((ALL, 128), BF16),
        pltpu.VMEM((ALL, 3 * D), BF16),
        pltpu.VMEM((D, 128), F32),
        pltpu.VMEM((D, 128), F32),
        pltpu.VMEM((256, 128), F32),
    )

    base = starts["vecs"]
    lane = iota((1, 128), 1)
    for r, a in enumerate((A_PRED_GAIN, A_PRED_SHIFT, A_IN_BIAS)):
        put_row(buffer, base + 3 * r, acc_vec[a : a + 1, :])
    mid_bias = acc_small[A_MID_BIAS : A_MID_BIAS + 1, 0:256]
    low_bias = pltpu.roll(acc_small[A_LOW_BIAS : A_LOW_BIAS + 1, 0:128], 64, 1)
    out_bias = pltpu.roll(acc_small[A_OUT_BIAS : A_OUT_BIAS + 1, 0:128], 32, 1)
    buffer[base + 9 : base + 10, :] = mid_bias[:, 0:128]
    buffer[base + 10 : base + 11, :] = jnp.where(lane < 64, mid_bias[:, 128:256], low_bias)
    buffer[base + 11 : base + 12, :] = jnp.where(lane < 32, low_bias, out_bias)
    for r, a in enumerate(
        (A_ONE_GAIN, A_ONE_SHIFT, A_QUERY_BIAS, A_VALUE_BIAS, A_PROJ_BIAS, A_TWO_GAIN, A_TWO_SHIFT)
    ):
        put_row(buffer, base + 12 + 3 * r, acc_vec[a : a + 1, :])
    put_row(buffer, base + 33, acc_small[A_UP_BIAS : A_UP_BIAS + 1, :])
    put_row(buffer, base + 45, acc_vec[A_DOWN_BIAS : A_DOWN_BIAS + 1, :])

    def settle(name, ordered):
        base = starts[name]
        if name.startswith("m"):
            n = int(name[1:])
            for c in range(4):
                ordered[pl.ds(ROW_UP + 4 * n + c, D, stride=12), :] = buffer[base + c * D : base + (c + 1) * D, :]
            ordered[ROW_DOWN + 1536 * n : ROW_DOWN + 1536 * (n + 1), :] = buffer[base + 1536 : base + 3072, :]
        elif name.startswith("qkv"):
            p = int(name[3:])
            for c in range(3):
                ordered[pl.ds(ROW_QKV + 3 * c + p, D, stride=9), :] = buffer[base + c * D : base + (c + 1) * D, :]
        else:
            first, rows = {"proj": (ROW_PROJ, 1152), "pred": (0, ROW_QKV), "vecs": (ROW_VEC, 48)}[name]
            ordered[first : first + rows, :] = buffer[base : base + rows, :]

    tick("vecs")
    for name in DRAIN:
        run(take(name))
    names = [p.name for p in pieces]
    while any(done[n] < len(plan[n]) for n in names):
        for n in names:
            run(take(n))

    def hand_over(ordered):
        for n in starts:
            settle(n, ordered)
        copy = pltpu.make_async_copy(ordered, grads, sem)
        copy.start()
        copy.wait()

    pl.run_scoped(hand_over, pltpu.VMEM((GRAD_ROWS, 128), F32))


TICKS = {
    "part0": ("m0a", "m0b", "m0c",),
    "part1.0": ("m0a", "m0b",),
    "part1.1": ("m0c",),
    "part1": ("m1",),
    "part2.1": ("m0a", "m1", "m0b",),
    "part2": ("m2",),
    "descend1": ("m0a",),
    "proj": ("proj", "m0c", "m2",),
    "pair0.1": ("proj", "m0a", "m0b",),
    "qkv0": ("qkv0",),
    "pair1.1": ("m0c", "m1", "qkv0",),
    "pair1.3": ("proj", "m0b", "m0c",),
    "qkv1": ("qkv1", "m2",),
    "pair2.0": ("m0a",),
    "pair2.1": ("m0b", "qkv1", "m0c", "qkv0",),
    "pair2.3": ("proj", "m0a",),
    "qkv2": ("qkv2a", "qkv2b", "m1",),
    "predict0": ("qkv2a", "qkv2b", "qkv1", "m2", "qkv0", "m0b", "m0c", "proj",),
    "predict2": ("m0a", "qkv1", "qkv2a", "qkv2b",),
    "predict3": ("m1", "m0a", "m2", "m0b", "qkv0",),
    "pred": ("preda", "predb", "qkv2a", "qkv2b", "m0b",),
    "finish1": ("qkv1", "preda", "proj", "m0c", "predb",),
    "finish3": ("m2", "m0c", "qkv2b",),
    "vecs": ("vecs", "qkv0",),
}
DRAIN = (
    "qkv1", "vecs", "proj", "qkv2a", "m1", "m2", "qkv2b", "qkv0", "m1", "proj", "qkv1", "qkv2a", "preda",
    "qkv2b", "qkv1", "predb", "vecs", "qkv2a", "proj", "m2", "qkv2b", "qkv0", "qkv2a", "preda", "qkv1",
    "predb", "vecs", "qkv0", "proj", "m2", "proj", "qkv2b", "qkv2a", "preda", "qkv1", "predb", "vecs", "qkv1",
    "qkv0", "qkv2b", "qkv0", "qkv2b", "preda", "m2", "preda", "predb", "qkv2a", "vecs", "m2", "predb",
    "qkv2a", "vecs",
)

(
    V_PRED_GAIN, V_PRED_SHIFT, V_IN_BIAS, V_MID_BIAS, V_LOW_BIAS, V_OUT_BIAS, V_ONE_GAIN, V_ONE_SHIFT, V_PROJ_BIAS,
    V_TWO_GAIN, V_TWO_SHIFT, V_UP_BIAS, V_DOWN_BIAS,
) = range(13)
(
    A_PRED_GAIN, A_PRED_SHIFT, A_IN_BIAS, A_ONE_GAIN, A_ONE_SHIFT, A_QUERY_BIAS, A_VALUE_BIAS, A_PROJ_BIAS, A_TWO_GAIN,
    A_TWO_SHIFT, A_DOWN_BIAS,
) = range(11)
A_UP_BIAS, A_MID_BIAS, A_LOW_BIAS, A_OUT_BIAS = range(4)


def doubling():
    return (iota((128, 256), 1) // 2 == iota((128, 256), 0)).astype(F32).astype(BF16)


def unpack(flat, flat_end, flat_one, flat_two, sem, w_qkv, w_proj, w_up, w_down, w_in, w_mid, w_low, w_out, vecs,
           qkv_bias):
    copy = pltpu.make_async_copy(flat.at[pl.ds(0, NPARAM // 1024 * 1024)], flat_one, sem)
    copy.start()
    copy.wait()

    def spread(i, _):
        flat_two[pl.ds(pl.multiple_of(i * 384, 384), 384), :] = flat_one[
            pl.ds(pl.multiple_of(i * 49152, 49152), 49152)
        ].reshape(384, 128)
        return 0

    lax.fori_loop(0, 41, spread, 0)
    flat_two[15744:15752, :] = flat_end[...].reshape(8, 128)

    for c in range(3):
        w_in[:, c * 128 : (c + 1) * 128] = flat_two[pl.ds(c, D, stride=3), :].astype(BF16)
        w_proj[:, c * 128 : (c + 1) * 128] = shifted(flat_two, ROW_PROJ - 1 + c, D, 3).astype(BF16)
        w_down[:, c * 128 : (c + 1) * 128] = shifted(flat_two, ROW_DOWN - 1 + c, MLP, 3).astype(BF16)
        for p in range(PAIRS):
            tile = shifted(flat_two, ROW_QKV - 1 + 3 * c + p, D, 9).astype(BF16)
            w_qkv[:, p * D + c * 128 : p * D + (c + 1) * 128] = tile
    for c in range(12):
        w_up[:, c * 128 : (c + 1) * 128] = shifted(flat_two, ROW_UP - 1 + c, D, 12).astype(BF16)

    a, b, c = (flat_two[pl.ds(ROW_MID + s, 192, stride=3), :] for s in range(3))
    lane = iota((192, 128), 1)
    zero = jnp.zeros((192, 128), F32)

    def interleave(tiles):
        count = len(tiles)
        rows = tiles[0].shape[0]
        for s, tile in enumerate(tiles):
            flat_two[pl.ds(s, rows, stride=count), :] = tile
        return flat_two[0 : rows * count, :].astype(BF16)

    w_mid[:, 0:128] = interleave((a, pltpu.roll(jnp.where(lane < 64, c, b), 64, 1)))
    w_mid[:, 128:256] = interleave(
        (jnp.where(lane < 64, b, zero), jnp.where(lane < 64, pltpu.roll(c, 64, 1), zero))
    )
    lane = iota((48, 128), 1)
    a, b, c = (flat_two[pl.ds(ROW_LOW + s, 48, stride=3), :] for s in range(3))
    low = (
        a,
        jnp.where(lane < 32, pltpu.roll(a, 32, 1), pltpu.roll(b, 32, 1)),
        jnp.where(lane < 64, pltpu.roll(b, 64, 1), pltpu.roll(c, 64, 1)),
        pltpu.roll(c, 96, 1),
    )
    w_low[0:192, :] = interleave([jnp.where(lane < 96, tile, 0.0) for tile in low])
    w_low[192:256, :] = jnp.zeros((64, 128), BF16)
    head = jnp.concatenate([flat_two[ROW_OUT : ROW_OUT + 1, :], flat_two[ROW_OUT + 1 : ROW_OUT + 2, :]], 1)
    head = jnp.broadcast_to(head, (128, 256))
    lane = iota((128, 256), 1)
    chosen = (lane % 2 == iota((128, 256), 0)) & (lane < 192)
    w_out[...] = dot_nt(jnp.where(chosen, head, 0.0).astype(BF16), doubling()).astype(BF16)

    lane = iota((16, 128), 1)
    flat_two[0:16, :] = pltpu.roll(jnp.where(lane < 64, flat_two[15698:15714, :], flat_two[15697:15713, :]), 64, 1)
    lane = iota((36, 128), 1)
    flat_two[16:52, :] = pltpu.roll(jnp.where(lane < 98, flat_two[15709:15745, :], flat_two[15708:15744, :]), 30, 1)
    for r, base in (
        (V_PRED_GAIN, 0), (V_PRED_SHIFT, 3), (V_IN_BIAS, 6), (V_ONE_GAIN, 16), (V_ONE_SHIFT, 19), (V_PROJ_BIAS, 28),
        (V_TWO_GAIN, 31), (V_TWO_SHIFT, 34), (V_DOWN_BIAS, 49),
    ):
        vecs[r : r + 1, 0:D] = row_of(flat_two, base, 3)
    vecs[V_UP_BIAS : V_UP_BIAS + 1, :] = row_of(flat_two, 37, 12)
    lane = iota((1, 128), 1)
    zero = jnp.zeros((1, 128), F32)
    r9, r10, r11 = (flat_two[r : r + 1, :] for r in (9, 10, 11))
    vecs[V_MID_BIAS : V_MID_BIAS + 1, 0:128] = r9
    vecs[V_MID_BIAS : V_MID_BIAS + 1, 128:256] = jnp.where(lane < 64, r10, zero)
    vecs[V_LOW_BIAS : V_LOW_BIAS + 1, 0:128] = jnp.where(
        lane < 96, pltpu.roll(jnp.where(lane < 64, r11, r10), 64, 1), zero
    )
    vecs[V_OUT_BIAS : V_OUT_BIAS + 1, 0:128] = jnp.where(lane < 2, pltpu.roll(r11, 96, 1), zero)
    for p in range(PAIRS):
        qkv_bias[0:1, p * D : p * D + 128] = flat_two[22 + p : 23 + p, :]
        qkv_bias[0:1, p * D + 128 : p * D + 256] = zero
        qkv_bias[0:1, p * D + 256 : p * D + 384] = flat_two[25 + p : 26 + p, :]


def counting(sizes, groups, keep, out, held, landed, sems):
    stages = [s for axis in ("gy", "gx", "gz") for s in whole(sizes, axis)]
    first = [0]
    for stage in stages:
        first.append(first[-1] + stage[2] - 1)

    def copies(s):
        return [
            pltpu.make_async_remote_copy(
                held.at[s], landed.at[first[s] + slot], sems.at[0, first[s] + slot], sems.at[1, first[s] + slot],
                device, MESH,
            )
            for device, slot, _ in partners(stages[s])
        ]

    def begin():
        kept = jnp.zeros((1, 1), F32)
        valid = jnp.zeros((1, 1), F32)
        position = iota((1, SLOT), 1)
        for b in range(IMG):
            spatial = jnp.where((position > 0) & (position < length_of(groups, b)), 1.0, 0.0)
            kept += jnp.sum(spatial * keep[b : b + 1, :].astype(F32), keepdims=True)
            valid += jnp.sum(spatial, keepdims=True)
        row = iota((8, 128), 0)
        held[0] = jnp.where(row == 0, kept, jnp.where(row == 1, valid, 0.0))

    def step(s):
        if s == 0:
            begin()
        else:
            total = held[s - 1]
            for slot, copy in enumerate(copies(s - 1)):
                copy.wait()
                total = total + landed[first[s - 1] + slot]
            held[s] = total
        if s < len(stages):
            for copy in copies(s):
                copy.start()
        else:
            total = held[s]
            row = iota((8, 128), 0)
            excess = total[0:1, :] / total[1:2, :] - KEEP_TARGET
            loss = RATIO_WEIGHT * total[1:2, :] * excess * excess
            out[...] = jnp.where(row == 2, 2.0 * RATIO_WEIGHT * excess, jnp.where(row == 3, loss, total))

    return [functools.partial(step, s) for s in range(len(stages) + 1)]


def layer(sizes, *operands):
    pieces, starts, rows = pieces_of(sizes)
    copies = max(sum(p.copies for p in pieces), 1)
    small = max(sum(sizes[a] - 1 for a in AXES), 1)
    vmem = pl.BlockSpec(memory_space=pltpu.VMEM)
    smem = pl.BlockSpec(memory_space=pltpu.SMEM)
    shape = jax.ShapeDtypeStruct
    return pl.pallas_call(
        functools.partial(layer_kernel, sizes, pieces, starts),
        grid=(1,),
        out_shape=(
            shape((IMG, SLOT, D), BF16),
            shape((IMG, SLOT, D), BF16),
            shape((GRAD_ROWS, 128), F32),
            shape((8, 128), F32),
        ),
        in_specs=[
            smem, vmem, vmem, vmem, pl.BlockSpec(memory_space=pl.ANY),
            pl.BlockSpec((1024,), lambda i: (NPARAM // 1024,)),
        ],
        out_specs=[vmem, vmem, pl.BlockSpec(memory_space=pl.ANY), vmem],
        scratch_shapes=[
            pltpu.VMEM((D, 3 * D), BF16),
            pltpu.VMEM((D, D), BF16),
            pltpu.VMEM((D, MLP), BF16),
            pltpu.VMEM((MLP, D), BF16),
            pltpu.VMEM((D, D), BF16),
            pltpu.VMEM((D, 256), BF16),
            pltpu.VMEM((256, 128), BF16),
            pltpu.VMEM((128, 128), BF16),
            pltpu.VMEM((16, MLP), F32),
            pltpu.VMEM((8, 3 * D), F32),
            pltpu.VMEM((IMG, PAIRS, WIDE, 128), BF16),
            pltpu.VMEM((IMG, PAIRS, ROWS, 128), BF16),
            pltpu.VMEM((IMG, PAIRS, ROWS, 128), BF16),
            pltpu.VMEM((IMG, PAIRS, WIDE, 128), BF16),
            pltpu.VMEM((IMG, PAIRS, 3, 8, 256), F32),
            pltpu.VMEM((PAIRS, 128, ROWS), BF16),
            pltpu.VMEM((IMG, D, WIDE), BF16),
            pltpu.VMEM((ALL, D), BF16),
            pltpu.VMEM((ALL, D), F32),
            pltpu.VMEM((16, D), F32),
            pltpu.VMEM((8, MLP), F32),
            pltpu.VMEM((rows, 128), F32),
            pltpu.VMEM((rows, 128), F32),
            pltpu.SemaphoreType.DMA((4, copies)),
            pltpu.SemaphoreType.REGULAR((max(sum(len(p.stages) for p in pieces), 1),)),
            pltpu.VMEM((4, 8, 128), F32),
            pltpu.VMEM((small, 8, 128), F32),
            pltpu.SemaphoreType.DMA((2, small)),
            pltpu.SemaphoreType.DMA,
        ],
        compiler_params=pltpu.CompilerParams(
            collective_id=0, has_side_effects=True, vmem_limit_bytes=62 << 20
        ),
        name="layer",
    )(*operands)


UPDATE_ROWS = 768


def update_kernel(grads, after, params, momentum, average, new_params, new_momentum, new_average, joined):
    i = pl.program_id(0)
    n = UPDATE_ROWS
    joined[0:n, :] = grads[...]
    joined[n : n + 8, :] = after[...]
    here = joined[0:n, :]
    row = iota((n, 128), 0) + i * n
    lane = iota((n, 128), 1)
    moved = pltpu.roll(jnp.where(lane < 64, joined[1 : n + 1, :], here), 64, 1)
    flat = jnp.where(row < ROW_QKV - 1, here, moved)
    joined[0:n, :] = flat

    @pl.when(i == pl.num_programs(0) - 1)
    def _():
        first = 15708 - (NPARAM // (n * 128)) * n
        lane = iota((40, 128), 1)
        one = grads[first + 1 : first + 41, :]
        two = grads[first + 2 : first + 42, :]
        tail = pltpu.roll(jnp.where(lane < 30, two, one), 98, 1)
        keep_old = (iota((40, 128), 0) == 0) & (lane < 98)
        joined[first : first + 40, :] = jnp.where(keep_old, joined[first : first + 40, :], tail)

    g = joined[0:n, :].reshape(n * 128)
    moment = MOMENTUM_DECAY * momentum[...] + g
    value = params[...] - LEARN_RATE * (g + MOMENTUM_DECAY * moment)
    new_momentum[...] = moment
    new_params[...] = value
    new_average[...] = AVERAGE_DECAY * average[...] + (1.0 - AVERAGE_DECAY) * value


def update(grads, params, momentum, average):
    n = UPDATE_ROWS
    flat = pl.BlockSpec((n * 128,), lambda i: (i,))
    out = jax.ShapeDtypeStruct((NPARAM,), F32)
    return pl.pallas_call(
        update_kernel,
        grid=(pl.cdiv(NPARAM, n * 128),),
        out_shape=(out, out, out),
        in_specs=[
            pl.BlockSpec((n, 128), lambda i: (i, 0)),
            pl.BlockSpec((8, 128), lambda i: ((i + 1) * (n // 8), 0)),
            flat,
            flat,
            flat,
        ],
        out_specs=[flat] * 3,
        scratch_shapes=[pltpu.VMEM((n + 8, 128), F32)],
        compiler_params=pltpu.CompilerParams(vmem_limit_bytes=40 << 20),
        name="update",
    )(grads, grads, params, momentum, average)


GRAD_ROWS = -(-(NPARAM // 128 + 40) // UPDATE_ROWS) * UPDATE_ROWS + 8


def solution(mesh):
    sizes = dict(mesh.shape)

    def per_device(tokens, cotangent, groups, keep_mask, params, momentum, average):
        mixed, input_gradient, grads, counts = layer(sizes, groups, tokens, cotangent, keep_mask, params, params)
        new_params, new_momentum, new_average = update(grads, params, momentum, average)
        block = grads[ROW_BLOCK : ROW_BLOCK + 36].reshape(-1)
        return (mixed, input_gradient, counts[3, 0], new_params, new_momentum, new_average, block)

    split = P(("gx", "gy", "gz"))
    return jax.shard_map(
        per_device,
        mesh=mesh,
        in_specs=(split, split, split, split, P(), P(), P()),
        out_specs=(split, split, P(), P(), P(), P(), P()),
        check_vma=False,
    )
```

```python
import functools
import math

import jax
import jax.numpy as jnp
from jax import lax
from jax.experimental import pallas as pl
from jax.experimental.pallas import tpu as pltpu
from jax.sharding import PartitionSpec as P

MESH = pl.DeviceIdType.MESH
F32 = jnp.float32
BF16 = jnp.bfloat16

D = 384
HEADS = 6
PAIRS = 3
MLP = 1536
LEN_A, LEN_B, LEN_C = 101, 197, 325
IMG = 4
SLOT = 328
ROWS = 336
WIDE = 384
ALL = IMG * ROWS
NPARAM = 2015330
NORM_EPS = 1e-06
RATIO_WEIGHT = 2.0
KEEP_TARGET = 0.7
MOMENTUM_DECAY = 0.5
AVERAGE_DECAY = 0.5
LEARN_RATE = 0.0001

ROW_MID = 1152
ROW_LOW = 1728
ROW_OUT = 1872
ROW_QKV = 1874
ROW_PROJ = 5330
ROW_UP = 6482
ROW_DOWN = 11090
ROW_VEC = 15698
ROW_BLOCK = 15710
EARLY_BASE = 5328
EARLY_ROWS = 10376
FLAT_ROWS = 15752


def dot_nn(a, b):
    return lax.dot_general(a, b, (((1,), (0,)), ((), ())), preferred_element_type=F32)


def dot_nt(a, b):
    return lax.dot_general(a, b, (((1,), (1,)), ((), ())), preferred_element_type=F32)


def dot_tn(a, b):
    return lax.dot_general(a, b, (((0,), (0,)), ((), ())), preferred_element_type=F32)


def iota(shape, axis):
    return lax.broadcasted_iota(jnp.int32, shape, axis)


def gelu_pair(v):
    cdf = 0.5 * lax.erf(v * 0.7071067811865476) + 0.5
    return v * cdf, cdf + v * jnp.exp(v * v * -0.5) * 0.3989422804014327


def normalise(x):
    mean = jnp.sum(x, -1, keepdims=True) * (1.0 / D)
    centered = x - mean
    spread = jnp.sum(centered * centered, -1, keepdims=True) * (1.0 / D)
    rstd = lax.rsqrt(spread + NORM_EPS)
    return centered * rstd, rstd


def normalise_back(grad, gain, xhat, rstd):
    scaled = grad * gain
    first = jnp.sum(scaled, -1, keepdims=True) * (1.0 / D)
    second = jnp.sum(scaled * xhat, -1, keepdims=True) * (1.0 / D)
    return rstd * (scaled - first - xhat * second)


def column_sum(x):
    return jnp.sum(x, 0, keepdims=True)


def load_padded(ref, b):
    x = ref[b].astype(F32)
    return jnp.concatenate([x, jnp.zeros((ROWS - SLOT, D), F32)], 0)


def length_of(groups, b):
    g = groups[b]
    return jnp.where(g == 0, LEN_A, jnp.where(g == 1, LEN_B, LEN_C))


def policy_lanes(keep, length, b):
    row = keep[pl.ds(b, 1), :].astype(F32)
    row = jnp.concatenate([row, jnp.zeros((1, WIDE - SLOT), F32)], 1)
    kept = jnp.broadcast_to(row, (128, WIDE)).T[:ROWS]
    position = iota((ROWS, 128), 0)
    return jnp.where(position == 0, 1.0, jnp.where(position < length, kept, 0.0))


def split_heads(tile):
    left = iota(tile.shape, 1) < 64
    zero = jnp.zeros_like(tile)
    return jnp.concatenate([jnp.where(left, tile, zero), jnp.where(left, zero, tile)], 0)


def diagonal_blocks(x):
    return jnp.concatenate([x[:64, :128], x[64:, 128:]], 0)


def put(ref, base, stride, value):
    rows, columns = value.shape
    for c in range(columns // 128):
        ref[pl.ds(base + c, rows, stride=stride), :] = value[:, c * 128 : (c + 1) * 128]


def put_row(ref, base, value):
    for c in range(value.shape[1] // 128):
        ref[base + c : base + c + 1, :] = value[:, c * 128 : (c + 1) * 128]


def row_of(ref, base, count):
    return jnp.concatenate([ref[base + c : base + c + 1, :] for c in range(count)], 1)


def shifted(ref, base, rows, stride):
    first = ref[pl.ds(base, rows, stride=stride), :]
    second = ref[pl.ds(base + 1, rows, stride=stride), :]
    low = iota((rows, 128), 1) < 64
    return pltpu.roll(jnp.where(low, second, first), 64, 1)


AXES = ("gx", "gy", "gz")


def digits(sizes, axis):
    size, stride, found = sizes[axis], 1, []
    while size > 1:
        base = 2 if size % 2 == 0 else size
        found.append((axis, stride, base))
        size //= base
        stride *= base
    return found


def whole(sizes, axis):
    return [(axis, 1, sizes[axis])] if sizes[axis] > 1 else []


def digit_of(stage):
    axis, stride, base = stage
    return lax.rem(lax.axis_index(axis) // stride, base)


def partners(stage):
    axis, stride, base = stage
    mine = digit_of(stage)
    found = []
    for k in range(1, base):
        other = lax.rem(mine + k, base)
        index = lax.axis_index(axis) + (other - mine) * stride
        found.append((tuple(index if a == axis else lax.axis_index(a) for a in AXES), k - 1, other))
    return found


def greet(sizes):
    barrier = pltpu.get_barrier_semaphore()
    total = 0
    for axis in AXES:
        for stage in whole(sizes, axis):
            for device, _, _ in partners(stage):
                pl.semaphore_signal(barrier, inc=1, device_id=device, device_id_type=MESH)
                total += 1
    return barrier, total


class Piece:
    def __init__(self, name, rows, base, stages):
        self.name, self.rows, self.base, self.stages = name, rows, base, stages
        self.copies = sum(s[2] - 1 for s in stages)

    def steps(self, buffer, landing, sems, free, first, first_stage):
        stages = self.stages
        rows_after = [self.rows]
        for stage in stages:
            rows_after.append(rows_after[-1] // stage[2])
        landing_at, sem_at = [self.base], [first]
        for s, stage in enumerate(stages):
            landing_at.append(landing_at[-1] + (stage[2] - 1) * rows_after[s + 1])
            sem_at.append(sem_at[-1] + stage[2] - 1)

        def place(s):
            begin = self.base
            for i in range(s):
                begin = begin + digit_of(stages[i]) * rows_after[i + 1]
            return begin

        def block(s, digit):
            return pl.ds(pl.multiple_of(place(s) + digit * rows_after[s + 1], 8), rows_after[s + 1])

        def scatter(s):
            found = []
            for device, slot, other in partners(stages[s]):
                found.append(
                    pltpu.make_async_remote_copy(
                        buffer.at[block(s, other), :],
                        landing.at[pl.ds(landing_at[s] + slot * rows_after[s + 1], rows_after[s + 1]), :],
                        sems.at[0, sem_at[s] + slot],
                        sems.at[1, sem_at[s] + slot],
                        device,
                        MESH,
                    )
                )
            return found

        def gather(s):
            found = []
            for device, slot, _ in partners(stages[s]):
                own = buffer.at[block(s, digit_of(stages[s])), :]
                found.append(
                    pltpu.make_async_remote_copy(
                        own, own, sems.at[2, sem_at[s] + slot], sems.at[3, sem_at[s] + slot], device, MESH
                    )
                )
            return found

        def start(copies):
            for copy in copies:
                copy.start()

        def end_scatter(s):
            for copy in scatter(s):
                copy.wait()
            for device, _, _ in partners(stages[s]):
                pl.semaphore_signal(free.at[first_stage + s], inc=1, device_id=device, device_id_type=MESH)
            rows = rows_after[s + 1]
            begin = place(s) + digit_of(stages[s]) * rows
            step = math.gcd(rows, 64)

            def body(i, _):
                own = pl.ds(pl.multiple_of(begin + i * step, 8), step)
                total = buffer[own, :]
                for slot in range(stages[s][2] - 1):
                    at = landing_at[s] + slot * rows
                    total = total + landing[pl.ds(pl.multiple_of(at + i * step, 8), step), :]
                buffer[own, :] = total
                return 0

            lax.fori_loop(0, rows // step, body, 0)

        def end_gather(s):
            for copy in gather(s):
                copy.wait()

        count = len(stages)
        found = []
        for s in range(count):

            def there(s=s):
                if s:
                    end_scatter(s - 1)
                start(scatter(s))

            found.append(there)
        for s in reversed(range(count)):

            def back(s=s):
                if s == count - 1:
                    end_scatter(s)
                else:
                    end_gather(s + 1)
                pl.semaphore_wait(free.at[first_stage + s], stages[s][2] - 1)
                start(gather(s))

            found.append(back)
        if count:
            found.append(lambda: end_gather(0))
        return found


SECTIONS = (
    ("m0", 3072, ((1024, "CGAB"), (1024, "CXHY"), (1024, "CHXY"),)),
    ("m1", 3072, ((3072, "CGH"),)),
    ("m2", 3072, ((3072, "CAXYB"),)),
    ("proj", 1152, ((1280, "CYXAB"),)),
    ("qkv0", 1152, ((1280, "CXAYB"),)),
    ("qkv1", 1152, ((1280, "CYXAB"),)),
    ("qkv2", 1152, ((512, "CAXYB"), (768, "CYXAB"),)),
    ("pred", 1874, ((1280, "CGH"), (768, "CGH"),)),
    ("vecs", 48, ((256, "CGH"),)),
)


def pieces_of(sizes):
    unit = 8 * math.prod(sizes.values())
    core, x, z = digits(sizes, "gy"), digits(sizes, "gx"), digits(sizes, "gz")
    ways = {
        "C": core, "X": x[:1], "Y": x[1:], "A": z[:1], "B": z[1:], "G": whole(sizes, "gx"), "H": whole(sizes, "gz"),
    }
    found, starts, base = [], {}, 0
    for name, rows, parts in SECTIONS:
        starts[name] = base
        if unit > 256 or len(parts) == 1:
            parts = ((rows, parts[0][1]),)
        for i, (part_rows, way) in enumerate(parts):
            stages = [stage for letter in way for stage in ways[letter]]
            part_rows = -(-part_rows // unit) * unit
            found.append(Piece(name + "abcd"[i] if len(parts) > 1 else name, part_rows, base, stages))
            base += part_rows
    return found, starts, base


PART = 512
PARTS = MLP // PART
HALF = ALL // 4


def layer_kernel(
    sizes, pieces, starts,
    groups_in, tokens_in, cotangent_in, keep_in, flat, flat_end,
    mixed, input_gradient, grads, counts,
    w_qkv, w_proj, w_up, w_down, w_in, w_mid, w_low, w_out, vecs, qkv_bias,
    q_all, k_all, v_all, do_all, lse_all, v_turned, o_turned, n1_all, dx_all, acc_vec, acc_small,
    buffer, landing, sems, free, held, landed, count_sems, sem, groups, tokens, cotangent, keep, in_sems,
):
    plan, first, first_stage = {}, 0, 0
    for p in pieces:
        plan[p.name] = p.steps(buffer, landing, sems, free, first, first_stage)
        first += p.copies
        first_stage += len(p.stages)
    done = {p.name: 0 for p in pieces}

    def take(*names):
        found = []
        for name in names:
            if name in plan and done[name] < len(plan[name]):
                found.append(plan[name][done[name]])
                done[name] += 1
        return found

    def run(steps):
        for step in steps:
            step()

    def tick(name):
        run(take(*TICKS.get(name, ())))

    arriving = [
        pltpu.make_async_copy(source, target, in_sems.at[i])
        for i, (source, target) in enumerate(
            ((groups_in, groups), (keep_in, keep), (tokens_in, tokens), (cotangent_in, cotangent))
        )
    ]
    for copy in arriving[:2]:
        copy.start()
    barrier, greetings = greet(sizes)
    count_steps = counting(sizes, groups, keep, counts, held, landed, count_sems)

    def weights(one, two, rows):
        unpack(flat, flat_end, (one, two), rows, sem, arriving[2:], w_qkv, w_proj, w_up, w_down, w_in, w_mid, w_low, w_out, vecs,
               qkv_bias)

    pl.run_scoped(
        weights,
        pltpu.VMEM((CHUNK * 128,), F32),
        pltpu.VMEM((CHUNK * 128,), F32),
        pltpu.VMEM((CHUNK + 8, 128), F32),
    )
    for copy in arriving:
        copy.wait()
    if greetings:
        pl.semaphore_wait(barrier, greetings)
    run(count_steps[:1])

    def vec(r, size=D):
        return vecs[r : r + 1, 0:size]

    acc_vec[...] = jnp.zeros_like(acc_vec)
    acc_small[...] = jnp.zeros_like(acc_small)

    def rows_of(b):
        if isinstance(b, int):
            return slice(b * ROWS, (b + 1) * ROWS)
        return pl.ds(pl.multiple_of(b * ROWS, 16), ROWS)

    x1_all = dx_all

    def first_half(x2_all, dn2_all, n2_all, gd_all, up_part, gup_part, weight):
        def attend(b, _):
            length = length_of(groups, b)
            x = load_padded(tokens, b)
            xhat, _ = normalise(x)
            n1 = (xhat * vec(V_ONE_GAIN) + vec(V_ONE_SHIFT)).astype(BF16)
            n1_all[rows_of(b), :] = n1
            zeros = jnp.zeros((WIDE - ROWS, 128), BF16)
            for p in range(PAIRS):
                part = dot_nn(n1, w_qkv[:, p * D : (p + 1) * D]) + qkv_bias[0:1, p * D : (p + 1) * D]
                q_all[b, p] = jnp.concatenate([part[:, 0:128].astype(BF16) * jnp.array(0.125, BF16), zeros], 0)
                k_all[b, p] = part[:, 128:256].astype(BF16)
                v_all[b, p] = part[:, 256:384].astype(BF16)
                v_turned[p] = part[:, 256:384].T.astype(BF16)

            weight[...] = policy_lanes(keep, length, b)
            row_id = iota((ROWS, 128), 0)
            lane_id = iota((ROWS, 128), 1)

            def pair(p):
                k_pair = k_all[b, p]
                vt = v_turned[p]
                tiles = [slice(128 * t, 128 * (t + 1)) for t in range(3)]
                where = slice(p * 128, (p + 1) * 128)

                def soft(t, s):
                    top = jnp.max(s, 0, keepdims=True)
                    w = jnp.where(row_id == lane_id + 128 * t, 1.0, weight[...])
                    e = jnp.exp(s - top) * jnp.concatenate([w, w], 1)
                    total = jnp.sum(e, 0, keepdims=True)
                    lse_all[b, p, t, 0:1, :] = top + jnp.log(total)
                    return e.astype(BF16), 1.0 / total

                def score(t):
                    return dot_nt(k_pair, split_heads(q_all[b, p, tiles[t], :]))

                def mix(t, e, inverse):
                    o = diagonal_blocks(dot_nn(vt, e) * inverse).astype(BF16)
                    o_turned[b, where, tiles[t]] = o

                s0 = score(0)
                s1 = score(1)
                e0 = soft(0, s0)
                s2 = score(2)
                e1 = soft(1, s1)
                mix(0, *e0)
                e2 = soft(2, s2)
                mix(1, *e1)
                mix(2, *e2)

            for p in range(PAIRS):
                pair(p)
            x1 = x + dot_tn(o_turned[b], w_proj[...])[:ROWS] + vec(V_PROJ_BIAS)
            x1_all[rows_of(b), :] = x1
            x2_all[rows_of(b), :] = x1 + vec(V_DOWN_BIAS)
            dn2_all[rows_of(b), :] = jnp.zeros((ROWS, D), F32)
            xhat2, _ = normalise(x1)
            n2_all[rows_of(b), :] = (xhat2 * vec(V_TWO_GAIN) + vec(V_TWO_SHIFT)).astype(BF16)
            valid = (iota((ROWS, D), 0) < length).astype(F32)
            g = load_padded(cotangent, b) * valid
            gd_all[rows_of(b), :] = g.astype(BF16)
            acc_vec[A_DOWN_BIAS : A_DOWN_BIAS + 1, :] += column_sum(g)
            return 0

        lax.fori_loop(0, IMG, attend, 0)
        run(count_steps[1:2])

        for n in range(PARTS):
            columns = slice(n * PART, (n + 1) * PART)

            def mlp(h):
                rows = slice(h * HALF, (h + 1) * HALF)
                n2 = n2_all[rows, :]
                g_d = gd_all[rows, :]
                u, slope = gelu_pair(dot_nn(n2, w_up[:, columns]) + vecs[V_UP_BIAS : V_UP_BIAS + 1, columns])
                u = u.astype(BF16)
                gu = (slope * dot_nt(g_d, w_down[columns, :])).astype(BF16)
                up_part[rows, :] = u
                gup_part[rows, :] = gu
                acc_small[A_UP_BIAS : A_UP_BIAS + 1, columns] += column_sum(gu.astype(F32))
                x2_all[rows, :] += dot_nn(u, w_down[columns, :])
                dn2_all[rows, :] += dot_nt(gu, w_up[:, columns])

            for h in range(4):
                mlp(h)
                if h % 2:
                    tick(f"part{n}.{h // 2}")

            base = starts[f"m{n}"]
            up = dot_tn(n2_all[...], gup_part[...])
            for c in range(PART // 128):
                buffer[base + c * D : base + (c + 1) * D, :] = up[:, c * 128 : (c + 1) * 128]
            put(buffer, base + 1536, 3, dot_tn(up_part[...], gd_all[...]))
            tick(f"part{n}")

        run(count_steps[2:3])

        def descend(b):
            length = length_of(groups, b)
            valid = (iota((ROWS, D), 0) < length).astype(F32)
            mixed[b] = (x2_all[rows_of(b), :] * valid)[:SLOT].astype(BF16)
            xhat2, rstd2 = normalise(x1_all[rows_of(b), :])
            dn2 = dn2_all[rows_of(b), :]
            acc_vec[A_TWO_GAIN : A_TWO_GAIN + 1, :] += column_sum(dn2 * xhat2)
            acc_vec[A_TWO_SHIFT : A_TWO_SHIFT + 1, :] += column_sum(dn2)
            g = load_padded(cotangent, b) * valid
            dx1 = g + normalise_back(dn2, vec(V_TWO_GAIN), xhat2, rstd2)
            dx_all[rows_of(b), :] = dx1
            g_o = dx1.astype(BF16)
            acc_vec[A_PROJ_BIAS : A_PROJ_BIAS + 1, :] += column_sum(g_o.astype(F32))
            d_o = dot_nt(g_o, w_proj[...]).astype(BF16)
            zeros = jnp.zeros((WIDE - ROWS, 128), BF16)
            for p in range(PAIRS):
                do_all[b, p] = jnp.concatenate([d_o[:, p * 128 : (p + 1) * 128], zeros], 0)

        for b in range(IMG):
            descend(b)
            tick(f"descend{b}")

        below = jnp.zeros((WIDE - ROWS, D), BF16)
        grad_proj = jnp.zeros((D, D), F32)
        for b in range(IMG):
            grad_proj += dot_nn(o_turned[b], jnp.concatenate([dx_all[rows_of(b), :].astype(BF16), below], 0))
        put(buffer, starts["proj"], 3, grad_proj)
        run(count_steps[3:])
        tick("proj")

    pl.run_scoped(
        first_half,
        pltpu.VMEM((ALL, D), F32),
        pltpu.VMEM((ALL, D), F32),
        pltpu.VMEM((ALL, D), BF16),
        pltpu.VMEM((ALL, D), BF16),
        pltpu.VMEM((ALL, PART), BF16),
        pltpu.VMEM((ALL, PART), BF16),
        pltpu.VMEM((ROWS, 128), F32),
    )
    coefficient = counts[2:3, 0:1]

    def second_half(acc_policy, h0_all, ga_all, z_all, g1_all, m1_all, g2_all, m2_all, gl_all, dqkv_all, mid_one,
                    mid_two, low_one):
        acc_policy[...] = jnp.zeros_like(acc_policy)
        row_id = iota((ROWS, 128), 0)
        lane_id = iota((ROWS, 128), 1)

        for p in range(PAIRS):
            def attend(b):
                policy = policy_lanes(keep, length_of(groups, b), b)
                k_pair = k_all[b, p]
                v_pair = v_all[b, p]
                kt = k_pair.T
                tiles = [slice(128 * t, 128 * (t + 1)) for t in range(3)]
                q_two = [split_heads(q_all[b, p, tile, :]) for tile in tiles]
                do_two = [split_heads(do_all[b, p, tile, :]) for tile in tiles]

                def score(t):
                    return dot_nt(k_pair, q_two[t]), dot_nt(v_pair, do_two[t])

                def soft(t, s, dp):
                    f = jnp.exp(s - lse_all[b, p, t, 0:1, :])
                    same = row_id == lane_id + 128 * t
                    w = jnp.where(same, 1.0, policy)
                    prob = f * jnp.concatenate([w, w], 1)
                    centred = dp - jnp.sum(prob * dp, 0, keepdims=True)
                    dw = f * centred
                    acc_policy[b] += jnp.where(same, 0.0, dw[:, :128] + dw[:, 128:])
                    return prob.astype(BF16), (prob * centred).astype(BF16)

                def query(t, ds):
                    dq = diagonal_blocks(dot_nn(kt, ds)).T * 0.125
                    count = min(128, ROWS - 128 * t)
                    first = b * ROWS + 128 * t
                    dqkv_all[pl.ds(first, count), p * D : p * D + 128] = dq[:count].astype(BF16)

                s0 = score(0)
                s1 = score(1)
                p0, d0 = soft(0, *s0)
                s2 = score(2)
                p1, d1 = soft(1, *s1)
                query(0, d0)
                p2, d2 = soft(2, *s2)
                query(1, d1)
                dv = dot_nn(jnp.concatenate([p0, p1, p2], 1), jnp.concatenate(do_two, 0))
                dk = dot_nn(jnp.concatenate([d0, d1, d2], 1), jnp.concatenate(q_two, 0))
                query(2, d2)
                dqkv_all[rows_of(b), p * D + 128 : p * D + 256] = dk.astype(BF16)
                dqkv_all[rows_of(b), p * D + 256 : p * D + 384] = dv.astype(BF16)

            for b in range(IMG):
                attend(b)
                tick(f"pair{p}.{b}")
            dqkv = dqkv_all[:, p * D : (p + 1) * D]
            base = starts[f"qkv{p}"]
            grad = dot_tn(n1_all[...], dqkv)
            for c in range(3):
                buffer[base + c * D : base + (c + 1) * D, :] = grad[:, c * 128 : (c + 1) * 128]
            bias = column_sum(dqkv.astype(F32))
            acc_vec[A_QUERY_BIAS : A_QUERY_BIAS + 1, p * 128 : (p + 1) * 128] = bias[:, 0:128]
            acc_vec[A_VALUE_BIAS : A_VALUE_BIAS + 1, p * 128 : (p + 1) * 128] = bias[:, 256:384]
            tick(f"qkv{p}")

        spatial_of, share_of = {}, {}

        def predict(b):
            length = length_of(groups, b)
            rows = rows_of(b)
            dpolicy = jnp.sum(acc_policy[b], 1, keepdims=True)
            xhat, _ = normalise(load_padded(tokens, b))
            h0 = (xhat * vec(V_PRED_GAIN) + vec(V_PRED_SHIFT)).astype(BF16)
            h0_all[rows, :] = h0
            position = iota((ROWS, 1), 0)
            spatial = jnp.where((position > 0) & (position < length), 1.0, 0.0)
            share = 1.0 / (length - 1).astype(F32)
            act, act_slope = gelu_pair(dot_nn(h0, w_in[...]) + vec(V_IN_BIAS))
            pooled = column_sum(act * spatial) * share
            local = iota((ROWS, D), 1) < D // 2
            z = jnp.where(local, act, pooled).astype(BF16)
            z_all[rows, :] = z
            m1, m1_slope = gelu_pair(dot_nn(z, w_mid[...]) + vec(V_MID_BIAS, 256))
            m1 = m1.astype(BF16)
            m1_all[rows, :] = m1
            m2, m2_slope = gelu_pair(dot_nn(m1, w_low[...]) + vec(V_LOW_BIAS, 128))
            m2 = m2.astype(BF16)
            m2_all[rows, :] = m2
            logits = dot_nt(m2, w_out[...]) + vec(V_OUT_BIAS, 128)
            keep_prob = 1.0 / (1.0 + jnp.exp(logits[:, 1:2] - logits[:, 0:1]))
            drop_prob = 1.0 / (1.0 + jnp.exp(logits[:, 0:1] - logits[:, 1:2]))
            dlog = spatial * (dpolicy + coefficient * spatial) * keep_prob * drop_prob
            lane = iota((ROWS, 128), 1)
            g_l = jnp.where(lane == 0, dlog, jnp.where(lane == 1, -dlog, 0.0)).astype(BF16)
            gl_all[rows, :] = g_l
            g_2 = (m2_slope * dot_nn(g_l, w_out[...])).astype(BF16)
            g2_all[rows, :] = g_2
            g_1 = (m1_slope * dot_nt(g_2, w_low[...])).astype(BF16)
            g1_all[rows, :] = g_1
            dz = dot_nt(g_1, w_mid[...])
            da = jnp.where(local, dz, spatial * share * column_sum(dz))
            g_a = (act_slope * da).astype(BF16)
            ga_all[rows, :] = g_a
            acc_vec[A_IN_BIAS : A_IN_BIAS + 1, :] += column_sum(g_a.astype(F32))
            acc_small[A_MID_BIAS : A_MID_BIAS + 1, 0:256] += column_sum(g_1.astype(F32))
            acc_small[A_LOW_BIAS : A_LOW_BIAS + 1, 0:128] += column_sum(g_2.astype(F32))
            acc_small[A_OUT_BIAS : A_OUT_BIAS + 1, 0:128] += column_sum(g_l.astype(F32))

        for b in range(IMG):
            predict(b)
            tick(f"predict{b}")


        base = starts["pred"]
        put(buffer, base, 3, dot_tn(h0_all[...], ga_all[...]))
        grad_mid = dot_tn(z_all[...], g1_all[...])
        mid_one[...] = grad_mid[:, 0:128]
        mid_two[...] = grad_mid[:, 128:256]
        lane = iota((192, 128), 1)
        odd = pltpu.roll(mid_one[pl.ds(1, 192, stride=2), :], 64, 1)
        buffer[pl.ds(base + ROW_MID, 192, stride=3), :] = mid_one[pl.ds(0, 192, stride=2), :]
        buffer[pl.ds(base + ROW_MID + 1, 192, stride=3), :] = jnp.where(
            lane < 64, mid_two[pl.ds(0, 192, stride=2), :], odd
        )
        buffer[pl.ds(base + ROW_MID + 2, 192, stride=3), :] = jnp.where(
            lane < 64, odd, pltpu.roll(mid_two[pl.ds(1, 192, stride=2), :], 64, 1)
        )
        low_one[...] = dot_tn(m1_all[...], g2_all[...])
        lane = iota((48, 128), 1)
        r0, r1, r2, r3 = (low_one[pl.ds(s, 48, stride=4), :] for s in range(4))
        r1, r2, r3 = pltpu.roll(r1, 96, 1), pltpu.roll(r2, 64, 1), pltpu.roll(r3, 32, 1)
        buffer[pl.ds(base + ROW_LOW, 48, stride=3), :] = jnp.where(lane < 96, r0, r1)
        buffer[pl.ds(base + ROW_LOW + 1, 48, stride=3), :] = jnp.where(lane < 64, r1, r2)
        buffer[pl.ds(base + ROW_LOW + 2, 48, stride=3), :] = jnp.where(lane < 32, r2, r3)
        m2_doubled = dot_nn(m2_all[...], doubling()).astype(BF16)
        both = dot_tn(gl_all[...], m2_doubled)
        head = jnp.where(iota((1, 256), 1) % 2 == 0, both[0:1, :], both[1:2, :])
        buffer[base + ROW_OUT : base + ROW_OUT + 1, :] = head[:, 0:128]
        buffer[base + ROW_OUT + 1 : base + ROW_OUT + 2, :] = pltpu.roll(head[:, 128:256], 64, 1)
        tick("pred")

        def finish(b):
            rows = rows_of(b)
            xhat, rstd = normalise(load_padded(tokens, b))
            dh0 = dot_nt(ga_all[rows, :], w_in[...])
            acc_vec[A_PRED_GAIN : A_PRED_GAIN + 1, :] += column_sum(dh0 * xhat)
            acc_vec[A_PRED_SHIFT : A_PRED_SHIFT + 1, :] += column_sum(dh0)
            dn1 = dot_nt(dqkv_all[rows, :], w_qkv[...])
            acc_vec[A_ONE_GAIN : A_ONE_GAIN + 1, :] += column_sum(dn1 * xhat)
            acc_vec[A_ONE_SHIFT : A_ONE_SHIFT + 1, :] += column_sum(dn1)
            total = (
                dx_all[rows, :]
                + normalise_back(dn1, vec(V_ONE_GAIN), xhat, rstd)
                + normalise_back(dh0, vec(V_PRED_GAIN), xhat, rstd)
            )
            input_gradient[b] = total[:SLOT].astype(BF16)

        for b in range(IMG):
            finish(b)
            tick(f"finish{b}")


    pl.run_scoped(
        second_half,
        pltpu.VMEM((IMG, ROWS, 128), F32),
        pltpu.VMEM((ALL, D), BF16),
        pltpu.VMEM((ALL, D), BF16),
        pltpu.VMEM((ALL, D), BF16),
        pltpu.VMEM((ALL, 256), BF16),
        pltpu.VMEM((ALL, 256), BF16),
        pltpu.VMEM((ALL, 128), BF16),
        pltpu.VMEM((ALL, 128), BF16),
        pltpu.VMEM((ALL, 128), BF16),
        pltpu.VMEM((ALL, 3 * D), BF16),
        pltpu.VMEM((D, 128), F32),
        pltpu.VMEM((D, 128), F32),
        pltpu.VMEM((256, 128), F32),
    )

    base = starts["vecs"]
    lane = iota((1, 128), 1)
    for r, a in enumerate((A_PRED_GAIN, A_PRED_SHIFT, A_IN_BIAS)):
        put_row(buffer, base + 3 * r, acc_vec[a : a + 1, :])
    mid_bias = acc_small[A_MID_BIAS : A_MID_BIAS + 1, 0:256]
    low_bias = pltpu.roll(acc_small[A_LOW_BIAS : A_LOW_BIAS + 1, 0:128], 64, 1)
    out_bias = pltpu.roll(acc_small[A_OUT_BIAS : A_OUT_BIAS + 1, 0:128], 32, 1)
    buffer[base + 9 : base + 10, :] = mid_bias[:, 0:128]
    buffer[base + 10 : base + 11, :] = jnp.where(lane < 64, mid_bias[:, 128:256], low_bias)
    buffer[base + 11 : base + 12, :] = jnp.where(lane < 32, low_bias, out_bias)
    for r, a in enumerate(
        (A_ONE_GAIN, A_ONE_SHIFT, A_QUERY_BIAS, A_VALUE_BIAS, A_PROJ_BIAS, A_TWO_GAIN, A_TWO_SHIFT)
    ):
        put_row(buffer, base + 12 + 3 * r, acc_vec[a : a + 1, :])
    put_row(buffer, base + 33, acc_small[A_UP_BIAS : A_UP_BIAS + 1, :])
    put_row(buffer, base + 45, acc_vec[A_DOWN_BIAS : A_DOWN_BIAS + 1, :])

    def settle(name, ordered):
        base = starts[name]
        if name.startswith("m"):
            n = int(name[1:])
            for c in range(4):
                ordered[pl.ds(ROW_UP + 4 * n + c, D, stride=12), :] = buffer[base + c * D : base + (c + 1) * D, :]
            ordered[ROW_DOWN + 1536 * n : ROW_DOWN + 1536 * (n + 1), :] = buffer[base + 1536 : base + 3072, :]
        elif name.startswith("qkv"):
            p = int(name[3:])
            for c in range(3):
                ordered[pl.ds(ROW_QKV + 3 * c + p, D, stride=9), :] = buffer[base + c * D : base + (c + 1) * D, :]
        else:
            first, rows = {"proj": (ROW_PROJ, 1152), "pred": (0, ROW_QKV), "vecs": (ROW_VEC, 48)}[name]
            ordered[first : first + rows, :] = buffer[base : base + rows, :]

    tick("vecs")
    owner = {}
    for name in plan:
        owner.setdefault(name if name in starts else name[:-1], []).append(name)
    settled = set()

    def hand_over(ordered):
        early = slice(ROW_PROJ // 8 * 8 + 8, ROW_VEC // 8 * 8)
        parts = (early, slice(0, early.start), slice(early.stop, GRAD_ROWS))
        copies = [pltpu.make_async_copy(ordered.at[part, :], grads.at[part, :], sem.at[i]) for i, part in enumerate(parts)]

        def look():
            for section, members in owner.items():
                if section not in settled and all(done[m] == len(plan[m]) for m in members):
                    settle(section, ordered)
                    settled.add(section)
                    if section in EARLY and all(e in settled for e in EARLY):
                        copies[0].start()

        look()
        for name in DRAIN:
            run(take(name))
            look()
        while any(done[n] < len(plan[n]) for n in plan):
            for name in plan:
                run(take(name))
            look()
        for copy in copies[1:]:
            copy.start()
        for copy in copies:
            copy.wait()

    pl.run_scoped(hand_over, pltpu.VMEM((GRAD_ROWS, 128), F32))


EARLY = ("m0", "m1", "m2", "proj")

TICKS = {
    "part0": ("m0a", "m0b", "m0c",),
    "part1.0": ("m0a", "m0b",),
    "part1.1": ("m0c",),
    "part1": ("m1",),
    "part2.1": ("m0a", "m1", "m0b",),
    "part2": ("m2",),
    "descend1": ("m0a",),
    "proj": ("proj", "m0c", "m2",),
    "pair0.1": ("proj", "m0a", "m0b",),
    "qkv0": ("qkv0",),
    "pair1.1": ("m0c", "m1", "qkv0",),
    "pair1.3": ("proj", "m0b", "m0c",),
    "qkv1": ("qkv1", "m2",),
    "pair2.0": ("m0a",),
    "pair2.1": ("m0b", "qkv1", "m0c", "qkv0",),
    "pair2.3": ("proj", "m0a",),
    "qkv2": ("qkv2a", "qkv2b", "m1",),
    "predict0": ("qkv2a", "qkv2b", "qkv1", "m2", "qkv0", "m0b", "m0c", "proj",),
    "predict2": ("m0a", "qkv1", "qkv2a", "qkv2b",),
    "predict3": ("m1", "m0a", "m2", "m0b", "qkv0",),
    "pred": ("preda", "predb", "qkv2a", "qkv2b", "m0b",),
    "finish1": ("qkv1", "preda", "proj", "m0c", "predb",),
    "finish3": ("m2", "m0c", "qkv2b",),
    "vecs": ("vecs", "qkv0",),
}
DRAIN = (
    "qkv1", "vecs", "proj", "qkv2a", "m1", "m2", "qkv2b", "qkv0", "m1", "proj", "qkv1", "qkv2a", "preda",
    "qkv2b", "qkv1", "predb", "vecs", "qkv2a", "proj", "m2", "qkv2b", "qkv0", "qkv2a", "preda", "qkv1",
    "predb", "vecs", "qkv0", "proj", "m2", "proj", "qkv2b", "qkv2a", "preda", "qkv1", "predb", "vecs", "qkv1",
    "qkv0", "qkv2b", "qkv0", "qkv2b", "preda", "m2", "preda", "predb", "qkv2a", "vecs", "m2", "predb",
    "qkv2a", "vecs",
)

(
    V_PRED_GAIN, V_PRED_SHIFT, V_IN_BIAS, V_MID_BIAS, V_LOW_BIAS, V_OUT_BIAS, V_ONE_GAIN, V_ONE_SHIFT, V_PROJ_BIAS,
    V_TWO_GAIN, V_TWO_SHIFT, V_UP_BIAS, V_DOWN_BIAS,
) = range(13)
(
    A_PRED_GAIN, A_PRED_SHIFT, A_IN_BIAS, A_ONE_GAIN, A_ONE_SHIFT, A_QUERY_BIAS, A_VALUE_BIAS, A_PROJ_BIAS, A_TWO_GAIN,
    A_TWO_SHIFT, A_DOWN_BIAS,
) = range(11)
A_UP_BIAS, A_MID_BIAS, A_LOW_BIAS, A_OUT_BIAS = range(4)


def doubling():
    return (iota((128, 256), 1) // 2 == iota((128, 256), 0)).astype(F32).astype(BF16)


CHUNK = 5952
CHUNKS = ((10944, 4800), (0, 5376), (5328, 5952))


def unpack(flat, flat_end, flat_one, rows, sems, others, w_qkv, w_proj, w_up, w_down, w_in, w_mid, w_low, w_out, vecs, qkv_bias):
    copies = [
        pltpu.make_async_copy(
            flat.at[pl.ds(start * 128, count * 128)], flat_one[i % 2].at[pl.ds(0, count * 128)], sems.at[i]
        )
        for i, (start, count) in enumerate(CHUNKS)
    ]

    def spread(i):
        copies[i].wait()

        def body(k, _):
            rows[pl.ds(pl.multiple_of(k * 192, 192), 192), :] = flat_one[i % 2][
                pl.ds(pl.multiple_of(k * 24576, 24576), 24576)
            ].reshape(192, 128)
            return 0

        lax.fori_loop(0, CHUNKS[i][1] // 192, body, 0)

    copies[0].start()
    copies[1].start()
    for copy in others:
        copy.start()
    spread(0)
    copies[2].start()
    start, count = CHUNKS[0]
    rows[count : count + 8, :] = flat_end[...].reshape(8, 128)
    for c in range(3):
        w_down[:, c * 128 : (c + 1) * 128] = shifted(rows, ROW_DOWN - 1 + c - start, MLP, 3).astype(BF16)
    lane = iota((16, 128), 1)
    at = 15697 - start
    vec_one = pltpu.roll(jnp.where(lane < 64, rows[at + 1 : at + 17, :], rows[at : at + 16, :]), 64, 1)
    lane = iota((36, 128), 1)
    at = 15708 - start
    vec_two = pltpu.roll(jnp.where(lane < 98, rows[at + 1 : at + 37, :], rows[at : at + 36, :]), 30, 1)
    rows[0:16, :] = vec_one
    rows[16:52, :] = vec_two
    for r, base in (
        (V_PRED_GAIN, 0), (V_PRED_SHIFT, 3), (V_IN_BIAS, 6), (V_ONE_GAIN, 16), (V_ONE_SHIFT, 19), (V_PROJ_BIAS, 28),
        (V_TWO_GAIN, 31), (V_TWO_SHIFT, 34), (V_DOWN_BIAS, 49),
    ):
        vecs[r : r + 1, 0:D] = row_of(rows, base, 3)
    vecs[V_UP_BIAS : V_UP_BIAS + 1, :] = row_of(rows, 37, 12)
    lane = iota((1, 128), 1)
    zero = jnp.zeros((1, 128), F32)
    r9, r10, r11 = (rows[r : r + 1, :] for r in (9, 10, 11))
    vecs[V_MID_BIAS : V_MID_BIAS + 1, 0:128] = r9
    vecs[V_MID_BIAS : V_MID_BIAS + 1, 128:256] = jnp.where(lane < 64, r10, zero)
    vecs[V_LOW_BIAS : V_LOW_BIAS + 1, 0:128] = jnp.where(
        lane < 96, pltpu.roll(jnp.where(lane < 64, r11, r10), 64, 1), zero
    )
    vecs[V_OUT_BIAS : V_OUT_BIAS + 1, 0:128] = jnp.where(lane < 2, pltpu.roll(r11, 96, 1), zero)
    for p in range(PAIRS):
        qkv_bias[0:1, p * D : p * D + 128] = rows[22 + p : 23 + p, :]
        qkv_bias[0:1, p * D + 128 : p * D + 256] = zero
        qkv_bias[0:1, p * D + 256 : p * D + 384] = rows[25 + p : 26 + p, :]

    spread(1)
    for c in range(3):
        w_in[:, c * 128 : (c + 1) * 128] = rows[pl.ds(c, D, stride=3), :].astype(BF16)
        for p in range(PAIRS):
            tile = shifted(rows, ROW_QKV - 1 + 3 * c + p, D, 9).astype(BF16)
            w_qkv[:, p * D + c * 128 : p * D + (c + 1) * 128] = tile

    a, b, c = (rows[pl.ds(ROW_MID + s, 192, stride=3), :] for s in range(3))
    lane = iota((192, 128), 1)
    zero = jnp.zeros((192, 128), F32)

    def interleave(tiles):
        count = len(tiles)
        size = tiles[0].shape[0]
        for s, tile in enumerate(tiles):
            rows[pl.ds(s, size, stride=count), :] = tile
        return rows[0 : size * count, :].astype(BF16)

    w_mid[:, 0:128] = interleave((a, pltpu.roll(jnp.where(lane < 64, c, b), 64, 1)))
    w_mid[:, 128:256] = interleave(
        (jnp.where(lane < 64, b, zero), jnp.where(lane < 64, pltpu.roll(c, 64, 1), zero))
    )
    lane = iota((48, 128), 1)
    a, b, c = (rows[pl.ds(ROW_LOW + s, 48, stride=3), :] for s in range(3))
    low = (
        a,
        jnp.where(lane < 32, pltpu.roll(a, 32, 1), pltpu.roll(b, 32, 1)),
        jnp.where(lane < 64, pltpu.roll(b, 64, 1), pltpu.roll(c, 64, 1)),
        pltpu.roll(c, 96, 1),
    )
    w_low[0:192, :] = interleave([jnp.where(lane < 96, tile, 0.0) for tile in low])
    w_low[192:256, :] = jnp.zeros((64, 128), BF16)
    head = jnp.concatenate([rows[ROW_OUT : ROW_OUT + 1, :], rows[ROW_OUT + 1 : ROW_OUT + 2, :]], 1)
    head = jnp.broadcast_to(head, (128, 256))
    lane = iota((128, 256), 1)
    chosen = (lane % 2 == iota((128, 256), 0)) & (lane < 192)
    w_out[...] = dot_nt(jnp.where(chosen, head, 0.0).astype(BF16), doubling()).astype(BF16)

    spread(2)
    start = CHUNKS[2][0]
    for c in range(3):
        w_proj[:, c * 128 : (c + 1) * 128] = shifted(rows, ROW_PROJ - 1 + c - start, D, 3).astype(BF16)
    for c in range(12):
        w_up[:, c * 128 : (c + 1) * 128] = shifted(rows, ROW_UP - 1 + c - start, D, 12).astype(BF16)


def counting(sizes, groups, keep, out, held, landed, sems):
    stages = [s for axis in ("gy", "gx", "gz") for s in whole(sizes, axis)]
    first = [0]
    for stage in stages:
        first.append(first[-1] + stage[2] - 1)

    def copies(s):
        return [
            pltpu.make_async_remote_copy(
                held.at[s], landed.at[first[s] + slot], sems.at[0, first[s] + slot], sems.at[1, first[s] + slot],
                device, MESH,
            )
            for device, slot, _ in partners(stages[s])
        ]

    def begin():
        kept = jnp.zeros((1, 1), F32)
        valid = jnp.zeros((1, 1), F32)
        position = iota((1, SLOT), 1)
        for b in range(IMG):
            spatial = jnp.where((position > 0) & (position < length_of(groups, b)), 1.0, 0.0)
            kept += jnp.sum(spatial * keep[b : b + 1, :].astype(F32), keepdims=True)
            valid += jnp.sum(spatial, keepdims=True)
        row = iota((8, 128), 0)
        held[0] = jnp.where(row == 0, kept, jnp.where(row == 1, valid, 0.0))

    def step(s):
        if s == 0:
            begin()
        else:
            total = held[s - 1]
            for slot, copy in enumerate(copies(s - 1)):
                copy.wait()
                total = total + landed[first[s - 1] + slot]
            held[s] = total
        if s < len(stages):
            for copy in copies(s):
                copy.start()
        else:
            total = held[s]
            row = iota((8, 128), 0)
            excess = total[0:1, :] / total[1:2, :] - KEEP_TARGET
            loss = RATIO_WEIGHT * total[1:2, :] * excess * excess
            out[...] = jnp.where(row == 2, 2.0 * RATIO_WEIGHT * excess, jnp.where(row == 3, loss, total))

    return [functools.partial(step, s) for s in range(len(stages) + 1)]


def layer(sizes, *operands):
    pieces, starts, rows = pieces_of(sizes)
    copies = max(sum(p.copies for p in pieces), 1)
    fits = rows <= 17408
    small = max(sum(sizes[a] - 1 for a in AXES), 1)
    vmem = pl.BlockSpec(memory_space=pltpu.VMEM)
    hbm = pl.BlockSpec(memory_space=pltpu.HBM)
    shape = jax.ShapeDtypeStruct
    return pl.pallas_call(
        functools.partial(layer_kernel, sizes, pieces, starts),
        grid=(1,),
        out_shape=(
            shape((IMG, SLOT, D), BF16),
            shape((IMG, SLOT, D), BF16),
            pltpu.VMEM((GRAD_ROWS, 128), F32) if fits else shape((GRAD_ROWS, 128), F32),
            shape((8, 128), F32),
        ),
        in_specs=[
            hbm, hbm, hbm, hbm, hbm,
            pl.BlockSpec((1024,), lambda i: (NPARAM // 1024,)),
        ],
        out_specs=[vmem, vmem, pl.BlockSpec(memory_space=pl.ANY), vmem],
        scratch_shapes=[
            pltpu.VMEM((D, 3 * D), BF16),
            pltpu.VMEM((D, D), BF16),
            pltpu.VMEM((D, MLP), BF16),
            pltpu.VMEM((MLP, D), BF16),
            pltpu.VMEM((D, D), BF16),
            pltpu.VMEM((D, 256), BF16),
            pltpu.VMEM((256, 128), BF16),
            pltpu.VMEM((128, 128), BF16),
            pltpu.VMEM((16, MLP), F32),
            pltpu.VMEM((8, 3 * D), F32),
            pltpu.VMEM((IMG, PAIRS, WIDE, 128), BF16),
            pltpu.VMEM((IMG, PAIRS, ROWS, 128), BF16),
            pltpu.VMEM((IMG, PAIRS, ROWS, 128), BF16),
            pltpu.VMEM((IMG, PAIRS, WIDE, 128), BF16),
            pltpu.VMEM((IMG, PAIRS, 3, 8, 256), F32),
            pltpu.VMEM((PAIRS, 128, ROWS), BF16),
            pltpu.VMEM((IMG, D, WIDE), BF16),
            pltpu.VMEM((ALL, D), BF16),
            pltpu.VMEM((ALL, D), F32),
            pltpu.VMEM((16, D), F32),
            pltpu.VMEM((8, MLP), F32),
            pltpu.VMEM((rows, 128), F32),
            pltpu.VMEM((rows, 128), F32),
            pltpu.SemaphoreType.DMA((4, copies)),
            pltpu.SemaphoreType.REGULAR((max(sum(len(p.stages) for p in pieces), 1),)),
            pltpu.VMEM((4, 8, 128), F32),
            pltpu.VMEM((small, 8, 128), F32),
            pltpu.SemaphoreType.DMA((2, small)),
            pltpu.SemaphoreType.DMA((3,)),
            pltpu.SMEM((IMG,), jnp.int32),
            pltpu.VMEM((IMG, SLOT, D), BF16),
            pltpu.VMEM((IMG, SLOT, D), BF16),
            pltpu.VMEM((IMG, SLOT), jnp.int32),
            pltpu.SemaphoreType.DMA((4,)),
        ],
        compiler_params=pltpu.CompilerParams(
            collective_id=0, has_side_effects=True, vmem_limit_bytes=(50 if fits else 58) << 20
        ),
        name="layer",
    )(*operands)


UPDATE_ROWS = 2304


def update_kernel(
    grads, after, counts, mixed_in, gradient_in, params, momentum, average,
    new_params, new_momentum, new_average, mixed, input_gradient, loss, block, joined,
):
    i = pl.program_id(0)
    n = UPDATE_ROWS
    mixed[...] = mixed_in[...]
    input_gradient[...] = gradient_in[...]
    loss[0, 0] = counts[3, 0]
    joined[0:n, :] = grads[...]
    joined[n : n + 8, :] = after[...]
    here = joined[0:n, :]
    row = iota((n, 128), 0) + i * n
    lane = iota((n, 128), 1)
    moved = pltpu.roll(jnp.where(lane < 64, joined[1 : n + 1, :], here), 64, 1)
    flat = jnp.where(row < ROW_QKV - 1, here, moved)
    joined[0:n, :] = flat

    @pl.when(i == pl.num_programs(0) - 1)
    def _():
        first = 15708 - (NPARAM // (n * 128)) * n
        lane = iota((40, 128), 1)
        one = grads[first + 1 : first + 41, :]
        two = grads[first + 2 : first + 42, :]
        tail = pltpu.roll(jnp.where(lane < 30, two, one), 98, 1)
        keep_old = (iota((40, 128), 0) == 0) & (lane < 98)
        joined[first : first + 40, :] = jnp.where(keep_old, joined[first : first + 40, :], tail)
        block[...] = grads[first + 2 : first + 38, :].reshape(4608)

    g = joined[0:n, :].reshape(n * 128)
    moment = MOMENTUM_DECAY * momentum[...] + g
    value = params[...] - LEARN_RATE * (g + MOMENTUM_DECAY * moment)
    new_momentum[...] = moment
    new_params[...] = value
    new_average[...] = AVERAGE_DECAY * average[...] + (1.0 - AVERAGE_DECAY) * value


def update(grads, counts, mixed, input_gradient, params, momentum, average):
    others = (mixed, input_gradient, params, momentum, average)
    n = UPDATE_ROWS
    flat = pl.BlockSpec((n * 128,), lambda i: (i,))
    image = pl.BlockSpec((1, SLOT, D), lambda i: (jnp.minimum(i, IMG - 1), 0, 0))
    out = jax.ShapeDtypeStruct((NPARAM,), F32)
    return pl.pallas_call(
        update_kernel,
        grid=(pl.cdiv(NPARAM, n * 128),),
        out_shape=(
            out, out, out,
            jax.ShapeDtypeStruct(mixed.shape, BF16),
            jax.ShapeDtypeStruct(mixed.shape, BF16),
            jax.ShapeDtypeStruct((1, 1), F32),
            jax.ShapeDtypeStruct((4608,), F32),
        ),
        in_specs=[
            pl.BlockSpec((n, 128), lambda i: (i, 0)),
            pl.BlockSpec((8, 128), lambda i: ((i + 1) * (n // 8), 0)),
            pl.BlockSpec((8, 128), lambda i: (0, 0)),
            image,
            image,
            flat,
            flat,
            flat,
        ],
        out_specs=[
            flat, flat, flat, image, image,
            pl.BlockSpec(memory_space=pltpu.SMEM),
            pl.BlockSpec((4608,), lambda i: (0,)),
        ],
        scratch_shapes=[pltpu.VMEM((n + 8, 128), F32)],
        compiler_params=pltpu.CompilerParams(vmem_limit_bytes=28 << 20),
        name="update",
    )(grads, grads, *(pltpu.with_memory_space_constraint(x, pltpu.HBM) for x in (counts, *others)))


GRAD_ROWS = -(-(NPARAM // 128 + 40) // UPDATE_ROWS) * UPDATE_ROWS + 8


def solution(mesh):
    sizes = dict(mesh.shape)

    def per_device(tokens, cotangent, groups, keep_mask, params, momentum, average):
        mixed, input_gradient, grads, counts = layer(sizes, groups, tokens, cotangent, keep_mask, params, params)
        new_params, new_momentum, new_average, mixed, input_gradient, loss, block = update(
            grads, counts, mixed, input_gradient, params, momentum, average
        )
        return (mixed, input_gradient, loss.reshape(()), new_params, new_momentum, new_average, block)

    split = P(("gx", "gy", "gz"))
    return jax.shard_map(
        per_device,
        mesh=mesh,
        in_specs=(split, split, split, split, P(), P(), P()),
        out_specs=(split, split, P(), P(), P(), P(), P()),
        check_vma=False,
    )
```

```python
import functools
import math

import jax
import jax.numpy as jnp
from jax import lax
from jax.experimental import pallas as pl
from jax.experimental.pallas import tpu as pltpu
from jax.sharding import PartitionSpec as P

MESH = pl.DeviceIdType.MESH
F32 = jnp.float32
BF16 = jnp.bfloat16

D = 384
HEADS = 6
PAIRS = 3
MLP = 1536
LEN_A, LEN_B, LEN_C = 101, 197, 325
IMG = 4
SLOT = 328
ROWS = 336
WIDE = 384
ALL = IMG * ROWS
NPARAM = 2015330
NORM_EPS = 1e-06
RATIO_WEIGHT = 2.0
KEEP_TARGET = 0.7
MOMENTUM_DECAY = 0.5
AVERAGE_DECAY = 0.5
LEARN_RATE = 0.0001

ROW_MID = 1152
ROW_LOW = 1728
ROW_OUT = 1872
ROW_QKV = 1874
ROW_PROJ = 5330
ROW_UP = 6482
ROW_DOWN = 11090
ROW_VEC = 15698
ROW_BLOCK = 15710
EARLY_BASE = 5328
EARLY_ROWS = 10376
FLAT_ROWS = 15752


def dot_nn(a, b):
    return lax.dot_general(a, b, (((1,), (0,)), ((), ())), preferred_element_type=F32)


def dot_nt(a, b):
    return lax.dot_general(a, b, (((1,), (1,)), ((), ())), preferred_element_type=F32)


def dot_tn(a, b):
    return lax.dot_general(a, b, (((0,), (0,)), ((), ())), preferred_element_type=F32)


def iota(shape, axis):
    return lax.broadcasted_iota(jnp.int32, shape, axis)


def gelu_pair(v):
    cdf = 0.5 * lax.erf(v * 0.7071067811865476) + 0.5
    return v * cdf, cdf + v * jnp.exp(v * v * -0.5) * 0.3989422804014327


def normalise(x):
    mean = jnp.sum(x, -1, keepdims=True) * (1.0 / D)
    centered = x - mean
    spread = jnp.sum(centered * centered, -1, keepdims=True) * (1.0 / D)
    rstd = lax.rsqrt(spread + NORM_EPS)
    return centered * rstd, rstd


def normalise_back(grad, gain, xhat, rstd):
    scaled = grad * gain
    first = jnp.sum(scaled, -1, keepdims=True) * (1.0 / D)
    second = jnp.sum(scaled * xhat, -1, keepdims=True) * (1.0 / D)
    return rstd * (scaled - first - xhat * second)


def column_sum(x):
    return jnp.sum(x, 0, keepdims=True)


def load_padded(ref, b):
    x = ref[b].astype(F32)
    return jnp.concatenate([x, jnp.zeros((ROWS - SLOT, D), F32)], 0)


def length_of(groups, b):
    g = groups[b]
    return jnp.where(g == 0, LEN_A, jnp.where(g == 1, LEN_B, LEN_C))


def policy_lanes(keep, length, b):
    row = keep[pl.ds(b, 1), :].astype(F32)
    row = jnp.concatenate([row, jnp.zeros((1, WIDE - SLOT), F32)], 1)
    kept = jnp.broadcast_to(row, (128, WIDE)).T[:ROWS]
    position = iota((ROWS, 128), 0)
    return jnp.where(position == 0, 1.0, jnp.where(position < length, kept, 0.0))


def split_heads(tile):
    left = iota(tile.shape, 1) < 64
    zero = jnp.zeros_like(tile)
    return jnp.concatenate([jnp.where(left, tile, zero), jnp.where(left, zero, tile)], 0)


def diagonal_blocks(x):
    return jnp.concatenate([x[:64, :128], x[64:, 128:]], 0)


def put(ref, base, stride, value):
    rows, columns = value.shape
    for c in range(columns // 128):
        ref[pl.ds(base + c, rows, stride=stride), :] = value[:, c * 128 : (c + 1) * 128]


def put_row(ref, base, value):
    for c in range(value.shape[1] // 128):
        ref[base + c : base + c + 1, :] = value[:, c * 128 : (c + 1) * 128]


def row_of(ref, base, count):
    return jnp.concatenate([ref[base + c : base + c + 1, :] for c in range(count)], 1)


def shifted(ref, base, rows, stride):
    first = ref[pl.ds(base, rows, stride=stride), :]
    second = ref[pl.ds(base + 1, rows, stride=stride), :]
    low = iota((rows, 128), 1) < 64
    return pltpu.roll(jnp.where(low, second, first), 64, 1)


AXES = ("gx", "gy", "gz")


def digits(sizes, axis):
    size, stride, found = sizes[axis], 1, []
    while size > 1:
        base = 2 if size % 2 == 0 else size
        found.append((axis, stride, base))
        size //= base
        stride *= base
    return found


def whole(sizes, axis):
    return [(axis, 1, sizes[axis])] if sizes[axis] > 1 else []


def digit_of(stage):
    axis, stride, base = stage
    return lax.rem(lax.axis_index(axis) // stride, base)


def partners(stage):
    axis, stride, base = stage
    mine = digit_of(stage)
    found = []
    for k in range(1, base):
        other = lax.rem(mine + k, base)
        index = lax.axis_index(axis) + (other - mine) * stride
        found.append((tuple(index if a == axis else lax.axis_index(a) for a in AXES), k - 1, other))
    return found


def greet(sizes):
    barrier = pltpu.get_barrier_semaphore()
    total = 0
    for axis in AXES:
        for stage in whole(sizes, axis):
            for device, _, _ in partners(stage):
                pl.semaphore_signal(barrier, inc=1, device_id=device, device_id_type=MESH)
                total += 1
    return barrier, total


class Piece:
    def __init__(self, name, rows, base, stages):
        self.name, self.rows, self.base, self.stages = name, rows, base, stages
        self.copies = sum(s[2] - 1 for s in stages)

    def steps(self, buffer, landing, sems, free, first, first_stage):
        stages = self.stages
        rows_after = [self.rows]
        for stage in stages:
            rows_after.append(rows_after[-1] // stage[2])
        landing_at, sem_at = [self.base], [first]
        for s, stage in enumerate(stages):
            landing_at.append(landing_at[-1] + (stage[2] - 1) * rows_after[s + 1])
            sem_at.append(sem_at[-1] + stage[2] - 1)

        def place(s):
            begin = self.base
            for i in range(s):
                begin = begin + digit_of(stages[i]) * rows_after[i + 1]
            return begin

        def block(s, digit):
            return pl.ds(pl.multiple_of(place(s) + digit * rows_after[s + 1], 8), rows_after[s + 1])

        def scatter(s):
            found = []
            for device, slot, other in partners(stages[s]):
                found.append(
                    pltpu.make_async_remote_copy(
                        buffer.at[block(s, other), :],
                        landing.at[pl.ds(landing_at[s] + slot * rows_after[s + 1], rows_after[s + 1]), :],
                        sems.at[0, sem_at[s] + slot],
                        sems.at[1, sem_at[s] + slot],
                        device,
                        MESH,
                    )
                )
            return found

        def gather(s):
            found = []
            for device, slot, _ in partners(stages[s]):
                own = buffer.at[block(s, digit_of(stages[s])), :]
                found.append(
                    pltpu.make_async_remote_copy(
                        own, own, sems.at[2, sem_at[s] + slot], sems.at[3, sem_at[s] + slot], device, MESH
                    )
                )
            return found

        def start(copies):
            for copy in copies:
                copy.start()

        def end_scatter(s):
            for copy in scatter(s):
                copy.wait()
            for device, _, _ in partners(stages[s]):
                pl.semaphore_signal(free.at[first_stage + s], inc=1, device_id=device, device_id_type=MESH)
            rows = rows_after[s + 1]
            begin = place(s) + digit_of(stages[s]) * rows
            step = math.gcd(rows, 64)

            def body(i, _):
                own = pl.ds(pl.multiple_of(begin + i * step, 8), step)
                total = buffer[own, :]
                for slot in range(stages[s][2] - 1):
                    at = landing_at[s] + slot * rows
                    total = total + landing[pl.ds(pl.multiple_of(at + i * step, 8), step), :]
                buffer[own, :] = total
                return 0

            lax.fori_loop(0, rows // step, body, 0)

        def end_gather(s):
            for copy in gather(s):
                copy.wait()

        count = len(stages)
        found = []
        for s in range(count):

            def there(s=s):
                if s:
                    end_scatter(s - 1)
                start(scatter(s))

            found.append(there)
        for s in reversed(range(count)):

            def back(s=s):
                if s == count - 1:
                    end_scatter(s)
                else:
                    end_gather(s + 1)
                pl.semaphore_wait(free.at[first_stage + s], stages[s][2] - 1)
                start(gather(s))

            found.append(back)
        if count:
            found.append(lambda: end_gather(0))
        return found


SECTIONS = (
    ("m0", 3072, ((1024, "CGAB"), (1024, "CXHY"), (1024, "CHXY"),)),
    ("m1", 3072, ((3072, "CGH"),)),
    ("m2", 3072, ((3072, "CAXYB"),)),
    ("proj", 1152, ((1280, "CYXAB"),)),
    ("qkv0", 1152, ((1280, "CXAYB"),)),
    ("qkv1", 1152, ((1280, "CYXAB"),)),
    ("qkv2", 1152, ((512, "CAXYB"), (768, "CYXAB"),)),
    ("pred", 1874, ((1280, "CGH"), (768, "CGH"),)),
    ("vecs", 48, ((256, "CGH"),)),
)


def pieces_of(sizes):
    unit = 8 * math.prod(sizes.values())
    core, x, z = digits(sizes, "gy"), digits(sizes, "gx"), digits(sizes, "gz")
    ways = {
        "C": core, "X": x[:1], "Y": x[1:], "A": z[:1], "B": z[1:], "G": whole(sizes, "gx"), "H": whole(sizes, "gz"),
    }
    found, starts, base = [], {}, 0
    for name, rows, parts in SECTIONS:
        starts[name] = base
        if unit > 256 or len(parts) == 1:
            parts = ((rows, parts[0][1]),)
        for i, (part_rows, way) in enumerate(parts):
            stages = [stage for letter in way for stage in ways[letter]]
            part_rows = -(-part_rows // unit) * unit
            found.append(Piece(name + "abcd"[i] if len(parts) > 1 else name, part_rows, base, stages))
            base += part_rows
    return found, starts, base


PART = 512
PARTS = MLP // PART
HALF = ALL // 4


def layer_kernel(
    sizes, pieces, starts,
    groups_in, tokens_in, cotangent_in, keep_in, flat, flat_end,
    mixed, input_gradient, grads, counts,
    w_qkv, w_proj, w_up, w_down, w_in, w_mid, w_low, w_out, vecs, qkv_bias,
    q_all, k_all, v_all, do_all, lse_all, v_turned, o_turned, n1_all, dx_all, acc_vec, acc_small,
    buffer, landing, sems, free, held, landed, count_sems, sem, groups, tokens, cotangent, keep, in_sems,
):
    plan, first, first_stage = {}, 0, 0
    for p in pieces:
        plan[p.name] = p.steps(buffer, landing, sems, free, first, first_stage)
        first += p.copies
        first_stage += len(p.stages)
    done = {p.name: 0 for p in pieces}

    def take(*names):
        found = []
        for name in names:
            if name in plan and done[name] < len(plan[name]):
                found.append(plan[name][done[name]])
                done[name] += 1
        return found

    def run(steps):
        for step in steps:
            step()

    def tick(name):
        run(take(*TICKS.get(name, ())))

    arriving = [
        pltpu.make_async_copy(source, target, in_sems.at[i])
        for i, (source, target) in enumerate(
            ((groups_in, groups), (keep_in, keep), (tokens_in, tokens), (cotangent_in, cotangent))
        )
    ]
    for copy in arriving[:2]:
        copy.start()
    barrier, greetings = greet(sizes)
    count_steps = counting(sizes, groups, keep, counts, held, landed, count_sems)

    def weights(one, two, rows):
        unpack(flat, flat_end, (one, two), rows, sem, arriving[2:], w_qkv, w_proj, w_up, w_down, w_in, w_mid, w_low, w_out, vecs,
               qkv_bias)

    pl.run_scoped(
        weights,
        pltpu.VMEM((CHUNK * 128,), F32),
        pltpu.VMEM((CHUNK * 128,), F32),
        pltpu.VMEM((CHUNK + 8, 128), F32),
    )
    for copy in arriving:
        copy.wait()
    if greetings:
        pl.semaphore_wait(barrier, greetings)
    run(count_steps[:1])

    def vec(r, size=D):
        return vecs[r : r + 1, 0:size]

    acc_vec[...] = jnp.zeros_like(acc_vec)
    acc_small[...] = jnp.zeros_like(acc_small)

    def rows_of(b):
        if isinstance(b, int):
            return slice(b * ROWS, (b + 1) * ROWS)
        return pl.ds(pl.multiple_of(b * ROWS, 16), ROWS)

    x1_all = dx_all

    def first_half(x2_all, dn2_all, n2_all, gd_all, up_part, gup_part, weight):
        def attend(b, _):
            length = length_of(groups, b)
            x = load_padded(tokens, b)
            xhat, _ = normalise(x)
            n1 = (xhat * vec(V_ONE_GAIN) + vec(V_ONE_SHIFT)).astype(BF16)
            n1_all[rows_of(b), :] = n1
            zeros = jnp.zeros((WIDE - ROWS, 128), BF16)
            for p in range(PAIRS):
                part = dot_nn(n1, w_qkv[:, p * D : (p + 1) * D]) + qkv_bias[0:1, p * D : (p + 1) * D]
                q_all[b, p] = jnp.concatenate([part[:, 0:128].astype(BF16) * jnp.array(0.125, BF16), zeros], 0)
                k_all[b, p] = part[:, 128:256].astype(BF16)
                v_all[b, p] = part[:, 256:384].astype(BF16)
                v_turned[p] = part[:, 256:384].T.astype(BF16)

            weight[...] = policy_lanes(keep, length, b)
            row_id = iota((ROWS, 128), 0)
            lane_id = iota((ROWS, 128), 1)

            def pair(p):
                k_pair = k_all[b, p]
                vt = v_turned[p]
                tiles = [slice(128 * t, 128 * (t + 1)) for t in range(3)]
                where = slice(p * 128, (p + 1) * 128)

                def soft(t, s):
                    top = jnp.max(s, 0, keepdims=True)
                    w = jnp.where(row_id == lane_id + 128 * t, 1.0, weight[...])
                    e = jnp.exp(s - top) * jnp.concatenate([w, w], 1)
                    total = jnp.sum(e, 0, keepdims=True)
                    lse_all[b, p, t, 0:1, :] = top + jnp.log(total)
                    return e.astype(BF16), 1.0 / total

                def score(t):
                    return dot_nt(k_pair, split_heads(q_all[b, p, tiles[t], :]))

                def mix(t, e, inverse):
                    o = diagonal_blocks(dot_nn(vt, e) * inverse).astype(BF16)
                    o_turned[b, where, tiles[t]] = o

                s0 = score(0)
                s1 = score(1)
                e0 = soft(0, s0)
                s2 = score(2)
                e1 = soft(1, s1)
                mix(0, *e0)
                e2 = soft(2, s2)
                mix(1, *e1)
                mix(2, *e2)

            for p in range(PAIRS):
                pair(p)
            x1 = x + dot_tn(o_turned[b], w_proj[...])[:ROWS] + vec(V_PROJ_BIAS)
            x1_all[rows_of(b), :] = x1
            x2_all[rows_of(b), :] = x1 + vec(V_DOWN_BIAS)
            dn2_all[rows_of(b), :] = jnp.zeros((ROWS, D), F32)
            xhat2, _ = normalise(x1)
            n2_all[rows_of(b), :] = (xhat2 * vec(V_TWO_GAIN) + vec(V_TWO_SHIFT)).astype(BF16)
            valid = (iota((ROWS, D), 0) < length).astype(F32)
            g = load_padded(cotangent, b) * valid
            gd_all[rows_of(b), :] = g.astype(BF16)
            acc_vec[A_DOWN_BIAS : A_DOWN_BIAS + 1, :] += column_sum(g)
            return 0

        lax.fori_loop(0, IMG, attend, 0)
        run(count_steps[1:2])

        for n in range(PARTS):
            columns = slice(n * PART, (n + 1) * PART)

            def mlp(h):
                rows = slice(h * HALF, (h + 1) * HALF)
                n2 = n2_all[rows, :]
                g_d = gd_all[rows, :]
                u, slope = gelu_pair(dot_nn(n2, w_up[:, columns]) + vecs[V_UP_BIAS : V_UP_BIAS + 1, columns])
                u = u.astype(BF16)
                gu = (slope * dot_nt(g_d, w_down[columns, :])).astype(BF16)
                up_part[rows, :] = u
                gup_part[rows, :] = gu
                acc_small[A_UP_BIAS : A_UP_BIAS + 1, columns] += column_sum(gu.astype(F32))
                x2_all[rows, :] += dot_nn(u, w_down[columns, :])
                dn2_all[rows, :] += dot_nt(gu, w_up[:, columns])

            for h in range(4):
                mlp(h)
                if h % 2:
                    tick(f"part{n}.{h // 2}")

            base = starts[f"m{n}"]
            up = dot_tn(n2_all[...], gup_part[...])
            for c in range(PART // 128):
                buffer[base + c * D : base + (c + 1) * D, :] = up[:, c * 128 : (c + 1) * 128]
            put(buffer, base + 1536, 3, dot_tn(up_part[...], gd_all[...]))
            tick(f"part{n}")

        run(count_steps[2:3])

        def descend(b):
            length = length_of(groups, b)
            valid = (iota((ROWS, D), 0) < length).astype(F32)
            mixed[b] = (x2_all[rows_of(b), :] * valid)[:SLOT].astype(BF16)
            xhat2, rstd2 = normalise(x1_all[rows_of(b), :])
            dn2 = dn2_all[rows_of(b), :]
            acc_vec[A_TWO_GAIN : A_TWO_GAIN + 1, :] += column_sum(dn2 * xhat2)
            acc_vec[A_TWO_SHIFT : A_TWO_SHIFT + 1, :] += column_sum(dn2)
            g = load_padded(cotangent, b) * valid
            dx1 = g + normalise_back(dn2, vec(V_TWO_GAIN), xhat2, rstd2)
            dx_all[rows_of(b), :] = dx1
            g_o = dx1.astype(BF16)
            acc_vec[A_PROJ_BIAS : A_PROJ_BIAS + 1, :] += column_sum(g_o.astype(F32))
            d_o = dot_nt(g_o, w_proj[...]).astype(BF16)
            zeros = jnp.zeros((WIDE - ROWS, 128), BF16)
            for p in range(PAIRS):
                do_all[b, p] = jnp.concatenate([d_o[:, p * 128 : (p + 1) * 128], zeros], 0)

        for b in range(IMG):
            descend(b)
            tick(f"descend{b}")

        below = jnp.zeros((WIDE - ROWS, D), BF16)
        grad_proj = jnp.zeros((D, D), F32)
        for b in range(IMG):
            grad_proj += dot_nn(o_turned[b], jnp.concatenate([dx_all[rows_of(b), :].astype(BF16), below], 0))
        put(buffer, starts["proj"], 3, grad_proj)
        run(count_steps[3:])
        tick("proj")

    pl.run_scoped(
        first_half,
        pltpu.VMEM((ALL, D), F32),
        pltpu.VMEM((ALL, D), F32),
        pltpu.VMEM((ALL, D), BF16),
        pltpu.VMEM((ALL, D), BF16),
        pltpu.VMEM((ALL, PART), BF16),
        pltpu.VMEM((ALL, PART), BF16),
        pltpu.VMEM((ROWS, 128), F32),
    )
    coefficient = counts[2:3, 0:1]

    def second_half(acc_policy, h0_all, ga_all, z_all, g1_all, m1_all, g2_all, m2_all, gl_all, dqkv_all, mid_one,
                    mid_two, low_one):
        acc_policy[...] = jnp.zeros_like(acc_policy)
        row_id = iota((ROWS, 128), 0)
        lane_id = iota((ROWS, 128), 1)

        for p in range(PAIRS):
            def attend(b):
                policy = policy_lanes(keep, length_of(groups, b), b)
                k_pair = k_all[b, p]
                v_pair = v_all[b, p]
                kt = k_pair.T
                tiles = [slice(128 * t, 128 * (t + 1)) for t in range(3)]
                q_two = [split_heads(q_all[b, p, tile, :]) for tile in tiles]
                do_two = [split_heads(do_all[b, p, tile, :]) for tile in tiles]

                def score(t):
                    return dot_nt(k_pair, q_two[t]), dot_nt(v_pair, do_two[t])

                def soft(t, s, dp):
                    f = jnp.exp(s - lse_all[b, p, t, 0:1, :])
                    same = row_id == lane_id + 128 * t
                    w = jnp.where(same, 1.0, policy)
                    prob = f * jnp.concatenate([w, w], 1)
                    centred = dp - jnp.sum(prob * dp, 0, keepdims=True)
                    dw = f * centred
                    acc_policy[b] += jnp.where(same, 0.0, dw[:, :128] + dw[:, 128:])
                    return prob.astype(BF16), (prob * centred).astype(BF16)

                def query(t, ds):
                    dq = diagonal_blocks(dot_nn(kt, ds)).T * 0.125
                    count = min(128, ROWS - 128 * t)
                    first = b * ROWS + 128 * t
                    dqkv_all[pl.ds(first, count), p * D : p * D + 128] = dq[:count].astype(BF16)

                s0 = score(0)
                s1 = score(1)
                p0, d0 = soft(0, *s0)
                s2 = score(2)
                p1, d1 = soft(1, *s1)
                query(0, d0)
                p2, d2 = soft(2, *s2)
                query(1, d1)
                dv = dot_nn(jnp.concatenate([p0, p1, p2], 1), jnp.concatenate(do_two, 0))
                dk = dot_nn(jnp.concatenate([d0, d1, d2], 1), jnp.concatenate(q_two, 0))
                query(2, d2)
                dqkv_all[rows_of(b), p * D + 128 : p * D + 256] = dk.astype(BF16)
                dqkv_all[rows_of(b), p * D + 256 : p * D + 384] = dv.astype(BF16)

            for b in range(IMG):
                attend(b)
                tick(f"pair{p}.{b}")
            dqkv = dqkv_all[:, p * D : (p + 1) * D]
            base = starts[f"qkv{p}"]
            grad = dot_tn(n1_all[...], dqkv)
            for c in range(3):
                buffer[base + c * D : base + (c + 1) * D, :] = grad[:, c * 128 : (c + 1) * 128]
            bias = column_sum(dqkv.astype(F32))
            acc_vec[A_QUERY_BIAS : A_QUERY_BIAS + 1, p * 128 : (p + 1) * 128] = bias[:, 0:128]
            acc_vec[A_VALUE_BIAS : A_VALUE_BIAS + 1, p * 128 : (p + 1) * 128] = bias[:, 256:384]
            tick(f"qkv{p}")

        spatial_of, share_of = {}, {}

        def predict(b):
            length = length_of(groups, b)
            rows = rows_of(b)
            dpolicy = jnp.sum(acc_policy[b], 1, keepdims=True)
            xhat, _ = normalise(load_padded(tokens, b))
            h0 = (xhat * vec(V_PRED_GAIN) + vec(V_PRED_SHIFT)).astype(BF16)
            h0_all[rows, :] = h0
            position = iota((ROWS, 1), 0)
            spatial = jnp.where((position > 0) & (position < length), 1.0, 0.0)
            share = 1.0 / (length - 1).astype(F32)
            act, act_slope = gelu_pair(dot_nn(h0, w_in[...]) + vec(V_IN_BIAS))
            pooled = column_sum(act * spatial) * share
            local = iota((ROWS, D), 1) < D // 2
            z = jnp.where(local, act, pooled).astype(BF16)
            z_all[rows, :] = z
            m1, m1_slope = gelu_pair(dot_nn(z, w_mid[...]) + vec(V_MID_BIAS, 256))
            m1 = m1.astype(BF16)
            m1_all[rows, :] = m1
            m2, m2_slope = gelu_pair(dot_nn(m1, w_low[...]) + vec(V_LOW_BIAS, 128))
            m2 = m2.astype(BF16)
            m2_all[rows, :] = m2
            logits = dot_nt(m2, w_out[...]) + vec(V_OUT_BIAS, 128)
            keep_prob = 1.0 / (1.0 + jnp.exp(logits[:, 1:2] - logits[:, 0:1]))
            drop_prob = 1.0 / (1.0 + jnp.exp(logits[:, 0:1] - logits[:, 1:2]))
            dlog = spatial * (dpolicy + coefficient * spatial) * keep_prob * drop_prob
            lane = iota((ROWS, 128), 1)
            g_l = jnp.where(lane == 0, dlog, jnp.where(lane == 1, -dlog, 0.0)).astype(BF16)
            gl_all[rows, :] = g_l
            g_2 = (m2_slope * dot_nn(g_l, w_out[...])).astype(BF16)
            g2_all[rows, :] = g_2
            g_1 = (m1_slope * dot_nt(g_2, w_low[...])).astype(BF16)
            g1_all[rows, :] = g_1
            dz = dot_nt(g_1, w_mid[...])
            da = jnp.where(local, dz, spatial * share * column_sum(dz))
            g_a = (act_slope * da).astype(BF16)
            ga_all[rows, :] = g_a
            acc_vec[A_IN_BIAS : A_IN_BIAS + 1, :] += column_sum(g_a.astype(F32))
            acc_small[A_MID_BIAS : A_MID_BIAS + 1, 0:256] += column_sum(g_1.astype(F32))
            acc_small[A_LOW_BIAS : A_LOW_BIAS + 1, 0:128] += column_sum(g_2.astype(F32))
            acc_small[A_OUT_BIAS : A_OUT_BIAS + 1, 0:128] += column_sum(g_l.astype(F32))

        for b in range(IMG):
            predict(b)
            tick(f"predict{b}")


        base = starts["pred"]
        put(buffer, base, 3, dot_tn(h0_all[...], ga_all[...]))
        grad_mid = dot_tn(z_all[...], g1_all[...])
        mid_one[...] = grad_mid[:, 0:128]
        mid_two[...] = grad_mid[:, 128:256]
        lane = iota((192, 128), 1)
        odd = pltpu.roll(mid_one[pl.ds(1, 192, stride=2), :], 64, 1)
        buffer[pl.ds(base + ROW_MID, 192, stride=3), :] = mid_one[pl.ds(0, 192, stride=2), :]
        buffer[pl.ds(base + ROW_MID + 1, 192, stride=3), :] = jnp.where(
            lane < 64, mid_two[pl.ds(0, 192, stride=2), :], odd
        )
        buffer[pl.ds(base + ROW_MID + 2, 192, stride=3), :] = jnp.where(
            lane < 64, odd, pltpu.roll(mid_two[pl.ds(1, 192, stride=2), :], 64, 1)
        )
        low_one[...] = dot_tn(m1_all[...], g2_all[...])
        lane = iota((48, 128), 1)
        r0, r1, r2, r3 = (low_one[pl.ds(s, 48, stride=4), :] for s in range(4))
        r1, r2, r3 = pltpu.roll(r1, 96, 1), pltpu.roll(r2, 64, 1), pltpu.roll(r3, 32, 1)
        buffer[pl.ds(base + ROW_LOW, 48, stride=3), :] = jnp.where(lane < 96, r0, r1)
        buffer[pl.ds(base + ROW_LOW + 1, 48, stride=3), :] = jnp.where(lane < 64, r1, r2)
        buffer[pl.ds(base + ROW_LOW + 2, 48, stride=3), :] = jnp.where(lane < 32, r2, r3)
        m2_doubled = dot_nn(m2_all[...], doubling()).astype(BF16)
        both = dot_tn(gl_all[...], m2_doubled)
        head = jnp.where(iota((1, 256), 1) % 2 == 0, both[0:1, :], both[1:2, :])
        buffer[base + ROW_OUT : base + ROW_OUT + 1, :] = head[:, 0:128]
        buffer[base + ROW_OUT + 1 : base + ROW_OUT + 2, :] = pltpu.roll(head[:, 128:256], 64, 1)
        tick("pred")

        def finish(b):
            rows = rows_of(b)
            xhat, rstd = normalise(load_padded(tokens, b))
            dh0 = dot_nt(ga_all[rows, :], w_in[...])
            acc_vec[A_PRED_GAIN : A_PRED_GAIN + 1, :] += column_sum(dh0 * xhat)
            acc_vec[A_PRED_SHIFT : A_PRED_SHIFT + 1, :] += column_sum(dh0)
            dn1 = dot_nt(dqkv_all[rows, :], w_qkv[...])
            acc_vec[A_ONE_GAIN : A_ONE_GAIN + 1, :] += column_sum(dn1 * xhat)
            acc_vec[A_ONE_SHIFT : A_ONE_SHIFT + 1, :] += column_sum(dn1)
            total = (
                dx_all[rows, :]
                + normalise_back(dn1, vec(V_ONE_GAIN), xhat, rstd)
                + normalise_back(dh0, vec(V_PRED_GAIN), xhat, rstd)
            )
            input_gradient[b] = total[:SLOT].astype(BF16)

        for b in range(IMG):
            finish(b)
            tick(f"finish{b}")


    pl.run_scoped(
        second_half,
        pltpu.VMEM((IMG, ROWS, 128), F32),
        pltpu.VMEM((ALL, D), BF16),
        pltpu.VMEM((ALL, D), BF16),
        pltpu.VMEM((ALL, D), BF16),
        pltpu.VMEM((ALL, 256), BF16),
        pltpu.VMEM((ALL, 256), BF16),
        pltpu.VMEM((ALL, 128), BF16),
        pltpu.VMEM((ALL, 128), BF16),
        pltpu.VMEM((ALL, 128), BF16),
        pltpu.VMEM((ALL, 3 * D), BF16),
        pltpu.VMEM((D, 128), F32),
        pltpu.VMEM((D, 128), F32),
        pltpu.VMEM((256, 128), F32),
    )

    base = starts["vecs"]
    lane = iota((1, 128), 1)
    for r, a in enumerate((A_PRED_GAIN, A_PRED_SHIFT, A_IN_BIAS)):
        put_row(buffer, base + 3 * r, acc_vec[a : a + 1, :])
    mid_bias = acc_small[A_MID_BIAS : A_MID_BIAS + 1, 0:256]
    low_bias = pltpu.roll(acc_small[A_LOW_BIAS : A_LOW_BIAS + 1, 0:128], 64, 1)
    out_bias = pltpu.roll(acc_small[A_OUT_BIAS : A_OUT_BIAS + 1, 0:128], 32, 1)
    buffer[base + 9 : base + 10, :] = mid_bias[:, 0:128]
    buffer[base + 10 : base + 11, :] = jnp.where(lane < 64, mid_bias[:, 128:256], low_bias)
    buffer[base + 11 : base + 12, :] = jnp.where(lane < 32, low_bias, out_bias)
    for r, a in enumerate(
        (A_ONE_GAIN, A_ONE_SHIFT, A_QUERY_BIAS, A_VALUE_BIAS, A_PROJ_BIAS, A_TWO_GAIN, A_TWO_SHIFT)
    ):
        put_row(buffer, base + 12 + 3 * r, acc_vec[a : a + 1, :])
    put_row(buffer, base + 33, acc_small[A_UP_BIAS : A_UP_BIAS + 1, :])
    put_row(buffer, base + 45, acc_vec[A_DOWN_BIAS : A_DOWN_BIAS + 1, :])

    def settle(name, ordered):
        base = starts[name]
        if name.startswith("m"):
            n = int(name[1:])
            for c in range(4):
                ordered[pl.ds(ROW_UP + 4 * n + c, D, stride=12), :] = buffer[base + c * D : base + (c + 1) * D, :]
            ordered[ROW_DOWN + 1536 * n : ROW_DOWN + 1536 * (n + 1), :] = buffer[base + 1536 : base + 3072, :]
        elif name.startswith("qkv"):
            p = int(name[3:])
            for c in range(3):
                ordered[pl.ds(ROW_QKV + 3 * c + p, D, stride=9), :] = buffer[base + c * D : base + (c + 1) * D, :]
        else:
            first, rows = {"proj": (ROW_PROJ, 1152), "pred": (0, ROW_QKV), "vecs": (ROW_VEC, 48)}[name]
            ordered[first : first + rows, :] = buffer[base : base + rows, :]

    tick("vecs")
    owner = {}
    for name in plan:
        owner.setdefault(name if name in starts else name[:-1], []).append(name)
    settled = set()

    def hand_over(ordered):
        early = slice(ROW_PROJ // 8 * 8 + 8, ROW_VEC // 8 * 8)
        parts = (early, slice(0, early.start), slice(early.stop, GRAD_ROWS))
        copies = [pltpu.make_async_copy(ordered.at[part, :], grads.at[part, :], sem.at[i]) for i, part in enumerate(parts)]

        def look():
            for section, members in owner.items():
                if section not in settled and all(done[m] == len(plan[m]) for m in members):
                    settle(section, ordered)
                    settled.add(section)
                    if section in EARLY and all(e in settled for e in EARLY):
                        copies[0].start()

        look()
        for name in DRAIN:
            run(take(name))
            look()
        while any(done[n] < len(plan[n]) for n in plan):
            for name in plan:
                run(take(name))
            look()
        for copy in copies[1:]:
            copy.start()
        for copy in copies:
            copy.wait()

    pl.run_scoped(hand_over, pltpu.VMEM((GRAD_ROWS, 128), F32))


EARLY = ("m0", "m1", "m2", "proj")

TICKS = {
    "part0": ("m0a", "m0b", "m0c",),
    "part1.0": ("m0a", "m0b",),
    "part1.1": ("m0c",),
    "part1": ("m1",),
    "part2.1": ("m0a", "m1", "m0b",),
    "part2": ("m2",),
    "descend1": ("m0a",),
    "proj": ("proj", "m0c", "m2",),
    "pair0.1": ("proj", "m0a", "m0b",),
    "qkv0": ("qkv0",),
    "pair1.1": ("m0c", "m1", "qkv0",),
    "pair1.3": ("proj", "m0b", "m0c",),
    "qkv1": ("qkv1", "m2",),
    "pair2.0": ("m0a",),
    "pair2.1": ("m0b", "qkv1", "m0c", "qkv0",),
    "pair2.3": ("proj", "m0a",),
    "qkv2": ("qkv2a", "qkv2b", "m1",),
    "predict0": ("qkv2a", "qkv2b", "qkv1", "m2", "qkv0", "m0b", "m0c", "proj",),
    "predict2": ("m0a", "qkv1", "qkv2a", "qkv2b",),
    "predict3": ("m1", "m0a", "m2", "m0b", "qkv0",),
    "pred": ("preda", "predb", "qkv2a", "qkv2b", "m0b",),
    "finish1": ("qkv1", "preda", "proj", "m0c", "predb",),
    "finish3": ("m2", "m0c", "qkv2b",),
    "vecs": ("vecs", "qkv0",),
}
DRAIN = (
    "qkv1", "vecs", "proj", "qkv2a", "m1", "m2", "qkv2b", "qkv0", "m1", "proj", "qkv1", "qkv2a", "preda",
    "qkv2b", "qkv1", "predb", "vecs", "qkv2a", "proj", "m2", "qkv2b", "qkv0", "qkv2a", "preda", "qkv1",
    "predb", "vecs", "qkv0", "proj", "m2", "proj", "qkv2b", "qkv2a", "preda", "qkv1", "predb", "vecs", "qkv1",
    "qkv0", "qkv2b", "qkv0", "qkv2b", "preda", "m2", "preda", "predb", "qkv2a", "vecs", "m2", "predb",
    "qkv2a", "vecs",
)

(
    V_PRED_GAIN, V_PRED_SHIFT, V_IN_BIAS, V_MID_BIAS, V_LOW_BIAS, V_OUT_BIAS, V_ONE_GAIN, V_ONE_SHIFT, V_PROJ_BIAS,
    V_TWO_GAIN, V_TWO_SHIFT, V_UP_BIAS, V_DOWN_BIAS,
) = range(13)
(
    A_PRED_GAIN, A_PRED_SHIFT, A_IN_BIAS, A_ONE_GAIN, A_ONE_SHIFT, A_QUERY_BIAS, A_VALUE_BIAS, A_PROJ_BIAS, A_TWO_GAIN,
    A_TWO_SHIFT, A_DOWN_BIAS,
) = range(11)
A_UP_BIAS, A_MID_BIAS, A_LOW_BIAS, A_OUT_BIAS = range(4)


def doubling():
    return (iota((128, 256), 1) // 2 == iota((128, 256), 0)).astype(F32).astype(BF16)


CHUNK = 5952
CHUNKS = ((10944, 4800), (0, 5376), (5328, 5952))


def unpack(flat, flat_end, flat_one, rows, sems, others, w_qkv, w_proj, w_up, w_down, w_in, w_mid, w_low, w_out, vecs, qkv_bias):
    copies = [
        pltpu.make_async_copy(
            flat.at[pl.ds(start * 128, count * 128)], flat_one[i % 2].at[pl.ds(0, count * 128)], sems.at[i]
        )
        for i, (start, count) in enumerate(CHUNKS)
    ]

    def spread(i):
        copies[i].wait()

        def body(k, _):
            rows[pl.ds(pl.multiple_of(k * 192, 192), 192), :] = flat_one[i % 2][
                pl.ds(pl.multiple_of(k * 24576, 24576), 24576)
            ].reshape(192, 128)
            return 0

        lax.fori_loop(0, CHUNKS[i][1] // 192, body, 0)

    copies[0].start()
    copies[1].start()
    for copy in others:
        copy.start()
    spread(0)
    copies[2].start()
    start, count = CHUNKS[0]
    rows[count : count + 8, :] = flat_end[...].reshape(8, 128)
    for c in range(3):
        w_down[:, c * 128 : (c + 1) * 128] = shifted(rows, ROW_DOWN - 1 + c - start, MLP, 3).astype(BF16)
    lane = iota((16, 128), 1)
    at = 15697 - start
    vec_one = pltpu.roll(jnp.where(lane < 64, rows[at + 1 : at + 17, :], rows[at : at + 16, :]), 64, 1)
    lane = iota((36, 128), 1)
    at = 15708 - start
    vec_two = pltpu.roll(jnp.where(lane < 98, rows[at + 1 : at + 37, :], rows[at : at + 36, :]), 30, 1)
    rows[0:16, :] = vec_one
    rows[16:52, :] = vec_two
    for r, base in (
        (V_PRED_GAIN, 0), (V_PRED_SHIFT, 3), (V_IN_BIAS, 6), (V_ONE_GAIN, 16), (V_ONE_SHIFT, 19), (V_PROJ_BIAS, 28),
        (V_TWO_GAIN, 31), (V_TWO_SHIFT, 34), (V_DOWN_BIAS, 49),
    ):
        vecs[r : r + 1, 0:D] = row_of(rows, base, 3)
    vecs[V_UP_BIAS : V_UP_BIAS + 1, :] = row_of(rows, 37, 12)
    lane = iota((1, 128), 1)
    zero = jnp.zeros((1, 128), F32)
    r9, r10, r11 = (rows[r : r + 1, :] for r in (9, 10, 11))
    vecs[V_MID_BIAS : V_MID_BIAS + 1, 0:128] = r9
    vecs[V_MID_BIAS : V_MID_BIAS + 1, 128:256] = jnp.where(lane < 64, r10, zero)
    vecs[V_LOW_BIAS : V_LOW_BIAS + 1, 0:128] = jnp.where(
        lane < 96, pltpu.roll(jnp.where(lane < 64, r11, r10), 64, 1), zero
    )
    vecs[V_OUT_BIAS : V_OUT_BIAS + 1, 0:128] = jnp.where(lane < 2, pltpu.roll(r11, 96, 1), zero)
    for p in range(PAIRS):
        qkv_bias[0:1, p * D : p * D + 128] = rows[22 + p : 23 + p, :]
        qkv_bias[0:1, p * D + 128 : p * D + 256] = zero
        qkv_bias[0:1, p * D + 256 : p * D + 384] = rows[25 + p : 26 + p, :]

    spread(1)
    for c in range(3):
        w_in[:, c * 128 : (c + 1) * 128] = rows[pl.ds(c, D, stride=3), :].astype(BF16)
        for p in range(PAIRS):
            tile = shifted(rows, ROW_QKV - 1 + 3 * c + p, D, 9).astype(BF16)
            w_qkv[:, p * D + c * 128 : p * D + (c + 1) * 128] = tile

    a, b, c = (rows[pl.ds(ROW_MID + s, 192, stride=3), :] for s in range(3))
    lane = iota((192, 128), 1)
    zero = jnp.zeros((192, 128), F32)

    def interleave(tiles):
        count = len(tiles)
        size = tiles[0].shape[0]
        for s, tile in enumerate(tiles):
            rows[pl.ds(s, size, stride=count), :] = tile
        return rows[0 : size * count, :].astype(BF16)

    w_mid[:, 0:128] = interleave((a, pltpu.roll(jnp.where(lane < 64, c, b), 64, 1)))
    w_mid[:, 128:256] = interleave(
        (jnp.where(lane < 64, b, zero), jnp.where(lane < 64, pltpu.roll(c, 64, 1), zero))
    )
    lane = iota((48, 128), 1)
    a, b, c = (rows[pl.ds(ROW_LOW + s, 48, stride=3), :] for s in range(3))
    low = (
        a,
        jnp.where(lane < 32, pltpu.roll(a, 32, 1), pltpu.roll(b, 32, 1)),
        jnp.where(lane < 64, pltpu.roll(b, 64, 1), pltpu.roll(c, 64, 1)),
        pltpu.roll(c, 96, 1),
    )
    w_low[0:192, :] = interleave([jnp.where(lane < 96, tile, 0.0) for tile in low])
    w_low[192:256, :] = jnp.zeros((64, 128), BF16)
    head = jnp.concatenate([rows[ROW_OUT : ROW_OUT + 1, :], rows[ROW_OUT + 1 : ROW_OUT + 2, :]], 1)
    head = jnp.broadcast_to(head, (128, 256))
    lane = iota((128, 256), 1)
    chosen = (lane % 2 == iota((128, 256), 0)) & (lane < 192)
    w_out[...] = dot_nt(jnp.where(chosen, head, 0.0).astype(BF16), doubling()).astype(BF16)

    spread(2)
    start = CHUNKS[2][0]
    for c in range(3):
        w_proj[:, c * 128 : (c + 1) * 128] = shifted(rows, ROW_PROJ - 1 + c - start, D, 3).astype(BF16)
    for c in range(12):
        w_up[:, c * 128 : (c + 1) * 128] = shifted(rows, ROW_UP - 1 + c - start, D, 12).astype(BF16)


def counting(sizes, groups, keep, out, held, landed, sems):
    stages = [s for axis in ("gy", "gx", "gz") for s in whole(sizes, axis)]
    first = [0]
    for stage in stages:
        first.append(first[-1] + stage[2] - 1)

    def copies(s):
        return [
            pltpu.make_async_remote_copy(
                held.at[s], landed.at[first[s] + slot], sems.at[0, first[s] + slot], sems.at[1, first[s] + slot],
                device, MESH,
            )
            for device, slot, _ in partners(stages[s])
        ]

    def begin():
        kept = jnp.zeros((1, 1), F32)
        valid = jnp.zeros((1, 1), F32)
        position = iota((1, SLOT), 1)
        for b in range(IMG):
            spatial = jnp.where((position > 0) & (position < length_of(groups, b)), 1.0, 0.0)
            kept += jnp.sum(spatial * keep[b : b + 1, :].astype(F32), keepdims=True)
            valid += jnp.sum(spatial, keepdims=True)
        row = iota((8, 128), 0)
        held[0] = jnp.where(row == 0, kept, jnp.where(row == 1, valid, 0.0))

    def step(s):
        if s == 0:
            begin()
        else:
            total = held[s - 1]
            for slot, copy in enumerate(copies(s - 1)):
                copy.wait()
                total = total + landed[first[s - 1] + slot]
            held[s] = total
        if s < len(stages):
            for copy in copies(s):
                copy.start()
        else:
            total = held[s]
            row = iota((8, 128), 0)
            excess = total[0:1, :] / total[1:2, :] - KEEP_TARGET
            loss = RATIO_WEIGHT * total[1:2, :] * excess * excess
            out[...] = jnp.where(row == 2, 2.0 * RATIO_WEIGHT * excess, jnp.where(row == 3, loss, total))

    return [functools.partial(step, s) for s in range(len(stages) + 1)]


def layer(sizes, *operands):
    pieces, starts, rows = pieces_of(sizes)
    copies = max(sum(p.copies for p in pieces), 1)
    fits = rows <= 17408
    small = max(sum(sizes[a] - 1 for a in AXES), 1)
    vmem = pl.BlockSpec(memory_space=pltpu.VMEM)
    hbm = pl.BlockSpec(memory_space=pltpu.HBM)
    shape = jax.ShapeDtypeStruct
    return pl.pallas_call(
        functools.partial(layer_kernel, sizes, pieces, starts),
        grid=(1,),
        out_shape=(
            shape((IMG, SLOT, D), BF16),
            shape((IMG, SLOT, D), BF16),
            pltpu.VMEM((GRAD_ROWS, 128), F32) if fits else shape((GRAD_ROWS, 128), F32),
            shape((8, 128), F32),
        ),
        in_specs=[
            hbm, hbm, hbm, hbm, hbm,
            pl.BlockSpec((1024,), lambda i: (NPARAM // 1024,)),
        ],
        out_specs=[vmem, vmem, pl.BlockSpec(memory_space=pl.ANY), vmem],
        scratch_shapes=[
            pltpu.VMEM((D, 3 * D), BF16),
            pltpu.VMEM((D, D), BF16),
            pltpu.VMEM((D, MLP), BF16),
            pltpu.VMEM((MLP, D), BF16),
            pltpu.VMEM((D, D), BF16),
            pltpu.VMEM((D, 256), BF16),
            pltpu.VMEM((256, 128), BF16),
            pltpu.VMEM((128, 128), BF16),
            pltpu.VMEM((16, MLP), F32),
            pltpu.VMEM((8, 3 * D), F32),
            pltpu.VMEM((IMG, PAIRS, WIDE, 128), BF16),
            pltpu.VMEM((IMG, PAIRS, ROWS, 128), BF16),
            pltpu.VMEM((IMG, PAIRS, ROWS, 128), BF16),
            pltpu.VMEM((IMG, PAIRS, WIDE, 128), BF16),
            pltpu.VMEM((IMG, PAIRS, 3, 8, 256), F32),
            pltpu.VMEM((PAIRS, 128, ROWS), BF16),
            pltpu.VMEM((IMG, D, WIDE), BF16),
            pltpu.VMEM((ALL, D), BF16),
            pltpu.VMEM((ALL, D), F32),
            pltpu.VMEM((16, D), F32),
            pltpu.VMEM((8, MLP), F32),
            pltpu.VMEM((rows, 128), F32),
            pltpu.VMEM((rows, 128), F32),
            pltpu.SemaphoreType.DMA((4, copies)),
            pltpu.SemaphoreType.REGULAR((max(sum(len(p.stages) for p in pieces), 1),)),
            pltpu.VMEM((4, 8, 128), F32),
            pltpu.VMEM((small, 8, 128), F32),
            pltpu.SemaphoreType.DMA((2, small)),
            pltpu.SemaphoreType.DMA((3,)),
            pltpu.SMEM((IMG,), jnp.int32),
            pltpu.VMEM((IMG, SLOT, D), BF16),
            pltpu.VMEM((IMG, SLOT, D), BF16),
            pltpu.VMEM((IMG, SLOT), jnp.int32),
            pltpu.SemaphoreType.DMA((4,)),
        ],
        compiler_params=pltpu.CompilerParams(
            collective_id=0, has_side_effects=True, vmem_limit_bytes=(95 if fits else 116) << 19
        ),
        name="layer",
    )(*operands)


UPDATE_ROWS = 2304


def update_kernel(
    grads, after, counts, mixed_in, gradient_in, params, momentum, average,
    new_params, new_momentum, new_average, mixed, input_gradient, loss, block, joined,
):
    i = pl.program_id(0)
    n = UPDATE_ROWS
    mixed[...] = mixed_in[...]
    input_gradient[...] = gradient_in[...]
    loss[0, 0] = counts[3, 0]
    joined[0:n, :] = grads[...]
    joined[n : n + 8, :] = after[...]
    here = joined[0:n, :]
    row = iota((n, 128), 0) + i * n
    lane = iota((n, 128), 1)
    moved = pltpu.roll(jnp.where(lane < 64, joined[1 : n + 1, :], here), 64, 1)
    flat = jnp.where(row < ROW_QKV - 1, here, moved)
    joined[0:n, :] = flat

    @pl.when(i == pl.num_programs(0) - 1)
    def _():
        first = 15708 - (NPARAM // (n * 128)) * n
        lane = iota((40, 128), 1)
        one = grads[first + 1 : first + 41, :]
        two = grads[first + 2 : first + 42, :]
        tail = pltpu.roll(jnp.where(lane < 30, two, one), 98, 1)
        keep_old = (iota((40, 128), 0) == 0) & (lane < 98)
        joined[first : first + 40, :] = jnp.where(keep_old, joined[first : first + 40, :], tail)
        block[...] = grads[first + 2 : first + 38, :].reshape(4608)

    g = joined[0:n, :].reshape(n * 128)
    moment = MOMENTUM_DECAY * momentum[...] + g
    value = params[...] - LEARN_RATE * (g + MOMENTUM_DECAY * moment)
    new_momentum[...] = moment
    new_params[...] = value
    new_average[...] = AVERAGE_DECAY * average[...] + (1.0 - AVERAGE_DECAY) * value


def update(grads, counts, mixed, input_gradient, params, momentum, average):
    n = UPDATE_ROWS
    flat = pl.BlockSpec((n * 128,), lambda i: (i,))
    image = pl.BlockSpec((1, SLOT, D), lambda i: (jnp.minimum(i, IMG - 1), 0, 0))
    out = jax.ShapeDtypeStruct((NPARAM,), F32)
    return pl.pallas_call(
        update_kernel,
        grid=(pl.cdiv(NPARAM, n * 128),),
        out_shape=(
            out, out, out,
            jax.ShapeDtypeStruct(mixed.shape, BF16),
            jax.ShapeDtypeStruct(mixed.shape, BF16),
            jax.ShapeDtypeStruct((1, 1), F32),
            jax.ShapeDtypeStruct((4608,), F32),
        ),
        in_specs=[
            pl.BlockSpec((n, 128), lambda i: (i, 0)),
            pl.BlockSpec((8, 128), lambda i: ((i + 1) * (n // 8), 0)),
            pl.BlockSpec((8, 128), lambda i: (0, 0)),
            image,
            image,
            flat,
            flat,
            flat,
        ],
        out_specs=[
            flat, flat, flat, image, image,
            pl.BlockSpec(memory_space=pltpu.SMEM),
            pl.BlockSpec((4608,), lambda i: (0,)),
        ],
        scratch_shapes=[pltpu.VMEM((n + 8, 128), F32)],
        compiler_params=pltpu.CompilerParams(vmem_limit_bytes=28 << 20),
        name="update",
    )(
        grads, grads,
        *(pltpu.with_memory_space_constraint(x, pltpu.HBM) for x in (counts, mixed, input_gradient)),
        params,
        *(pltpu.with_memory_space_constraint(x, pltpu.HBM) for x in (momentum, average)),
    )


GRAD_ROWS = -(-(NPARAM // 128 + 40) // UPDATE_ROWS) * UPDATE_ROWS + 8


def solution(mesh):
    sizes = dict(mesh.shape)

    def per_device(tokens, cotangent, groups, keep_mask, params, momentum, average):
        mixed, input_gradient, grads, counts = layer(sizes, groups, tokens, cotangent, keep_mask, params, params)
        new_params, new_momentum, new_average, mixed, input_gradient, loss, block = update(
            grads, counts, mixed, input_gradient, params, momentum, average
        )
        return (mixed, input_gradient, loss.reshape(()), new_params, new_momentum, new_average, block)

    split = P(("gx", "gy", "gz"))
    return jax.shard_map(
        per_device,
        mesh=mesh,
        in_specs=(split, split, split, split, P(), P(), P()),
        out_specs=(split, split, P(), P(), P(), P(), P()),
        check_vma=False,
    )
```

```python
import functools
import math

import jax
import jax.numpy as jnp
from jax import lax
from jax.experimental import pallas as pl
from jax.experimental.pallas import tpu as pltpu
from jax.sharding import PartitionSpec as P

MESH = pl.DeviceIdType.MESH
F32 = jnp.float32
BF16 = jnp.bfloat16

D = 384
HEADS = 6
PAIRS = 3
MLP = 1536
LEN_A, LEN_B, LEN_C = 101, 197, 325
IMG = 4
SLOT = 328
ROWS = 336
WIDE = 384
ALL = IMG * ROWS
NPARAM = 2015330
NORM_EPS = 1e-06
RATIO_WEIGHT = 2.0
KEEP_TARGET = 0.7
MOMENTUM_DECAY = 0.5
AVERAGE_DECAY = 0.5
LEARN_RATE = 0.0001

ROW_MID = 1152
ROW_LOW = 1728
ROW_OUT = 1872
ROW_QKV = 1874
ROW_PROJ = 5330
ROW_UP = 6482
ROW_DOWN = 11090
ROW_VEC = 15698
ROW_BLOCK = 15710
EARLY_BASE = 5328
EARLY_ROWS = 10376
FLAT_ROWS = 15752


def dot_nn(a, b):
    return lax.dot_general(a, b, (((1,), (0,)), ((), ())), preferred_element_type=F32)


def dot_nt(a, b):
    return lax.dot_general(a, b, (((1,), (1,)), ((), ())), preferred_element_type=F32)


def dot_tn(a, b):
    return lax.dot_general(a, b, (((0,), (0,)), ((), ())), preferred_element_type=F32)


def iota(shape, axis):
    return lax.broadcasted_iota(jnp.int32, shape, axis)


def gelu_pair(v):
    cdf = 0.5 * lax.erf(v * 0.7071067811865476) + 0.5
    return v * cdf, cdf + v * jnp.exp(v * v * -0.5) * 0.3989422804014327


def normalise(x):
    mean = jnp.sum(x, -1, keepdims=True) * (1.0 / D)
    centered = x - mean
    spread = jnp.sum(centered * centered, -1, keepdims=True) * (1.0 / D)
    rstd = lax.rsqrt(spread + NORM_EPS)
    return centered * rstd, rstd


def normalise_back(grad, gain, xhat, rstd):
    scaled = grad * gain
    first = jnp.sum(scaled, -1, keepdims=True) * (1.0 / D)
    second = jnp.sum(scaled * xhat, -1, keepdims=True) * (1.0 / D)
    return rstd * (scaled - first - xhat * second)


def column_sum(x):
    return jnp.sum(x, 0, keepdims=True)


def load_padded(ref, b):
    x = ref[b].astype(F32)
    return jnp.concatenate([x, jnp.zeros((ROWS - SLOT, D), F32)], 0)


def length_of(groups, b):
    g = groups[b]
    return jnp.where(g == 0, LEN_A, jnp.where(g == 1, LEN_B, LEN_C))


def policy_lanes(keep, length, b):
    row = keep[pl.ds(b, 1), :].astype(F32)
    row = jnp.concatenate([row, jnp.zeros((1, WIDE - SLOT), F32)], 1)
    kept = jnp.broadcast_to(row, (128, WIDE)).T[:ROWS]
    position = iota((ROWS, 128), 0)
    return jnp.where(position == 0, 1.0, jnp.where(position < length, kept, 0.0))


def split_heads(tile):
    left = iota(tile.shape, 1) < 64
    zero = jnp.zeros_like(tile)
    return jnp.concatenate([jnp.where(left, tile, zero), jnp.where(left, zero, tile)], 0)


def diagonal_blocks(x):
    return jnp.concatenate([x[:64, :128], x[64:, 128:]], 0)


def put(ref, base, stride, value):
    rows, columns = value.shape
    for c in range(columns // 128):
        ref[pl.ds(base + c, rows, stride=stride), :] = value[:, c * 128 : (c + 1) * 128]


def put_row(ref, base, value):
    for c in range(value.shape[1] // 128):
        ref[base + c : base + c + 1, :] = value[:, c * 128 : (c + 1) * 128]


def row_of(ref, base, count):
    return jnp.concatenate([ref[base + c : base + c + 1, :] for c in range(count)], 1)


def shifted(ref, base, rows, stride):
    first = ref[pl.ds(base, rows, stride=stride), :]
    second = ref[pl.ds(base + 1, rows, stride=stride), :]
    low = iota((rows, 128), 1) < 64
    return pltpu.roll(jnp.where(low, second, first), 64, 1)


AXES = ("gx", "gy", "gz")


def digits(sizes, axis):
    size, stride, found = sizes[axis], 1, []
    while size > 1:
        base = 2 if size % 2 == 0 else size
        found.append((axis, stride, base))
        size //= base
        stride *= base
    return found


def whole(sizes, axis):
    return [(axis, 1, sizes[axis])] if sizes[axis] > 1 else []


def digit_of(stage):
    axis, stride, base = stage
    return lax.rem(lax.axis_index(axis) // stride, base)


def partners(stage):
    axis, stride, base = stage
    mine = digit_of(stage)
    found = []
    for k in range(1, base):
        other = lax.rem(mine + k, base)
        index = lax.axis_index(axis) + (other - mine) * stride
        found.append((tuple(index if a == axis else lax.axis_index(a) for a in AXES), k - 1, other))
    return found


def greet(sizes):
    barrier = pltpu.get_barrier_semaphore()
    total = 0
    for axis in AXES:
        for stage in whole(sizes, axis):
            for device, _, _ in partners(stage):
                pl.semaphore_signal(barrier, inc=1, device_id=device, device_id_type=MESH)
                total += 1
    return barrier, total


class Piece:
    def __init__(self, name, rows, base, stages):
        self.name, self.rows, self.base, self.stages = name, rows, base, stages
        self.copies = sum(s[2] - 1 for s in stages)

    def steps(self, buffer, landing, sems, free, first, first_stage):
        stages = self.stages
        rows_after = [self.rows]
        for stage in stages:
            rows_after.append(rows_after[-1] // stage[2])
        landing_at, sem_at = [self.base], [first]
        for s, stage in enumerate(stages):
            landing_at.append(landing_at[-1] + (stage[2] - 1) * rows_after[s + 1])
            sem_at.append(sem_at[-1] + stage[2] - 1)

        def place(s):
            begin = self.base
            for i in range(s):
                begin = begin + digit_of(stages[i]) * rows_after[i + 1]
            return begin

        def block(s, digit):
            return pl.ds(pl.multiple_of(place(s) + digit * rows_after[s + 1], 8), rows_after[s + 1])

        def scatter(s):
            found = []
            for device, slot, other in partners(stages[s]):
                found.append(
                    pltpu.make_async_remote_copy(
                        buffer.at[block(s, other), :],
                        landing.at[pl.ds(landing_at[s] + slot * rows_after[s + 1], rows_after[s + 1]), :],
                        sems.at[0, sem_at[s] + slot],
                        sems.at[1, sem_at[s] + slot],
                        device,
                        MESH,
                    )
                )
            return found

        def gather(s):
            found = []
            for device, slot, _ in partners(stages[s]):
                own = buffer.at[block(s, digit_of(stages[s])), :]
                found.append(
                    pltpu.make_async_remote_copy(
                        own, own, sems.at[2, sem_at[s] + slot], sems.at[3, sem_at[s] + slot], device, MESH
                    )
                )
            return found

        def start(copies):
            for copy in copies:
                copy.start()

        def end_scatter(s):
            for copy in scatter(s):
                copy.wait()
            for device, _, _ in partners(stages[s]):
                pl.semaphore_signal(free.at[first_stage + s], inc=1, device_id=device, device_id_type=MESH)
            rows = rows_after[s + 1]
            begin = place(s) + digit_of(stages[s]) * rows
            step = math.gcd(rows, 64)

            def body(i, _):
                own = pl.ds(pl.multiple_of(begin + i * step, 8), step)
                total = buffer[own, :]
                for slot in range(stages[s][2] - 1):
                    at = landing_at[s] + slot * rows
                    total = total + landing[pl.ds(pl.multiple_of(at + i * step, 8), step), :]
                buffer[own, :] = total
                return 0

            lax.fori_loop(0, rows // step, body, 0)

        def end_gather(s):
            for copy in gather(s):
                copy.wait()

        count = len(stages)
        found = []
        for s in range(count):

            def there(s=s):
                if s:
                    end_scatter(s - 1)
                start(scatter(s))

            found.append(there)
        for s in reversed(range(count)):

            def back(s=s):
                if s == count - 1:
                    end_scatter(s)
                else:
                    end_gather(s + 1)
                pl.semaphore_wait(free.at[first_stage + s], stages[s][2] - 1)
                start(gather(s))

            found.append(back)
        if count:
            found.append(lambda: end_gather(0))
        return found


SECTIONS = (
    ("m0", 3072, ((1024, "CGAB"), (1024, "CXHY"), (1024, "CHXY"),)),
    ("m1", 3072, ((3072, "CGH"),)),
    ("m2", 3072, ((3072, "CAXYB"),)),
    ("proj", 1152, ((1280, "CYXAB"),)),
    ("qkv0", 1152, ((1280, "CXAYB"),)),
    ("qkv1", 1152, ((1280, "CYXAB"),)),
    ("qkv2", 1152, ((512, "CAXYB"), (768, "CYXAB"),)),
    ("pred", 1874, ((1280, "CGH"), (768, "CHG"),)),
    ("vecs", 48, ((256, "CGH"),)),
)


def pieces_of(sizes):
    unit = 8 * math.prod(sizes.values())
    core, x, z = digits(sizes, "gy"), digits(sizes, "gx"), digits(sizes, "gz")
    ways = {
        "C": core, "X": x[:1], "Y": x[1:], "A": z[:1], "B": z[1:], "G": whole(sizes, "gx"), "H": whole(sizes, "gz"),
    }
    found, starts, base = [], {}, 0
    for name, rows, parts in SECTIONS:
        starts[name] = base
        if unit > 256 or len(parts) == 1:
            parts = ((rows, parts[0][1]),)
        for i, (part_rows, way) in enumerate(parts):
            stages = [stage for letter in way for stage in ways[letter]]
            part_rows = -(-part_rows // unit) * unit
            found.append(Piece(name + "abcd"[i] if len(parts) > 1 else name, part_rows, base, stages))
            base += part_rows
    return found, starts, base


PART = 512
PARTS = MLP // PART
HALF = ALL // 4


def layer_kernel(
    sizes, pieces, starts,
    groups_in, tokens_in, cotangent_in, keep_in, flat, flat_end,
    mixed, input_gradient, grads, counts,
    w_qkv, w_proj, w_up, w_down, w_in, w_mid, w_low, w_out, vecs, qkv_bias,
    q_all, k_all, v_all, do_all, lse_all, v_turned, o_turned, n1_all, dx_all, acc_vec, acc_small,
    buffer, landing, sems, free, held, landed, count_sems, sem, groups, tokens, cotangent, keep, in_sems,
):
    plan, first, first_stage = {}, 0, 0
    for p in pieces:
        plan[p.name] = p.steps(buffer, landing, sems, free, first, first_stage)
        first += p.copies
        first_stage += len(p.stages)
    done = {p.name: 0 for p in pieces}

    def take(*names):
        found = []
        for name in names:
            if name in plan and done[name] < len(plan[name]):
                found.append(plan[name][done[name]])
                done[name] += 1
        return found

    def run(steps):
        for step in steps:
            step()

    def tick(name):
        run(take(*TICKS.get(name, ())))

    arriving = [
        pltpu.make_async_copy(source, target, in_sems.at[i])
        for i, (source, target) in enumerate(
            ((groups_in, groups), (keep_in, keep), (tokens_in, tokens), (cotangent_in, cotangent))
        )
    ]
    for copy in arriving[:2]:
        copy.start()
    barrier, greetings = greet(sizes)
    count_steps = counting(sizes, groups, keep, counts, held, landed, count_sems)

    def weights(one, two, rows):
        unpack(flat, flat_end, (one, two), rows, sem, arriving[2:], w_qkv, w_proj, w_up, w_down, w_in, w_mid, w_low, w_out, vecs,
               qkv_bias)

    pl.run_scoped(
        weights,
        pltpu.VMEM((CHUNK * 128,), F32),
        pltpu.VMEM((CHUNK * 128,), F32),
        pltpu.VMEM((CHUNK + 8, 128), F32),
    )
    for copy in arriving:
        copy.wait()
    if greetings:
        pl.semaphore_wait(barrier, greetings)
    run(count_steps[:1])

    def vec(r, size=D):
        return vecs[r : r + 1, 0:size]

    acc_vec[...] = jnp.zeros_like(acc_vec)
    acc_small[...] = jnp.zeros_like(acc_small)

    def rows_of(b):
        if isinstance(b, int):
            return slice(b * ROWS, (b + 1) * ROWS)
        return pl.ds(pl.multiple_of(b * ROWS, 16), ROWS)

    x1_all = dx_all

    def first_half(x2_all, dn2_all, n2_all, gd_all, up_part, gup_part, weight):
        def attend(b, _):
            length = length_of(groups, b)
            x = load_padded(tokens, b)
            xhat, _ = normalise(x)
            n1 = (xhat * vec(V_ONE_GAIN) + vec(V_ONE_SHIFT)).astype(BF16)
            n1_all[rows_of(b), :] = n1
            zeros = jnp.zeros((WIDE - ROWS, 128), BF16)
            for p in range(PAIRS):
                part = dot_nn(n1, w_qkv[:, p * D : (p + 1) * D]) + qkv_bias[0:1, p * D : (p + 1) * D]
                q_all[b, p] = jnp.concatenate([part[:, 0:128].astype(BF16) * jnp.array(0.125, BF16), zeros], 0)
                k_all[b, p] = part[:, 128:256].astype(BF16)
                v_all[b, p] = part[:, 256:384].astype(BF16)
                v_turned[p] = part[:, 256:384].T.astype(BF16)

            weight[...] = policy_lanes(keep, length, b)
            row_id = iota((ROWS, 128), 0)
            lane_id = iota((ROWS, 128), 1)

            def pair(p):
                k_pair = k_all[b, p]
                vt = v_turned[p]
                tiles = [slice(128 * t, 128 * (t + 1)) for t in range(3)]
                where = slice(p * 128, (p + 1) * 128)

                def soft(t, s):
                    top = jnp.max(s, 0, keepdims=True)
                    w = jnp.where(row_id == lane_id + 128 * t, 1.0, weight[...])
                    e = jnp.exp(s - top) * jnp.concatenate([w, w], 1)
                    total = jnp.sum(e, 0, keepdims=True)
                    lse_all[b, p, t, 0:1, :] = top + jnp.log(total)
                    return e.astype(BF16), 1.0 / total

                def score(t):
                    return dot_nt(k_pair, split_heads(q_all[b, p, tiles[t], :]))

                def mix(t, e, inverse):
                    o = diagonal_blocks(dot_nn(vt, e) * inverse).astype(BF16)
                    o_turned[b, where, tiles[t]] = o

                s0 = score(0)
                s1 = score(1)
                e0 = soft(0, s0)
                s2 = score(2)
                e1 = soft(1, s1)
                mix(0, *e0)
                e2 = soft(2, s2)
                mix(1, *e1)
                mix(2, *e2)

            for p in range(PAIRS):
                pair(p)
            x1 = x + dot_tn(o_turned[b], w_proj[...])[:ROWS] + vec(V_PROJ_BIAS)
            x1_all[rows_of(b), :] = x1
            x2_all[rows_of(b), :] = x1 + vec(V_DOWN_BIAS)
            dn2_all[rows_of(b), :] = jnp.zeros((ROWS, D), F32)
            xhat2, _ = normalise(x1)
            n2_all[rows_of(b), :] = (xhat2 * vec(V_TWO_GAIN) + vec(V_TWO_SHIFT)).astype(BF16)
            valid = (iota((ROWS, D), 0) < length).astype(F32)
            g = load_padded(cotangent, b) * valid
            gd_all[rows_of(b), :] = g.astype(BF16)
            acc_vec[A_DOWN_BIAS : A_DOWN_BIAS + 1, :] += column_sum(g)
            return 0

        lax.fori_loop(0, IMG, attend, 0)
        run(count_steps[1:2])

        for n in range(PARTS):
            columns = slice(n * PART, (n + 1) * PART)

            def mlp(h):
                rows = slice(h * HALF, (h + 1) * HALF)
                n2 = n2_all[rows, :]
                g_d = gd_all[rows, :]
                u, slope = gelu_pair(dot_nn(n2, w_up[:, columns]) + vecs[V_UP_BIAS : V_UP_BIAS + 1, columns])
                u = u.astype(BF16)
                gu = (slope * dot_nt(g_d, w_down[columns, :])).astype(BF16)
                up_part[rows, :] = u
                gup_part[rows, :] = gu
                acc_small[A_UP_BIAS : A_UP_BIAS + 1, columns] += column_sum(gu.astype(F32))
                x2_all[rows, :] += dot_nn(u, w_down[columns, :])
                dn2_all[rows, :] += dot_nt(gu, w_up[:, columns])

            for h in range(4):
                mlp(h)
                if h % 2:
                    tick(f"part{n}.{h // 2}")

            base = starts[f"m{n}"]
            up = dot_tn(n2_all[...], gup_part[...])
            for c in range(PART // 128):
                buffer[base + c * D : base + (c + 1) * D, :] = up[:, c * 128 : (c + 1) * 128]
            put(buffer, base + 1536, 3, dot_tn(up_part[...], gd_all[...]))
            tick(f"part{n}")

        run(count_steps[2:3])

        def descend(b):
            length = length_of(groups, b)
            valid = (iota((ROWS, D), 0) < length).astype(F32)
            mixed[b] = (x2_all[rows_of(b), :] * valid)[:SLOT].astype(BF16)
            xhat2, rstd2 = normalise(x1_all[rows_of(b), :])
            dn2 = dn2_all[rows_of(b), :]
            acc_vec[A_TWO_GAIN : A_TWO_GAIN + 1, :] += column_sum(dn2 * xhat2)
            acc_vec[A_TWO_SHIFT : A_TWO_SHIFT + 1, :] += column_sum(dn2)
            g = load_padded(cotangent, b) * valid
            dx1 = g + normalise_back(dn2, vec(V_TWO_GAIN), xhat2, rstd2)
            dx_all[rows_of(b), :] = dx1
            g_o = dx1.astype(BF16)
            acc_vec[A_PROJ_BIAS : A_PROJ_BIAS + 1, :] += column_sum(g_o.astype(F32))
            d_o = dot_nt(g_o, w_proj[...]).astype(BF16)
            zeros = jnp.zeros((WIDE - ROWS, 128), BF16)
            for p in range(PAIRS):
                do_all[b, p] = jnp.concatenate([d_o[:, p * 128 : (p + 1) * 128], zeros], 0)

        for b in range(IMG):
            descend(b)
            tick(f"descend{b}")

        below = jnp.zeros((WIDE - ROWS, D), BF16)
        grad_proj = jnp.zeros((D, D), F32)
        for b in range(IMG):
            grad_proj += dot_nn(o_turned[b], jnp.concatenate([dx_all[rows_of(b), :].astype(BF16), below], 0))
        put(buffer, starts["proj"], 3, grad_proj)
        run(count_steps[3:])
        tick("proj")

    pl.run_scoped(
        first_half,
        pltpu.VMEM((ALL, D), F32),
        pltpu.VMEM((ALL, D), F32),
        pltpu.VMEM((ALL, D), BF16),
        pltpu.VMEM((ALL, D), BF16),
        pltpu.VMEM((ALL, PART), BF16),
        pltpu.VMEM((ALL, PART), BF16),
        pltpu.VMEM((ROWS, 128), F32),
    )
    coefficient = counts[2:3, 0:1]

    def second_half(acc_policy, h0_all, ga_all, z_all, g1_all, m1_all, g2_all, m2_all, gl_all, dqkv_all, mid_one,
                    mid_two, low_one):
        acc_policy[...] = jnp.zeros_like(acc_policy)
        row_id = iota((ROWS, 128), 0)
        lane_id = iota((ROWS, 128), 1)

        for p in range(PAIRS):
            def attend(b):
                policy = policy_lanes(keep, length_of(groups, b), b)
                k_pair = k_all[b, p]
                v_pair = v_all[b, p]
                kt = k_pair.T
                tiles = [slice(128 * t, 128 * (t + 1)) for t in range(3)]
                q_two = [split_heads(q_all[b, p, tile, :]) for tile in tiles]
                do_two = [split_heads(do_all[b, p, tile, :]) for tile in tiles]

                def score(t):
                    return dot_nt(k_pair, q_two[t]), dot_nt(v_pair, do_two[t])

                def soft(t, s, dp):
                    f = jnp.exp(s - lse_all[b, p, t, 0:1, :])
                    same = row_id == lane_id + 128 * t
                    w = jnp.where(same, 1.0, policy)
                    prob = f * jnp.concatenate([w, w], 1)
                    centred = dp - jnp.sum(prob * dp, 0, keepdims=True)
                    dw = f * centred
                    acc_policy[b] += jnp.where(same, 0.0, dw[:, :128] + dw[:, 128:])
                    return prob.astype(BF16), (prob * centred).astype(BF16)

                def query(t, ds):
                    dq = diagonal_blocks(dot_nn(kt, ds)).T * 0.125
                    count = min(128, ROWS - 128 * t)
                    first = b * ROWS + 128 * t
                    dqkv_all[pl.ds(first, count), p * D : p * D + 128] = dq[:count].astype(BF16)

                s0 = score(0)
                s1 = score(1)
                p0, d0 = soft(0, *s0)
                s2 = score(2)
                p1, d1 = soft(1, *s1)
                query(0, d0)
                p2, d2 = soft(2, *s2)
                query(1, d1)
                dv = dot_nn(jnp.concatenate([p0, p1, p2], 1), jnp.concatenate(do_two, 0))
                dk = dot_nn(jnp.concatenate([d0, d1, d2], 1), jnp.concatenate(q_two, 0))
                query(2, d2)
                dqkv_all[rows_of(b), p * D + 128 : p * D + 256] = dk.astype(BF16)
                dqkv_all[rows_of(b), p * D + 256 : p * D + 384] = dv.astype(BF16)

            for b in range(IMG):
                attend(b)
                tick(f"pair{p}.{b}")
            dqkv = dqkv_all[:, p * D : (p + 1) * D]
            base = starts[f"qkv{p}"]
            grad = dot_tn(n1_all[...], dqkv)
            for c in range(3):
                buffer[base + c * D : base + (c + 1) * D, :] = grad[:, c * 128 : (c + 1) * 128]
            bias = column_sum(dqkv.astype(F32))
            acc_vec[A_QUERY_BIAS : A_QUERY_BIAS + 1, p * 128 : (p + 1) * 128] = bias[:, 0:128]
            acc_vec[A_VALUE_BIAS : A_VALUE_BIAS + 1, p * 128 : (p + 1) * 128] = bias[:, 256:384]
            tick(f"qkv{p}")

        spatial_of, share_of = {}, {}

        def predict(b):
            length = length_of(groups, b)
            rows = rows_of(b)
            dpolicy = jnp.sum(acc_policy[b], 1, keepdims=True)
            xhat, _ = normalise(load_padded(tokens, b))
            h0 = (xhat * vec(V_PRED_GAIN) + vec(V_PRED_SHIFT)).astype(BF16)
            h0_all[rows, :] = h0
            position = iota((ROWS, 1), 0)
            spatial = jnp.where((position > 0) & (position < length), 1.0, 0.0)
            share = 1.0 / (length - 1).astype(F32)
            act, act_slope = gelu_pair(dot_nn(h0, w_in[...]) + vec(V_IN_BIAS))
            pooled = column_sum(act * spatial) * share
            local = iota((ROWS, D), 1) < D // 2
            z = jnp.where(local, act, pooled).astype(BF16)
            z_all[rows, :] = z
            m1, m1_slope = gelu_pair(dot_nn(z, w_mid[...]) + vec(V_MID_BIAS, 256))
            m1 = m1.astype(BF16)
            m1_all[rows, :] = m1
            m2, m2_slope = gelu_pair(dot_nn(m1, w_low[...]) + vec(V_LOW_BIAS, 128))
            m2 = m2.astype(BF16)
            m2_all[rows, :] = m2
            logits = dot_nt(m2, w_out[...]) + vec(V_OUT_BIAS, 128)
            keep_prob = 1.0 / (1.0 + jnp.exp(logits[:, 1:2] - logits[:, 0:1]))
            drop_prob = 1.0 / (1.0 + jnp.exp(logits[:, 0:1] - logits[:, 1:2]))
            dlog = spatial * (dpolicy + coefficient * spatial) * keep_prob * drop_prob
            lane = iota((ROWS, 128), 1)
            g_l = jnp.where(lane == 0, dlog, jnp.where(lane == 1, -dlog, 0.0)).astype(BF16)
            gl_all[rows, :] = g_l
            g_2 = (m2_slope * dot_nn(g_l, w_out[...])).astype(BF16)
            g2_all[rows, :] = g_2
            g_1 = (m1_slope * dot_nt(g_2, w_low[...])).astype(BF16)
            g1_all[rows, :] = g_1
            dz = dot_nt(g_1, w_mid[...])
            da = jnp.where(local, dz, spatial * share * column_sum(dz))
            g_a = (act_slope * da).astype(BF16)
            ga_all[rows, :] = g_a
            acc_vec[A_IN_BIAS : A_IN_BIAS + 1, :] += column_sum(g_a.astype(F32))
            acc_small[A_MID_BIAS : A_MID_BIAS + 1, 0:256] += column_sum(g_1.astype(F32))
            acc_small[A_LOW_BIAS : A_LOW_BIAS + 1, 0:128] += column_sum(g_2.astype(F32))
            acc_small[A_OUT_BIAS : A_OUT_BIAS + 1, 0:128] += column_sum(g_l.astype(F32))

        for b in range(IMG):
            predict(b)
            tick(f"predict{b}")


        base = starts["pred"]
        put(buffer, base, 3, dot_tn(h0_all[...], ga_all[...]))
        grad_mid = dot_tn(z_all[...], g1_all[...])
        mid_one[...] = grad_mid[:, 0:128]
        mid_two[...] = grad_mid[:, 128:256]
        lane = iota((192, 128), 1)
        odd = pltpu.roll(mid_one[pl.ds(1, 192, stride=2), :], 64, 1)
        buffer[pl.ds(base + ROW_MID, 192, stride=3), :] = mid_one[pl.ds(0, 192, stride=2), :]
        buffer[pl.ds(base + ROW_MID + 1, 192, stride=3), :] = jnp.where(
            lane < 64, mid_two[pl.ds(0, 192, stride=2), :], odd
        )
        buffer[pl.ds(base + ROW_MID + 2, 192, stride=3), :] = jnp.where(
            lane < 64, odd, pltpu.roll(mid_two[pl.ds(1, 192, stride=2), :], 64, 1)
        )
        low_one[...] = dot_tn(m1_all[...], g2_all[...])
        lane = iota((48, 128), 1)
        r0, r1, r2, r3 = (low_one[pl.ds(s, 48, stride=4), :] for s in range(4))
        r1, r2, r3 = pltpu.roll(r1, 96, 1), pltpu.roll(r2, 64, 1), pltpu.roll(r3, 32, 1)
        buffer[pl.ds(base + ROW_LOW, 48, stride=3), :] = jnp.where(lane < 96, r0, r1)
        buffer[pl.ds(base + ROW_LOW + 1, 48, stride=3), :] = jnp.where(lane < 64, r1, r2)
        buffer[pl.ds(base + ROW_LOW + 2, 48, stride=3), :] = jnp.where(lane < 32, r2, r3)
        m2_doubled = dot_nn(m2_all[...], doubling()).astype(BF16)
        both = dot_tn(gl_all[...], m2_doubled)
        head = jnp.where(iota((1, 256), 1) % 2 == 0, both[0:1, :], both[1:2, :])
        buffer[base + ROW_OUT : base + ROW_OUT + 1, :] = head[:, 0:128]
        buffer[base + ROW_OUT + 1 : base + ROW_OUT + 2, :] = pltpu.roll(head[:, 128:256], 64, 1)
        tick("pred")

        def finish(b):
            rows = rows_of(b)
            xhat, rstd = normalise(load_padded(tokens, b))
            dh0 = dot_nt(ga_all[rows, :], w_in[...])
            acc_vec[A_PRED_GAIN : A_PRED_GAIN + 1, :] += column_sum(dh0 * xhat)
            acc_vec[A_PRED_SHIFT : A_PRED_SHIFT + 1, :] += column_sum(dh0)
            dn1 = dot_nt(dqkv_all[rows, :], w_qkv[...])
            acc_vec[A_ONE_GAIN : A_ONE_GAIN + 1, :] += column_sum(dn1 * xhat)
            acc_vec[A_ONE_SHIFT : A_ONE_SHIFT + 1, :] += column_sum(dn1)
            total = (
                dx_all[rows, :]
                + normalise_back(dn1, vec(V_ONE_GAIN), xhat, rstd)
                + normalise_back(dh0, vec(V_PRED_GAIN), xhat, rstd)
            )
            input_gradient[b] = total[:SLOT].astype(BF16)

        for b in range(IMG):
            finish(b)
            tick(f"finish{b}")


    pl.run_scoped(
        second_half,
        pltpu.VMEM((IMG, ROWS, 128), F32),
        pltpu.VMEM((ALL, D), BF16),
        pltpu.VMEM((ALL, D), BF16),
        pltpu.VMEM((ALL, D), BF16),
        pltpu.VMEM((ALL, 256), BF16),
        pltpu.VMEM((ALL, 256), BF16),
        pltpu.VMEM((ALL, 128), BF16),
        pltpu.VMEM((ALL, 128), BF16),
        pltpu.VMEM((ALL, 128), BF16),
        pltpu.VMEM((ALL, 3 * D), BF16),
        pltpu.VMEM((D, 128), F32),
        pltpu.VMEM((D, 128), F32),
        pltpu.VMEM((256, 128), F32),
    )

    base = starts["vecs"]
    lane = iota((1, 128), 1)
    for r, a in enumerate((A_PRED_GAIN, A_PRED_SHIFT, A_IN_BIAS)):
        put_row(buffer, base + 3 * r, acc_vec[a : a + 1, :])
    mid_bias = acc_small[A_MID_BIAS : A_MID_BIAS + 1, 0:256]
    low_bias = pltpu.roll(acc_small[A_LOW_BIAS : A_LOW_BIAS + 1, 0:128], 64, 1)
    out_bias = pltpu.roll(acc_small[A_OUT_BIAS : A_OUT_BIAS + 1, 0:128], 32, 1)
    buffer[base + 9 : base + 10, :] = mid_bias[:, 0:128]
    buffer[base + 10 : base + 11, :] = jnp.where(lane < 64, mid_bias[:, 128:256], low_bias)
    buffer[base + 11 : base + 12, :] = jnp.where(lane < 32, low_bias, out_bias)
    for r, a in enumerate(
        (A_ONE_GAIN, A_ONE_SHIFT, A_QUERY_BIAS, A_VALUE_BIAS, A_PROJ_BIAS, A_TWO_GAIN, A_TWO_SHIFT)
    ):
        put_row(buffer, base + 12 + 3 * r, acc_vec[a : a + 1, :])
    put_row(buffer, base + 33, acc_small[A_UP_BIAS : A_UP_BIAS + 1, :])
    put_row(buffer, base + 45, acc_vec[A_DOWN_BIAS : A_DOWN_BIAS + 1, :])

    def settle(name, ordered):
        base = starts[name]
        if name.startswith("m"):
            n = int(name[1:])
            for c in range(4):
                ordered[pl.ds(ROW_UP + 4 * n + c, D, stride=12), :] = buffer[base + c * D : base + (c + 1) * D, :]
            ordered[ROW_DOWN + 1536 * n : ROW_DOWN + 1536 * (n + 1), :] = buffer[base + 1536 : base + 3072, :]
        elif name.startswith("qkv"):
            p = int(name[3:])
            for c in range(3):
                ordered[pl.ds(ROW_QKV + 3 * c + p, D, stride=9), :] = buffer[base + c * D : base + (c + 1) * D, :]
        else:
            first, rows = {"proj": (ROW_PROJ, 1152), "pred": (0, ROW_QKV), "vecs": (ROW_VEC, 48)}[name]
            ordered[first : first + rows, :] = buffer[base : base + rows, :]

    tick("vecs")
    owner = {}
    for name in plan:
        owner.setdefault(name if name in starts else name[:-1], []).append(name)
    settled = set()

    def hand_over(ordered):
        early = slice(ROW_PROJ // 8 * 8 + 8, ROW_VEC // 8 * 8)
        parts = (early, slice(0, early.start), slice(early.stop, GRAD_ROWS))
        copies = [pltpu.make_async_copy(ordered.at[part, :], grads.at[part, :], sem.at[i]) for i, part in enumerate(parts)]

        def look():
            for section, members in owner.items():
                if section not in settled and all(done[m] == len(plan[m]) for m in members):
                    settle(section, ordered)
                    settled.add(section)
                    if section in EARLY and all(e in settled for e in EARLY):
                        copies[0].start()

        look()
        for name in DRAIN:
            run(take(name))
            look()
        while any(done[n] < len(plan[n]) for n in plan):
            for name in plan:
                run(take(name))
            look()
        for copy in copies[1:]:
            copy.start()
        for copy in copies:
            copy.wait()

    pl.run_scoped(hand_over, pltpu.VMEM((GRAD_ROWS, 128), F32))


EARLY = ("m0", "m1", "m2", "proj")

TICKS = {
    "part0": ("m0a", "m0b", "m0c",),
    "part1.0": ("m0a", "m0b",),
    "part1.1": ("m0c",),
    "part1": ("m1",),
    "part2.1": ("m0a", "m1", "m0b",),
    "part2": ("m2",),
    "descend1": ("m0a",),
    "proj": ("proj", "m0c", "m2",),
    "pair0.1": ("proj", "m0a", "m0b",),
    "qkv0": ("qkv0",),
    "pair1.1": ("m0c", "m1", "qkv0",),
    "pair1.3": ("proj", "m0b", "m0c",),
    "qkv1": ("qkv1", "m2",),
    "pair2.0": ("m0a",),
    "pair2.1": ("m0b", "qkv1", "m0c", "qkv0",),
    "pair2.3": ("proj", "m0a",),
    "qkv2": ("qkv2a", "qkv2b", "m1",),
    "predict0": ("qkv2a", "qkv2b", "qkv1", "m2", "qkv0", "m0b", "m0c", "proj",),
    "predict2": ("m0a", "qkv1", "qkv2a", "qkv2b",),
    "predict3": ("m1", "m0a", "m2", "m0b", "qkv0",),
    "pred": ("preda", "predb", "qkv2a", "qkv2b", "m0b",),
    "finish1": ("qkv1", "preda", "proj", "m0c", "predb",),
    "finish3": ("m2", "m0c", "qkv2b",),
    "vecs": ("vecs", "qkv0",),
}
DRAIN = (
    "qkv1", "vecs", "proj", "qkv2a", "m1", "m1", "predb", "preda", "m2", "vecs", "qkv2b", "qkv0", "proj",
    "qkv1", "predb", "qkv2a", "m2", "qkv0", "qkv2b", "qkv1", "preda", "proj", "vecs", "qkv2a", "predb",
    "qkv0", "qkv2b", "m2", "proj", "qkv2a", "qkv1", "preda", "vecs", "proj", "qkv0", "qkv2b", "predb", "qkv0",
    "qkv2a", "qkv1", "predb", "qkv1", "preda", "m2", "vecs", "preda", "qkv2b", "qkv2a", "m2", "vecs", "qkv2b",
    "qkv2a",
)

(
    V_PRED_GAIN, V_PRED_SHIFT, V_IN_BIAS, V_MID_BIAS, V_LOW_BIAS, V_OUT_BIAS, V_ONE_GAIN, V_ONE_SHIFT, V_PROJ_BIAS,
    V_TWO_GAIN, V_TWO_SHIFT, V_UP_BIAS, V_DOWN_BIAS,
) = range(13)
(
    A_PRED_GAIN, A_PRED_SHIFT, A_IN_BIAS, A_ONE_GAIN, A_ONE_SHIFT, A_QUERY_BIAS, A_VALUE_BIAS, A_PROJ_BIAS, A_TWO_GAIN,
    A_TWO_SHIFT, A_DOWN_BIAS,
) = range(11)
A_UP_BIAS, A_MID_BIAS, A_LOW_BIAS, A_OUT_BIAS = range(4)


def doubling():
    return (iota((128, 256), 1) // 2 == iota((128, 256), 0)).astype(F32).astype(BF16)


CHUNK = 5952
CHUNKS = ((10944, 4800), (0, 5376), (5328, 5952))


def unpack(flat, flat_end, flat_one, rows, sems, others, w_qkv, w_proj, w_up, w_down, w_in, w_mid, w_low, w_out, vecs, qkv_bias):
    copies = [
        pltpu.make_async_copy(
            flat.at[pl.ds(start * 128, count * 128)], flat_one[i % 2].at[pl.ds(0, count * 128)], sems.at[i]
        )
        for i, (start, count) in enumerate(CHUNKS)
    ]

    def spread(i):
        copies[i].wait()

        def body(k, _):
            rows[pl.ds(pl.multiple_of(k * 192, 192), 192), :] = flat_one[i % 2][
                pl.ds(pl.multiple_of(k * 24576, 24576), 24576)
            ].reshape(192, 128)
            return 0

        lax.fori_loop(0, CHUNKS[i][1] // 192, body, 0)

    copies[0].start()
    copies[1].start()
    for copy in others:
        copy.start()
    spread(0)
    copies[2].start()
    start, count = CHUNKS[0]
    rows[count : count + 8, :] = flat_end[...].reshape(8, 128)
    for c in range(3):
        w_down[:, c * 128 : (c + 1) * 128] = shifted(rows, ROW_DOWN - 1 + c - start, MLP, 3).astype(BF16)
    lane = iota((16, 128), 1)
    at = 15697 - start
    vec_one = pltpu.roll(jnp.where(lane < 64, rows[at + 1 : at + 17, :], rows[at : at + 16, :]), 64, 1)
    lane = iota((36, 128), 1)
    at = 15708 - start
    vec_two = pltpu.roll(jnp.where(lane < 98, rows[at + 1 : at + 37, :], rows[at : at + 36, :]), 30, 1)
    rows[0:16, :] = vec_one
    rows[16:52, :] = vec_two
    for r, base in (
        (V_PRED_GAIN, 0), (V_PRED_SHIFT, 3), (V_IN_BIAS, 6), (V_ONE_GAIN, 16), (V_ONE_SHIFT, 19), (V_PROJ_BIAS, 28),
        (V_TWO_GAIN, 31), (V_TWO_SHIFT, 34), (V_DOWN_BIAS, 49),
    ):
        vecs[r : r + 1, 0:D] = row_of(rows, base, 3)
    vecs[V_UP_BIAS : V_UP_BIAS + 1, :] = row_of(rows, 37, 12)
    lane = iota((1, 128), 1)
    zero = jnp.zeros((1, 128), F32)
    r9, r10, r11 = (rows[r : r + 1, :] for r in (9, 10, 11))
    vecs[V_MID_BIAS : V_MID_BIAS + 1, 0:128] = r9
    vecs[V_MID_BIAS : V_MID_BIAS + 1, 128:256] = jnp.where(lane < 64, r10, zero)
    vecs[V_LOW_BIAS : V_LOW_BIAS + 1, 0:128] = jnp.where(
        lane < 96, pltpu.roll(jnp.where(lane < 64, r11, r10), 64, 1), zero
    )
    vecs[V_OUT_BIAS : V_OUT_BIAS + 1, 0:128] = jnp.where(lane < 2, pltpu.roll(r11, 96, 1), zero)
    for p in range(PAIRS):
        qkv_bias[0:1, p * D : p * D + 128] = rows[22 + p : 23 + p, :]
        qkv_bias[0:1, p * D + 128 : p * D + 256] = zero
        qkv_bias[0:1, p * D + 256 : p * D + 384] = rows[25 + p : 26 + p, :]

    spread(1)
    for c in range(3):
        w_in[:, c * 128 : (c + 1) * 128] = rows[pl.ds(c, D, stride=3), :].astype(BF16)
        for p in range(PAIRS):
            tile = shifted(rows, ROW_QKV - 1 + 3 * c + p, D, 9).astype(BF16)
            w_qkv[:, p * D + c * 128 : p * D + (c + 1) * 128] = tile

    a, b, c = (rows[pl.ds(ROW_MID + s, 192, stride=3), :] for s in range(3))
    lane = iota((192, 128), 1)
    zero = jnp.zeros((192, 128), F32)

    def interleave(tiles):
        count = len(tiles)
        size = tiles[0].shape[0]
        for s, tile in enumerate(tiles):
            rows[pl.ds(s, size, stride=count), :] = tile
        return rows[0 : size * count, :].astype(BF16)

    w_mid[:, 0:128] = interleave((a, pltpu.roll(jnp.where(lane < 64, c, b), 64, 1)))
    w_mid[:, 128:256] = interleave(
        (jnp.where(lane < 64, b, zero), jnp.where(lane < 64, pltpu.roll(c, 64, 1), zero))
    )
    lane = iota((48, 128), 1)
    a, b, c = (rows[pl.ds(ROW_LOW + s, 48, stride=3), :] for s in range(3))
    low = (
        a,
        jnp.where(lane < 32, pltpu.roll(a, 32, 1), pltpu.roll(b, 32, 1)),
        jnp.where(lane < 64, pltpu.roll(b, 64, 1), pltpu.roll(c, 64, 1)),
        pltpu.roll(c, 96, 1),
    )
    w_low[0:192, :] = interleave([jnp.where(lane < 96, tile, 0.0) for tile in low])
    w_low[192:256, :] = jnp.zeros((64, 128), BF16)
    head = jnp.concatenate([rows[ROW_OUT : ROW_OUT + 1, :], rows[ROW_OUT + 1 : ROW_OUT + 2, :]], 1)
    head = jnp.broadcast_to(head, (128, 256))
    lane = iota((128, 256), 1)
    chosen = (lane % 2 == iota((128, 256), 0)) & (lane < 192)
    w_out[...] = dot_nt(jnp.where(chosen, head, 0.0).astype(BF16), doubling()).astype(BF16)

    spread(2)
    start = CHUNKS[2][0]
    for c in range(3):
        w_proj[:, c * 128 : (c + 1) * 128] = shifted(rows, ROW_PROJ - 1 + c - start, D, 3).astype(BF16)
    for c in range(12):
        w_up[:, c * 128 : (c + 1) * 128] = shifted(rows, ROW_UP - 1 + c - start, D, 12).astype(BF16)


def counting(sizes, groups, keep, out, held, landed, sems):
    stages = [s for axis in ("gy", "gx", "gz") for s in whole(sizes, axis)]
    first = [0]
    for stage in stages:
        first.append(first[-1] + stage[2] - 1)

    def copies(s):
        return [
            pltpu.make_async_remote_copy(
                held.at[s], landed.at[first[s] + slot], sems.at[0, first[s] + slot], sems.at[1, first[s] + slot],
                device, MESH,
            )
            for device, slot, _ in partners(stages[s])
        ]

    def begin():
        kept = jnp.zeros((1, 1), F32)
        valid = jnp.zeros((1, 1), F32)
        position = iota((1, SLOT), 1)
        for b in range(IMG):
            spatial = jnp.where((position > 0) & (position < length_of(groups, b)), 1.0, 0.0)
            kept += jnp.sum(spatial * keep[b : b + 1, :].astype(F32), keepdims=True)
            valid += jnp.sum(spatial, keepdims=True)
        row = iota((8, 128), 0)
        held[0] = jnp.where(row == 0, kept, jnp.where(row == 1, valid, 0.0))

    def step(s):
        if s == 0:
            begin()
        else:
            total = held[s - 1]
            for slot, copy in enumerate(copies(s - 1)):
                copy.wait()
                total = total + landed[first[s - 1] + slot]
            held[s] = total
        if s < len(stages):
            for copy in copies(s):
                copy.start()
        else:
            total = held[s]
            row = iota((8, 128), 0)
            excess = total[0:1, :] / total[1:2, :] - KEEP_TARGET
            loss = RATIO_WEIGHT * total[1:2, :] * excess * excess
            out[...] = jnp.where(row == 2, 2.0 * RATIO_WEIGHT * excess, jnp.where(row == 3, loss, total))

    return [functools.partial(step, s) for s in range(len(stages) + 1)]


def layer(sizes, *operands):
    pieces, starts, rows = pieces_of(sizes)
    copies = max(sum(p.copies for p in pieces), 1)
    fits = rows <= 17408
    small = max(sum(sizes[a] - 1 for a in AXES), 1)
    vmem = pl.BlockSpec(memory_space=pltpu.VMEM)
    hbm = pl.BlockSpec(memory_space=pltpu.HBM)
    shape = jax.ShapeDtypeStruct
    return pl.pallas_call(
        functools.partial(layer_kernel, sizes, pieces, starts),
        grid=(1,),
        out_shape=(
            shape((IMG, SLOT, D), BF16),
            shape((IMG, SLOT, D), BF16),
            pltpu.VMEM((GRAD_ROWS, 128), F32) if fits else shape((GRAD_ROWS, 128), F32),
            shape((8, 128), F32),
        ),
        in_specs=[
            hbm, hbm, hbm, hbm, hbm,
            pl.BlockSpec((1024,), lambda i: (NPARAM // 1024,)),
        ],
        out_specs=[vmem, vmem, pl.BlockSpec(memory_space=pl.ANY), vmem],
        scratch_shapes=[
            pltpu.VMEM((D, 3 * D), BF16),
            pltpu.VMEM((D, D), BF16),
            pltpu.VMEM((D, MLP), BF16),
            pltpu.VMEM((MLP, D), BF16),
            pltpu.VMEM((D, D), BF16),
            pltpu.VMEM((D, 256), BF16),
            pltpu.VMEM((256, 128), BF16),
            pltpu.VMEM((128, 128), BF16),
            pltpu.VMEM((16, MLP), F32),
            pltpu.VMEM((8, 3 * D), F32),
            pltpu.VMEM((IMG, PAIRS, WIDE, 128), BF16),
            pltpu.VMEM((IMG, PAIRS, ROWS, 128), BF16),
            pltpu.VMEM((IMG, PAIRS, ROWS, 128), BF16),
            pltpu.VMEM((IMG, PAIRS, WIDE, 128), BF16),
            pltpu.VMEM((IMG, PAIRS, 3, 8, 256), F32),
            pltpu.VMEM((PAIRS, 128, ROWS), BF16),
            pltpu.VMEM((IMG, D, WIDE), BF16),
            pltpu.VMEM((ALL, D), BF16),
            pltpu.VMEM((ALL, D), F32),
            pltpu.VMEM((16, D), F32),
            pltpu.VMEM((8, MLP), F32),
            pltpu.VMEM((rows, 128), F32),
            pltpu.VMEM((rows, 128), F32),
            pltpu.SemaphoreType.DMA((4, copies)),
            pltpu.SemaphoreType.REGULAR((max(sum(len(p.stages) for p in pieces), 1),)),
            pltpu.VMEM((4, 8, 128), F32),
            pltpu.VMEM((small, 8, 128), F32),
            pltpu.SemaphoreType.DMA((2, small)),
            pltpu.SemaphoreType.DMA((3,)),
            pltpu.SMEM((IMG,), jnp.int32),
            pltpu.VMEM((IMG, SLOT, D), BF16),
            pltpu.VMEM((IMG, SLOT, D), BF16),
            pltpu.VMEM((IMG, SLOT), jnp.int32),
            pltpu.SemaphoreType.DMA((4,)),
        ],
        compiler_params=pltpu.CompilerParams(
            collective_id=0, has_side_effects=True, vmem_limit_bytes=(95 if fits else 116) << 19
        ),
        name="layer",
    )(*operands)


UPDATE_ROWS = 4032


def update_kernel(
    grads, after, counts, mixed_in, gradient_in, params, momentum, average,
    new_params, new_momentum, new_average, mixed, input_gradient, loss, block, joined,
):
    i = pl.program_id(0)
    n = UPDATE_ROWS
    mixed[...] = mixed_in[...]
    input_gradient[...] = gradient_in[...]
    loss[0, 0] = counts[3, 0]
    joined[0:n, :] = grads[...]
    joined[n : n + 8, :] = after[...]
    here = joined[0:n, :]
    row = iota((n, 128), 0) + i * n
    lane = iota((n, 128), 1)
    moved = pltpu.roll(jnp.where(lane < 64, joined[1 : n + 1, :], here), 64, 1)
    flat = jnp.where(row < ROW_QKV - 1, here, moved)
    joined[0:n, :] = flat

    @pl.when(i == pl.num_programs(0) - 1)
    def _():
        first = 15708 - (NPARAM // (n * 128)) * n
        lane = iota((40, 128), 1)
        one = grads[first + 1 : first + 41, :]
        two = grads[first + 2 : first + 42, :]
        tail = pltpu.roll(jnp.where(lane < 30, two, one), 98, 1)
        keep_old = (iota((40, 128), 0) == 0) & (lane < 98)
        joined[first : first + 40, :] = jnp.where(keep_old, joined[first : first + 40, :], tail)
        block[...] = grads[first + 2 : first + 38, :].reshape(4608)

    g = joined[0:n, :].reshape(n * 128)
    moment = MOMENTUM_DECAY * momentum[...] + g
    value = params[...] - LEARN_RATE * (g + MOMENTUM_DECAY * moment)
    new_momentum[...] = moment
    new_params[...] = value
    new_average[...] = AVERAGE_DECAY * average[...] + (1.0 - AVERAGE_DECAY) * value


def update(grads, counts, mixed, input_gradient, params, momentum, average):
    n = UPDATE_ROWS
    flat = pl.BlockSpec((n * 128,), lambda i: (i,))
    image = pl.BlockSpec((1, SLOT, D), lambda i: (jnp.minimum(i, IMG - 1), 0, 0))
    out = jax.ShapeDtypeStruct((NPARAM,), F32)
    return pl.pallas_call(
        update_kernel,
        grid=(pl.cdiv(NPARAM, n * 128),),
        out_shape=(
            out, out, out,
            jax.ShapeDtypeStruct(mixed.shape, BF16),
            jax.ShapeDtypeStruct(mixed.shape, BF16),
            jax.ShapeDtypeStruct((1, 1), F32),
            jax.ShapeDtypeStruct((4608,), F32),
        ),
        in_specs=[
            pl.BlockSpec((n, 128), lambda i: (i, 0)),
            pl.BlockSpec((8, 128), lambda i: ((i + 1) * (n // 8), 0)),
            pl.BlockSpec((8, 128), lambda i: (0, 0)),
            image,
            image,
            flat,
            flat,
            flat,
        ],
        out_specs=[
            flat, flat, flat, image, image,
            pl.BlockSpec(memory_space=pltpu.SMEM),
            pl.BlockSpec((4608,), lambda i: (0,)),
        ],
        scratch_shapes=[pltpu.VMEM((n + 8, 128), F32)],
        compiler_params=pltpu.CompilerParams(vmem_limit_bytes=28 << 20),
        name="update",
    )(
        grads, grads,
        *(pltpu.with_memory_space_constraint(x, pltpu.HBM) for x in (counts, mixed, input_gradient)),
        params,
        *(pltpu.with_memory_space_constraint(x, pltpu.HBM) for x in (momentum, average)),
    )


GRAD_ROWS = -(-(NPARAM // 128 + 40) // UPDATE_ROWS) * UPDATE_ROWS + 8


def solution(mesh):
    sizes = dict(mesh.shape)

    def per_device(tokens, cotangent, groups, keep_mask, params, momentum, average):
        mixed, input_gradient, grads, counts = layer(sizes, groups, tokens, cotangent, keep_mask, params, params)
        new_params, new_momentum, new_average, mixed, input_gradient, loss, block = update(
            grads, counts, mixed, input_gradient, params, momentum, average
        )
        return (mixed, input_gradient, loss.reshape(()), new_params, new_momentum, new_average, block)

    split = P(("gx", "gy", "gz"))
    return jax.shard_map(
        per_device,
        mesh=mesh,
        in_specs=(split, split, split, split, P(), P(), P()),
        out_specs=(split, split, P(), P(), P(), P(), P()),
        check_vma=False,
    )
```

```python
import functools
import math

import jax
import jax.numpy as jnp
from jax import lax
from jax.experimental import pallas as pl
from jax.experimental.pallas import tpu as pltpu
from jax.sharding import PartitionSpec as P

MESH = pl.DeviceIdType.MESH
F32 = jnp.float32
BF16 = jnp.bfloat16

D = 384
HEADS = 6
PAIRS = 3
MLP = 1536
LEN_A, LEN_B, LEN_C = 101, 197, 325
IMG = 4
SLOT = 328
ROWS = 336
WIDE = 384
ALL = IMG * ROWS
NPARAM = 2015330
NORM_EPS = 1e-06
RATIO_WEIGHT = 2.0
KEEP_TARGET = 0.7
MOMENTUM_DECAY = 0.5
AVERAGE_DECAY = 0.5
LEARN_RATE = 0.0001

ROW_MID = 1152
ROW_LOW = 1728
ROW_OUT = 1872
ROW_QKV = 1874
ROW_PROJ = 5330
ROW_UP = 6482
ROW_DOWN = 11090
ROW_VEC = 15698
ROW_BLOCK = 15710
EARLY_BASE = 5328
EARLY_ROWS = 10376
FLAT_ROWS = 15752


def dot_nn(a, b):
    return lax.dot_general(a, b, (((1,), (0,)), ((), ())), preferred_element_type=F32)


def dot_nt(a, b):
    return lax.dot_general(a, b, (((1,), (1,)), ((), ())), preferred_element_type=F32)


def dot_tn(a, b):
    return lax.dot_general(a, b, (((0,), (0,)), ((), ())), preferred_element_type=F32)


def iota(shape, axis):
    return lax.broadcasted_iota(jnp.int32, shape, axis)


def gelu_pair(v):
    cdf = 0.5 * lax.erf(v * 0.7071067811865476) + 0.5
    return v * cdf, cdf + v * jnp.exp(v * v * -0.5) * 0.3989422804014327


def normalise(x):
    mean = jnp.sum(x, -1, keepdims=True) * (1.0 / D)
    centered = x - mean
    spread = jnp.sum(centered * centered, -1, keepdims=True) * (1.0 / D)
    rstd = lax.rsqrt(spread + NORM_EPS)
    return centered * rstd, rstd


def normalise_back(grad, gain, xhat, rstd):
    scaled = grad * gain
    first = jnp.sum(scaled, -1, keepdims=True) * (1.0 / D)
    second = jnp.sum(scaled * xhat, -1, keepdims=True) * (1.0 / D)
    return rstd * (scaled - first - xhat * second)


def column_sum(x):
    return jnp.sum(x, 0, keepdims=True)


def load_padded(ref, b):
    x = ref[b].astype(F32)
    return jnp.concatenate([x, jnp.zeros((ROWS - SLOT, D), F32)], 0)


def length_of(groups, b):
    g = groups[b]
    return jnp.where(g == 0, LEN_A, jnp.where(g == 1, LEN_B, LEN_C))


def policy_lanes(keep, length, b):
    row = keep[pl.ds(b, 1), :].astype(F32)
    row = jnp.concatenate([row, jnp.zeros((1, WIDE - SLOT), F32)], 1)
    kept = jnp.broadcast_to(row, (128, WIDE)).T[:ROWS]
    position = iota((ROWS, 128), 0)
    return jnp.where(position == 0, 1.0, jnp.where(position < length, kept, 0.0))


def split_heads(tile):
    left = iota(tile.shape, 1) < 64
    zero = jnp.zeros_like(tile)
    return jnp.concatenate([jnp.where(left, tile, zero), jnp.where(left, zero, tile)], 0)


def diagonal_blocks(x):
    return jnp.concatenate([x[:64, :128], x[64:, 128:]], 0)


def put(ref, base, stride, value):
    rows, columns = value.shape
    for c in range(columns // 128):
        ref[pl.ds(base + c, rows, stride=stride), :] = value[:, c * 128 : (c + 1) * 128]


def put_row(ref, base, value):
    for c in range(value.shape[1] // 128):
        ref[base + c : base + c + 1, :] = value[:, c * 128 : (c + 1) * 128]


def row_of(ref, base, count):
    return jnp.concatenate([ref[base + c : base + c + 1, :] for c in range(count)], 1)


def shifted(ref, base, rows, stride):
    first = ref[pl.ds(base, rows, stride=stride), :]
    second = ref[pl.ds(base + 1, rows, stride=stride), :]
    low = iota((rows, 128), 1) < 64
    return pltpu.roll(jnp.where(low, second, first), 64, 1)


AXES = ("gx", "gy", "gz")


def digits(sizes, axis):
    size, stride, found = sizes[axis], 1, []
    while size > 1:
        base = 2 if size % 2 == 0 else size
        found.append((axis, stride, base))
        size //= base
        stride *= base
    return found


def whole(sizes, axis):
    return [(axis, 1, sizes[axis])] if sizes[axis] > 1 else []


def digit_of(stage):
    axis, stride, base = stage
    return lax.rem(lax.axis_index(axis) // stride, base)


def partners(stage):
    axis, stride, base = stage
    mine = digit_of(stage)
    found = []
    for k in range(1, base):
        other = lax.rem(mine + k, base)
        index = lax.axis_index(axis) + (other - mine) * stride
        found.append((tuple(index if a == axis else lax.axis_index(a) for a in AXES), k - 1, other))
    return found


def greet(sizes):
    barrier = pltpu.get_barrier_semaphore()
    total = 0
    for axis in AXES:
        for stage in whole(sizes, axis):
            for device, _, _ in partners(stage):
                pl.semaphore_signal(barrier, inc=1, device_id=device, device_id_type=MESH)
                total += 1
    return barrier, total


class Piece:
    def __init__(self, name, rows, base, stages):
        self.name, self.rows, self.base, self.stages = name, rows, base, stages
        self.copies = sum(s[2] - 1 for s in stages)

    def steps(self, buffer, landing, sems, free, first, first_stage):
        stages = self.stages
        rows_after = [self.rows]
        for stage in stages:
            rows_after.append(rows_after[-1] // stage[2])
        landing_at, sem_at = [self.base], [first]
        for s, stage in enumerate(stages):
            landing_at.append(landing_at[-1] + (stage[2] - 1) * rows_after[s + 1])
            sem_at.append(sem_at[-1] + stage[2] - 1)

        def place(s):
            begin = self.base
            for i in range(s):
                begin = begin + digit_of(stages[i]) * rows_after[i + 1]
            return begin

        def block(s, digit):
            return pl.ds(pl.multiple_of(place(s) + digit * rows_after[s + 1], 8), rows_after[s + 1])

        def scatter(s):
            found = []
            for device, slot, other in partners(stages[s]):
                found.append(
                    pltpu.make_async_remote_copy(
                        buffer.at[block(s, other), :],
                        landing.at[pl.ds(landing_at[s] + slot * rows_after[s + 1], rows_after[s + 1]), :],
                        sems.at[0, sem_at[s] + slot],
                        sems.at[1, sem_at[s] + slot],
                        device,
                        MESH,
                    )
                )
            return found

        def gather(s):
            found = []
            for device, slot, _ in partners(stages[s]):
                own = buffer.at[block(s, digit_of(stages[s])), :]
                found.append(
                    pltpu.make_async_remote_copy(
                        own, own, sems.at[2, sem_at[s] + slot], sems.at[3, sem_at[s] + slot], device, MESH
                    )
                )
            return found

        def start(copies):
            for copy in copies:
                copy.start()

        def end_scatter(s):
            for copy in scatter(s):
                copy.wait()
            for device, _, _ in partners(stages[s]):
                pl.semaphore_signal(free.at[first_stage + s], inc=1, device_id=device, device_id_type=MESH)
            rows = rows_after[s + 1]
            begin = place(s) + digit_of(stages[s]) * rows
            step = math.gcd(rows, 64)

            def body(i, _):
                own = pl.ds(pl.multiple_of(begin + i * step, 8), step)
                total = buffer[own, :]
                for slot in range(stages[s][2] - 1):
                    at = landing_at[s] + slot * rows
                    total = total + landing[pl.ds(pl.multiple_of(at + i * step, 8), step), :]
                buffer[own, :] = total
                return 0

            lax.fori_loop(0, rows // step, body, 0)

        def end_gather(s):
            for copy in gather(s):
                copy.wait()

        count = len(stages)
        found = []
        for s in range(count):

            def there(s=s):
                if s:
                    end_scatter(s - 1)
                start(scatter(s))

            found.append(there)
        for s in reversed(range(count)):

            def back(s=s):
                if s == count - 1:
                    end_scatter(s)
                else:
                    end_gather(s + 1)
                pl.semaphore_wait(free.at[first_stage + s], stages[s][2] - 1)
                start(gather(s))

            found.append(back)
        if count:
            found.append(lambda: end_gather(0))
        return found


SECTIONS = (
    ("m0", 3072, ((1024, "CGAB"), (1024, "CXHY"), (1024, "CHXY"),)),
    ("m1", 3072, ((3072, "CGH"),)),
    ("m2", 3072, ((3072, "CAXYB"),)),
    ("proj", 1152, ((1280, "CYXAB"),)),
    ("qkv0", 1152, ((1280, "CXAYB"),)),
    ("qkv1", 1152, ((1280, "CYXAB"),)),
    ("qkv2", 1152, ((512, "CAXYB"), (768, "CYXAB"),)),
    ("pred", 1874, ((1280, "CGH"), (768, "CHG"),)),
    ("vecs", 48, ((256, "CGH"),)),
)


def pieces_of(sizes):
    unit = 8 * math.prod(sizes.values())
    core, x, z = digits(sizes, "gy"), digits(sizes, "gx"), digits(sizes, "gz")
    ways = {
        "C": core, "X": x[:1], "Y": x[1:], "A": z[:1], "B": z[1:], "G": whole(sizes, "gx"), "H": whole(sizes, "gz"),
    }
    found, starts, base = [], {}, 0
    for name, rows, parts in SECTIONS:
        starts[name] = base
        if unit > 256 or len(parts) == 1:
            parts = ((rows, parts[0][1]),)
        for i, (part_rows, way) in enumerate(parts):
            stages = [stage for letter in way for stage in ways[letter]]
            part_rows = -(-part_rows // unit) * unit
            found.append(Piece(name + "abcd"[i] if len(parts) > 1 else name, part_rows, base, stages))
            base += part_rows
    return found, starts, base


PART = 512
PARTS = MLP // PART
HALF = ALL // 4


def layer_kernel(
    sizes, pieces, starts,
    groups_in, tokens_in, cotangent_in, keep_in, flat, flat_end,
    mixed_out, gradient_out, grads, counts,
    w_qkv, w_proj, w_up, w_down, w_in, w_mid, w_low, w_out, vecs, qkv_bias,
    q_all, k_all, v_all, do_all, lse_all, v_turned, o_turned, n1_all, dx_all, acc_vec, acc_small,
    buffer, landing, sems, free, held, landed, count_sems, sem, groups, tokens, cotangent, keep, in_sems,
    mixed, input_gradient, out_sems,
):
    plan, first, first_stage = {}, 0, 0
    for p in pieces:
        plan[p.name] = p.steps(buffer, landing, sems, free, first, first_stage)
        first += p.copies
        first_stage += len(p.stages)
    done = {p.name: 0 for p in pieces}

    def take(*names):
        found = []
        for name in names:
            if name in plan and done[name] < len(plan[name]):
                found.append(plan[name][done[name]])
                done[name] += 1
        return found

    def run(steps):
        for step in steps:
            step()

    def tick(name):
        run(take(*TICKS.get(name, ())))

    arriving = [
        pltpu.make_async_copy(source, target, in_sems.at[i])
        for i, (source, target) in enumerate(
            ((groups_in, groups), (keep_in, keep), (tokens_in, tokens), (cotangent_in, cotangent))
        )
    ]
    leaving = [
        pltpu.make_async_copy(mixed, mixed_out, out_sems.at[0]),
        pltpu.make_async_copy(input_gradient, gradient_out, out_sems.at[1]),
    ]
    for copy in arriving[:2]:
        copy.start()
    barrier, greetings = greet(sizes)
    count_steps = counting(sizes, groups, keep, counts, held, landed, count_sems)

    def weights(one, two, rows):
        unpack(flat, flat_end, (one, two), rows, sem, arriving[2:], w_qkv, w_proj, w_up, w_down, w_in, w_mid, w_low, w_out, vecs,
               qkv_bias)

    pl.run_scoped(
        weights,
        pltpu.VMEM((CHUNK * 128,), F32),
        pltpu.VMEM((CHUNK * 128,), F32),
        pltpu.VMEM((CHUNK + 8, 128), F32),
    )
    for copy in arriving:
        copy.wait()
    if greetings:
        pl.semaphore_wait(barrier, greetings)
    run(count_steps[:1])

    def vec(r, size=D):
        return vecs[r : r + 1, 0:size]

    acc_vec[...] = jnp.zeros_like(acc_vec)
    acc_small[...] = jnp.zeros_like(acc_small)

    def rows_of(b):
        if isinstance(b, int):
            return slice(b * ROWS, (b + 1) * ROWS)
        return pl.ds(pl.multiple_of(b * ROWS, 16), ROWS)

    x1_all = dx_all

    def first_half(x2_all, dn2_all, n2_all, gd_all, up_part, gup_part, weight):
        def attend(b, _):
            length = length_of(groups, b)
            x = load_padded(tokens, b)
            xhat, _ = normalise(x)
            n1 = (xhat * vec(V_ONE_GAIN) + vec(V_ONE_SHIFT)).astype(BF16)
            n1_all[rows_of(b), :] = n1
            zeros = jnp.zeros((WIDE - ROWS, 128), BF16)
            for p in range(PAIRS):
                part = dot_nn(n1, w_qkv[:, p * D : (p + 1) * D]) + qkv_bias[0:1, p * D : (p + 1) * D]
                q_all[b, p] = jnp.concatenate([part[:, 0:128].astype(BF16) * jnp.array(0.125, BF16), zeros], 0)
                k_all[b, p] = part[:, 128:256].astype(BF16)
                v_all[b, p] = part[:, 256:384].astype(BF16)
                v_turned[p] = part[:, 256:384].T.astype(BF16)

            weight[...] = policy_lanes(keep, length, b)
            row_id = iota((ROWS, 128), 0)
            lane_id = iota((ROWS, 128), 1)

            def pair(p):
                k_pair = k_all[b, p]
                vt = v_turned[p]
                tiles = [slice(128 * t, 128 * (t + 1)) for t in range(3)]
                where = slice(p * 128, (p + 1) * 128)

                def soft(t, s):
                    top = jnp.max(s, 0, keepdims=True)
                    w = jnp.where(row_id == lane_id + 128 * t, 1.0, weight[...])
                    e = jnp.exp(s - top) * jnp.concatenate([w, w], 1)
                    total = jnp.sum(e, 0, keepdims=True)
                    lse_all[b, p, t, 0:1, :] = top + jnp.log(total)
                    return e.astype(BF16), 1.0 / total

                def score(t):
                    return dot_nt(k_pair, split_heads(q_all[b, p, tiles[t], :]))

                def mix(t, e, inverse):
                    o = diagonal_blocks(dot_nn(vt, e) * inverse).astype(BF16)
                    o_turned[b, where, tiles[t]] = o

                s0 = score(0)
                s1 = score(1)
                e0 = soft(0, s0)
                s2 = score(2)
                e1 = soft(1, s1)
                mix(0, *e0)
                e2 = soft(2, s2)
                mix(1, *e1)
                mix(2, *e2)

            for p in range(PAIRS):
                pair(p)
            x1 = x + dot_tn(o_turned[b], w_proj[...])[:ROWS] + vec(V_PROJ_BIAS)
            x1_all[rows_of(b), :] = x1
            x2_all[rows_of(b), :] = x1 + vec(V_DOWN_BIAS)
            dn2_all[rows_of(b), :] = jnp.zeros((ROWS, D), F32)
            xhat2, _ = normalise(x1)
            n2_all[rows_of(b), :] = (xhat2 * vec(V_TWO_GAIN) + vec(V_TWO_SHIFT)).astype(BF16)
            valid = (iota((ROWS, D), 0) < length).astype(F32)
            g = load_padded(cotangent, b) * valid
            gd_all[rows_of(b), :] = g.astype(BF16)
            acc_vec[A_DOWN_BIAS : A_DOWN_BIAS + 1, :] += column_sum(g)
            return 0

        lax.fori_loop(0, IMG, attend, 0)
        run(count_steps[1:2])

        for n in range(PARTS):
            columns = slice(n * PART, (n + 1) * PART)

            def mlp(h):
                rows = slice(h * HALF, (h + 1) * HALF)
                n2 = n2_all[rows, :]
                g_d = gd_all[rows, :]
                u, slope = gelu_pair(dot_nn(n2, w_up[:, columns]) + vecs[V_UP_BIAS : V_UP_BIAS + 1, columns])
                u = u.astype(BF16)
                gu = (slope * dot_nt(g_d, w_down[columns, :])).astype(BF16)
                up_part[rows, :] = u
                gup_part[rows, :] = gu
                acc_small[A_UP_BIAS : A_UP_BIAS + 1, columns] += column_sum(gu.astype(F32))
                x2_all[rows, :] += dot_nn(u, w_down[columns, :])
                dn2_all[rows, :] += dot_nt(gu, w_up[:, columns])

            for h in range(4):
                mlp(h)
                if h % 2:
                    tick(f"part{n}.{h // 2}")

            base = starts[f"m{n}"]
            up = dot_tn(n2_all[...], gup_part[...])
            for c in range(PART // 128):
                buffer[base + c * D : base + (c + 1) * D, :] = up[:, c * 128 : (c + 1) * 128]
            put(buffer, base + 1536, 3, dot_tn(up_part[...], gd_all[...]))
            tick(f"part{n}")

        run(count_steps[2:3])

        def descend(b):
            length = length_of(groups, b)
            valid = (iota((ROWS, D), 0) < length).astype(F32)
            mixed[b] = (x2_all[rows_of(b), :] * valid)[:SLOT].astype(BF16)
            xhat2, rstd2 = normalise(x1_all[rows_of(b), :])
            dn2 = dn2_all[rows_of(b), :]
            acc_vec[A_TWO_GAIN : A_TWO_GAIN + 1, :] += column_sum(dn2 * xhat2)
            acc_vec[A_TWO_SHIFT : A_TWO_SHIFT + 1, :] += column_sum(dn2)
            g = load_padded(cotangent, b) * valid
            dx1 = g + normalise_back(dn2, vec(V_TWO_GAIN), xhat2, rstd2)
            dx_all[rows_of(b), :] = dx1
            g_o = dx1.astype(BF16)
            acc_vec[A_PROJ_BIAS : A_PROJ_BIAS + 1, :] += column_sum(g_o.astype(F32))
            d_o = dot_nt(g_o, w_proj[...]).astype(BF16)
            zeros = jnp.zeros((WIDE - ROWS, 128), BF16)
            for p in range(PAIRS):
                do_all[b, p] = jnp.concatenate([d_o[:, p * 128 : (p + 1) * 128], zeros], 0)

        for b in range(IMG):
            descend(b)
            tick(f"descend{b}")
        leaving[0].start()

        below = jnp.zeros((WIDE - ROWS, D), BF16)
        grad_proj = jnp.zeros((D, D), F32)
        for b in range(IMG):
            grad_proj += dot_nn(o_turned[b], jnp.concatenate([dx_all[rows_of(b), :].astype(BF16), below], 0))
        put(buffer, starts["proj"], 3, grad_proj)
        run(count_steps[3:])
        tick("proj")

    pl.run_scoped(
        first_half,
        pltpu.VMEM((ALL, D), F32),
        pltpu.VMEM((ALL, D), F32),
        pltpu.VMEM((ALL, D), BF16),
        pltpu.VMEM((ALL, D), BF16),
        pltpu.VMEM((ALL, PART), BF16),
        pltpu.VMEM((ALL, PART), BF16),
        pltpu.VMEM((ROWS, 128), F32),
    )
    coefficient = counts[2:3, 0:1]

    def second_half(acc_policy, h0_all, ga_all, z_all, g1_all, m1_all, g2_all, m2_all, gl_all, dqkv_all, mid_one,
                    mid_two, low_one):
        acc_policy[...] = jnp.zeros_like(acc_policy)
        row_id = iota((ROWS, 128), 0)
        lane_id = iota((ROWS, 128), 1)

        for p in range(PAIRS):
            def attend(b):
                policy = policy_lanes(keep, length_of(groups, b), b)
                k_pair = k_all[b, p]
                v_pair = v_all[b, p]
                kt = k_pair.T
                tiles = [slice(128 * t, 128 * (t + 1)) for t in range(3)]
                q_two = [split_heads(q_all[b, p, tile, :]) for tile in tiles]
                do_two = [split_heads(do_all[b, p, tile, :]) for tile in tiles]

                def score(t):
                    return dot_nt(k_pair, q_two[t]), dot_nt(v_pair, do_two[t])

                def soft(t, s, dp):
                    f = jnp.exp(s - lse_all[b, p, t, 0:1, :])
                    same = row_id == lane_id + 128 * t
                    w = jnp.where(same, 1.0, policy)
                    prob = f * jnp.concatenate([w, w], 1)
                    centred = dp - jnp.sum(prob * dp, 0, keepdims=True)
                    dw = f * centred
                    acc_policy[b] += jnp.where(same, 0.0, dw[:, :128] + dw[:, 128:])
                    return prob.astype(BF16), (prob * centred).astype(BF16)

                def query(t, ds):
                    dq = diagonal_blocks(dot_nn(kt, ds)).T * 0.125
                    count = min(128, ROWS - 128 * t)
                    first = b * ROWS + 128 * t
                    dqkv_all[pl.ds(first, count), p * D : p * D + 128] = dq[:count].astype(BF16)

                s0 = score(0)
                s1 = score(1)
                p0, d0 = soft(0, *s0)
                s2 = score(2)
                p1, d1 = soft(1, *s1)
                query(0, d0)
                p2, d2 = soft(2, *s2)
                query(1, d1)
                dv = dot_nn(jnp.concatenate([p0, p1, p2], 1), jnp.concatenate(do_two, 0))
                dk = dot_nn(jnp.concatenate([d0, d1, d2], 1), jnp.concatenate(q_two, 0))
                query(2, d2)
                dqkv_all[rows_of(b), p * D + 128 : p * D + 256] = dk.astype(BF16)
                dqkv_all[rows_of(b), p * D + 256 : p * D + 384] = dv.astype(BF16)

            for b in range(IMG):
                attend(b)
                tick(f"pair{p}.{b}")
            dqkv = dqkv_all[:, p * D : (p + 1) * D]
            base = starts[f"qkv{p}"]
            grad = dot_tn(n1_all[...], dqkv)
            for c in range(3):
                buffer[base + c * D : base + (c + 1) * D, :] = grad[:, c * 128 : (c + 1) * 128]
            bias = column_sum(dqkv.astype(F32))
            acc_vec[A_QUERY_BIAS : A_QUERY_BIAS + 1, p * 128 : (p + 1) * 128] = bias[:, 0:128]
            acc_vec[A_VALUE_BIAS : A_VALUE_BIAS + 1, p * 128 : (p + 1) * 128] = bias[:, 256:384]
            tick(f"qkv{p}")

        spatial_of, share_of = {}, {}

        def predict(b):
            length = length_of(groups, b)
            rows = rows_of(b)
            dpolicy = jnp.sum(acc_policy[b], 1, keepdims=True)
            xhat, _ = normalise(load_padded(tokens, b))
            h0 = (xhat * vec(V_PRED_GAIN) + vec(V_PRED_SHIFT)).astype(BF16)
            h0_all[rows, :] = h0
            position = iota((ROWS, 1), 0)
            spatial = jnp.where((position > 0) & (position < length), 1.0, 0.0)
            share = 1.0 / (length - 1).astype(F32)
            act, act_slope = gelu_pair(dot_nn(h0, w_in[...]) + vec(V_IN_BIAS))
            pooled = column_sum(act * spatial) * share
            local = iota((ROWS, D), 1) < D // 2
            z = jnp.where(local, act, pooled).astype(BF16)
            z_all[rows, :] = z
            m1, m1_slope = gelu_pair(dot_nn(z, w_mid[...]) + vec(V_MID_BIAS, 256))
            m1 = m1.astype(BF16)
            m1_all[rows, :] = m1
            m2, m2_slope = gelu_pair(dot_nn(m1, w_low[...]) + vec(V_LOW_BIAS, 128))
            m2 = m2.astype(BF16)
            m2_all[rows, :] = m2
            logits = dot_nt(m2, w_out[...]) + vec(V_OUT_BIAS, 128)
            keep_prob = 1.0 / (1.0 + jnp.exp(logits[:, 1:2] - logits[:, 0:1]))
            drop_prob = 1.0 / (1.0 + jnp.exp(logits[:, 0:1] - logits[:, 1:2]))
            dlog = spatial * (dpolicy + coefficient * spatial) * keep_prob * drop_prob
            lane = iota((ROWS, 128), 1)
            g_l = jnp.where(lane == 0, dlog, jnp.where(lane == 1, -dlog, 0.0)).astype(BF16)
            gl_all[rows, :] = g_l
            g_2 = (m2_slope * dot_nn(g_l, w_out[...])).astype(BF16)
            g2_all[rows, :] = g_2
            g_1 = (m1_slope * dot_nt(g_2, w_low[...])).astype(BF16)
            g1_all[rows, :] = g_1
            dz = dot_nt(g_1, w_mid[...])
            da = jnp.where(local, dz, spatial * share * column_sum(dz))
            g_a = (act_slope * da).astype(BF16)
            ga_all[rows, :] = g_a
            acc_vec[A_IN_BIAS : A_IN_BIAS + 1, :] += column_sum(g_a.astype(F32))
            acc_small[A_MID_BIAS : A_MID_BIAS + 1, 0:256] += column_sum(g_1.astype(F32))
            acc_small[A_LOW_BIAS : A_LOW_BIAS + 1, 0:128] += column_sum(g_2.astype(F32))
            acc_small[A_OUT_BIAS : A_OUT_BIAS + 1, 0:128] += column_sum(g_l.astype(F32))

        for b in range(IMG):
            predict(b)
            tick(f"predict{b}")


        base = starts["pred"]
        put(buffer, base, 3, dot_tn(h0_all[...], ga_all[...]))
        grad_mid = dot_tn(z_all[...], g1_all[...])
        mid_one[...] = grad_mid[:, 0:128]
        mid_two[...] = grad_mid[:, 128:256]
        lane = iota((192, 128), 1)
        odd = pltpu.roll(mid_one[pl.ds(1, 192, stride=2), :], 64, 1)
        buffer[pl.ds(base + ROW_MID, 192, stride=3), :] = mid_one[pl.ds(0, 192, stride=2), :]
        buffer[pl.ds(base + ROW_MID + 1, 192, stride=3), :] = jnp.where(
            lane < 64, mid_two[pl.ds(0, 192, stride=2), :], odd
        )
        buffer[pl.ds(base + ROW_MID + 2, 192, stride=3), :] = jnp.where(
            lane < 64, odd, pltpu.roll(mid_two[pl.ds(1, 192, stride=2), :], 64, 1)
        )
        low_one[...] = dot_tn(m1_all[...], g2_all[...])
        lane = iota((48, 128), 1)
        r0, r1, r2, r3 = (low_one[pl.ds(s, 48, stride=4), :] for s in range(4))
        r1, r2, r3 = pltpu.roll(r1, 96, 1), pltpu.roll(r2, 64, 1), pltpu.roll(r3, 32, 1)
        buffer[pl.ds(base + ROW_LOW, 48, stride=3), :] = jnp.where(lane < 96, r0, r1)
        buffer[pl.ds(base + ROW_LOW + 1, 48, stride=3), :] = jnp.where(lane < 64, r1, r2)
        buffer[pl.ds(base + ROW_LOW + 2, 48, stride=3), :] = jnp.where(lane < 32, r2, r3)
        m2_doubled = dot_nn(m2_all[...], doubling()).astype(BF16)
        both = dot_tn(gl_all[...], m2_doubled)
        head = jnp.where(iota((1, 256), 1) % 2 == 0, both[0:1, :], both[1:2, :])
        buffer[base + ROW_OUT : base + ROW_OUT + 1, :] = head[:, 0:128]
        buffer[base + ROW_OUT + 1 : base + ROW_OUT + 2, :] = pltpu.roll(head[:, 128:256], 64, 1)
        tick("pred")

        def finish(b):
            rows = rows_of(b)
            xhat, rstd = normalise(load_padded(tokens, b))
            dh0 = dot_nt(ga_all[rows, :], w_in[...])
            acc_vec[A_PRED_GAIN : A_PRED_GAIN + 1, :] += column_sum(dh0 * xhat)
            acc_vec[A_PRED_SHIFT : A_PRED_SHIFT + 1, :] += column_sum(dh0)
            dn1 = dot_nt(dqkv_all[rows, :], w_qkv[...])
            acc_vec[A_ONE_GAIN : A_ONE_GAIN + 1, :] += column_sum(dn1 * xhat)
            acc_vec[A_ONE_SHIFT : A_ONE_SHIFT + 1, :] += column_sum(dn1)
            total = (
                dx_all[rows, :]
                + normalise_back(dn1, vec(V_ONE_GAIN), xhat, rstd)
                + normalise_back(dh0, vec(V_PRED_GAIN), xhat, rstd)
            )
            input_gradient[b] = total[:SLOT].astype(BF16)

        for b in range(IMG):
            finish(b)
            tick(f"finish{b}")
        leaving[1].start()


    pl.run_scoped(
        second_half,
        pltpu.VMEM((IMG, ROWS, 128), F32),
        pltpu.VMEM((ALL, D), BF16),
        pltpu.VMEM((ALL, D), BF16),
        pltpu.VMEM((ALL, D), BF16),
        pltpu.VMEM((ALL, 256), BF16),
        pltpu.VMEM((ALL, 256), BF16),
        pltpu.VMEM((ALL, 128), BF16),
        pltpu.VMEM((ALL, 128), BF16),
        pltpu.VMEM((ALL, 128), BF16),
        pltpu.VMEM((ALL, 3 * D), BF16),
        pltpu.VMEM((D, 128), F32),
        pltpu.VMEM((D, 128), F32),
        pltpu.VMEM((256, 128), F32),
    )

    base = starts["vecs"]
    lane = iota((1, 128), 1)
    for r, a in enumerate((A_PRED_GAIN, A_PRED_SHIFT, A_IN_BIAS)):
        put_row(buffer, base + 3 * r, acc_vec[a : a + 1, :])
    mid_bias = acc_small[A_MID_BIAS : A_MID_BIAS + 1, 0:256]
    low_bias = pltpu.roll(acc_small[A_LOW_BIAS : A_LOW_BIAS + 1, 0:128], 64, 1)
    out_bias = pltpu.roll(acc_small[A_OUT_BIAS : A_OUT_BIAS + 1, 0:128], 32, 1)
    buffer[base + 9 : base + 10, :] = mid_bias[:, 0:128]
    buffer[base + 10 : base + 11, :] = jnp.where(lane < 64, mid_bias[:, 128:256], low_bias)
    buffer[base + 11 : base + 12, :] = jnp.where(lane < 32, low_bias, out_bias)
    for r, a in enumerate(
        (A_ONE_GAIN, A_ONE_SHIFT, A_QUERY_BIAS, A_VALUE_BIAS, A_PROJ_BIAS, A_TWO_GAIN, A_TWO_SHIFT)
    ):
        put_row(buffer, base + 12 + 3 * r, acc_vec[a : a + 1, :])
    put_row(buffer, base + 33, acc_small[A_UP_BIAS : A_UP_BIAS + 1, :])
    put_row(buffer, base + 45, acc_vec[A_DOWN_BIAS : A_DOWN_BIAS + 1, :])

    def settle(name, ordered):
        base = starts[name]
        if name.startswith("m"):
            n = int(name[1:])
            for c in range(4):
                ordered[pl.ds(ROW_UP + 4 * n + c, D, stride=12), :] = buffer[base + c * D : base + (c + 1) * D, :]
            ordered[ROW_DOWN + 1536 * n : ROW_DOWN + 1536 * (n + 1), :] = buffer[base + 1536 : base + 3072, :]
        elif name.startswith("qkv"):
            p = int(name[3:])
            for c in range(3):
                ordered[pl.ds(ROW_QKV + 3 * c + p, D, stride=9), :] = buffer[base + c * D : base + (c + 1) * D, :]
        else:
            first, rows = {"proj": (ROW_PROJ, 1152), "pred": (0, ROW_QKV), "vecs": (ROW_VEC, 48)}[name]
            ordered[first : first + rows, :] = buffer[base : base + rows, :]

    tick("vecs")
    owner = {}
    for name in plan:
        owner.setdefault(name if name in starts else name[:-1], []).append(name)
    settled = set()

    def hand_over(ordered):
        early = slice(ROW_PROJ // 8 * 8 + 8, ROW_VEC // 8 * 8)
        parts = (early, slice(0, early.start), slice(early.stop, GRAD_ROWS))
        copies = [pltpu.make_async_copy(ordered.at[part, :], grads.at[part, :], sem.at[i]) for i, part in enumerate(parts)]

        def look():
            for section, members in owner.items():
                if section not in settled and all(done[m] == len(plan[m]) for m in members):
                    settle(section, ordered)
                    settled.add(section)
                    if section in EARLY and all(e in settled for e in EARLY):
                        copies[0].start()

        look()
        for name in DRAIN:
            run(take(name))
            look()
        while any(done[n] < len(plan[n]) for n in plan):
            for name in plan:
                run(take(name))
            look()
        for copy in copies[1:]:
            copy.start()
        for copy in copies + leaving:
            copy.wait()

    pl.run_scoped(hand_over, pltpu.VMEM((GRAD_ROWS, 128), F32))


EARLY = ("m0", "m1", "m2", "proj")

TICKS = {
    "part0": ("m0a", "m0b", "m0c",),
    "part1.0": ("m0a", "m0b",),
    "part1.1": ("m0c",),
    "part1": ("m1",),
    "part2.1": ("m0a", "m1", "m0b",),
    "part2": ("m2",),
    "descend1": ("m0a",),
    "proj": ("proj", "m0c", "m2",),
    "pair0.1": ("proj", "m0a", "m0b",),
    "qkv0": ("qkv0",),
    "pair1.1": ("m0c", "m1", "qkv0",),
    "pair1.3": ("proj", "m0b", "m0c",),
    "qkv1": ("qkv1", "m2",),
    "pair2.0": ("m0a",),
    "pair2.1": ("m0b", "qkv1", "m0c", "qkv0",),
    "pair2.3": ("proj", "m0a",),
    "qkv2": ("qkv2a", "qkv2b", "m1",),
    "predict0": ("qkv2a", "qkv2b", "qkv1", "m2", "qkv0", "m0b", "m0c", "proj",),
    "predict2": ("m0a", "qkv1", "qkv2a", "qkv2b",),
    "predict3": ("m1", "m0a", "m2", "m0b", "qkv0",),
    "pred": ("preda", "predb", "qkv2a", "qkv2b", "m0b",),
    "finish1": ("qkv1", "preda", "proj", "m0c", "predb",),
    "finish3": ("m2", "m0c", "qkv2b",),
    "vecs": ("vecs", "qkv0",),
}
DRAIN = (
    "qkv1", "vecs", "proj", "qkv2a", "m1", "m1", "predb", "preda", "m2", "vecs", "qkv2b", "qkv0", "proj",
    "qkv1", "predb", "qkv2a", "m2", "qkv0", "qkv2b", "qkv1", "preda", "proj", "vecs", "qkv2a", "predb",
    "qkv0", "qkv2b", "m2", "proj", "qkv2a", "qkv1", "preda", "vecs", "proj", "qkv0", "qkv2b", "predb", "qkv0",
    "qkv2a", "qkv1", "predb", "qkv1", "preda", "m2", "vecs", "preda", "qkv2b", "qkv2a", "m2", "vecs", "qkv2b",
    "qkv2a",
)

(
    V_PRED_GAIN, V_PRED_SHIFT, V_IN_BIAS, V_MID_BIAS, V_LOW_BIAS, V_OUT_BIAS, V_ONE_GAIN, V_ONE_SHIFT, V_PROJ_BIAS,
    V_TWO_GAIN, V_TWO_SHIFT, V_UP_BIAS, V_DOWN_BIAS,
) = range(13)
(
    A_PRED_GAIN, A_PRED_SHIFT, A_IN_BIAS, A_ONE_GAIN, A_ONE_SHIFT, A_QUERY_BIAS, A_VALUE_BIAS, A_PROJ_BIAS, A_TWO_GAIN,
    A_TWO_SHIFT, A_DOWN_BIAS,
) = range(11)
A_UP_BIAS, A_MID_BIAS, A_LOW_BIAS, A_OUT_BIAS = range(4)


def doubling():
    return (iota((128, 256), 1) // 2 == iota((128, 256), 0)).astype(F32).astype(BF16)


CHUNK = 5952
CHUNKS = ((10944, 4800), (0, 5376), (5328, 5952))


def unpack(flat, flat_end, flat_one, rows, sems, others, w_qkv, w_proj, w_up, w_down, w_in, w_mid, w_low, w_out, vecs, qkv_bias):
    copies = [
        pltpu.make_async_copy(
            flat.at[pl.ds(start * 128, count * 128)], flat_one[i % 2].at[pl.ds(0, count * 128)], sems.at[i]
        )
        for i, (start, count) in enumerate(CHUNKS)
    ]

    def spread(i):
        copies[i].wait()

        def body(k, _):
            rows[pl.ds(pl.multiple_of(k * 192, 192), 192), :] = flat_one[i % 2][
                pl.ds(pl.multiple_of(k * 24576, 24576), 24576)
            ].reshape(192, 128)
            return 0

        lax.fori_loop(0, CHUNKS[i][1] // 192, body, 0)

    copies[0].start()
    copies[1].start()
    for copy in others:
        copy.start()
    spread(0)
    copies[2].start()
    start, count = CHUNKS[0]
    rows[count : count + 8, :] = flat_end[...].reshape(8, 128)
    for c in range(3):
        w_down[:, c * 128 : (c + 1) * 128] = shifted(rows, ROW_DOWN - 1 + c - start, MLP, 3).astype(BF16)
    lane = iota((16, 128), 1)
    at = 15697 - start
    vec_one = pltpu.roll(jnp.where(lane < 64, rows[at + 1 : at + 17, :], rows[at : at + 16, :]), 64, 1)
    lane = iota((36, 128), 1)
    at = 15708 - start
    vec_two = pltpu.roll(jnp.where(lane < 98, rows[at + 1 : at + 37, :], rows[at : at + 36, :]), 30, 1)
    rows[0:16, :] = vec_one
    rows[16:52, :] = vec_two
    for r, base in (
        (V_PRED_GAIN, 0), (V_PRED_SHIFT, 3), (V_IN_BIAS, 6), (V_ONE_GAIN, 16), (V_ONE_SHIFT, 19), (V_PROJ_BIAS, 28),
        (V_TWO_GAIN, 31), (V_TWO_SHIFT, 34), (V_DOWN_BIAS, 49),
    ):
        vecs[r : r + 1, 0:D] = row_of(rows, base, 3)
    vecs[V_UP_BIAS : V_UP_BIAS + 1, :] = row_of(rows, 37, 12)
    lane = iota((1, 128), 1)
    zero = jnp.zeros((1, 128), F32)
    r9, r10, r11 = (rows[r : r + 1, :] for r in (9, 10, 11))
    vecs[V_MID_BIAS : V_MID_BIAS + 1, 0:128] = r9
    vecs[V_MID_BIAS : V_MID_BIAS + 1, 128:256] = jnp.where(lane < 64, r10, zero)
    vecs[V_LOW_BIAS : V_LOW_BIAS + 1, 0:128] = jnp.where(
        lane < 96, pltpu.roll(jnp.where(lane < 64, r11, r10), 64, 1), zero
    )
    vecs[V_OUT_BIAS : V_OUT_BIAS + 1, 0:128] = jnp.where(lane < 2, pltpu.roll(r11, 96, 1), zero)
    for p in range(PAIRS):
        qkv_bias[0:1, p * D : p * D + 128] = rows[22 + p : 23 + p, :]
        qkv_bias[0:1, p * D + 128 : p * D + 256] = zero
        qkv_bias[0:1, p * D + 256 : p * D + 384] = rows[25 + p : 26 + p, :]

    spread(1)
    for c in range(3):
        w_in[:, c * 128 : (c + 1) * 128] = rows[pl.ds(c, D, stride=3), :].astype(BF16)
        for p in range(PAIRS):
            tile = shifted(rows, ROW_QKV - 1 + 3 * c + p, D, 9).astype(BF16)
            w_qkv[:, p * D + c * 128 : p * D + (c + 1) * 128] = tile

    a, b, c = (rows[pl.ds(ROW_MID + s, 192, stride=3), :] for s in range(3))
    lane = iota((192, 128), 1)
    zero = jnp.zeros((192, 128), F32)

    def interleave(tiles):
        count = len(tiles)
        size = tiles[0].shape[0]
        for s, tile in enumerate(tiles):
            rows[pl.ds(s, size, stride=count), :] = tile
        return rows[0 : size * count, :].astype(BF16)

    w_mid[:, 0:128] = interleave((a, pltpu.roll(jnp.where(lane < 64, c, b), 64, 1)))
    w_mid[:, 128:256] = interleave(
        (jnp.where(lane < 64, b, zero), jnp.where(lane < 64, pltpu.roll(c, 64, 1), zero))
    )
    lane = iota((48, 128), 1)
    a, b, c = (rows[pl.ds(ROW_LOW + s, 48, stride=3), :] for s in range(3))
    low = (
        a,
        jnp.where(lane < 32, pltpu.roll(a, 32, 1), pltpu.roll(b, 32, 1)),
        jnp.where(lane < 64, pltpu.roll(b, 64, 1), pltpu.roll(c, 64, 1)),
        pltpu.roll(c, 96, 1),
    )
    w_low[0:192, :] = interleave([jnp.where(lane < 96, tile, 0.0) for tile in low])
    w_low[192:256, :] = jnp.zeros((64, 128), BF16)
    head = jnp.concatenate([rows[ROW_OUT : ROW_OUT + 1, :], rows[ROW_OUT + 1 : ROW_OUT + 2, :]], 1)
    head = jnp.broadcast_to(head, (128, 256))
    lane = iota((128, 256), 1)
    chosen = (lane % 2 == iota((128, 256), 0)) & (lane < 192)
    w_out[...] = dot_nt(jnp.where(chosen, head, 0.0).astype(BF16), doubling()).astype(BF16)

    spread(2)
    start = CHUNKS[2][0]
    for c in range(3):
        w_proj[:, c * 128 : (c + 1) * 128] = shifted(rows, ROW_PROJ - 1 + c - start, D, 3).astype(BF16)
    for c in range(12):
        w_up[:, c * 128 : (c + 1) * 128] = shifted(rows, ROW_UP - 1 + c - start, D, 12).astype(BF16)


def counting(sizes, groups, keep, out, held, landed, sems):
    stages = [s for axis in ("gy", "gx", "gz") for s in whole(sizes, axis)]
    first = [0]
    for stage in stages:
        first.append(first[-1] + stage[2] - 1)

    def copies(s):
        return [
            pltpu.make_async_remote_copy(
                held.at[s], landed.at[first[s] + slot], sems.at[0, first[s] + slot], sems.at[1, first[s] + slot],
                device, MESH,
            )
            for device, slot, _ in partners(stages[s])
        ]

    def begin():
        kept = jnp.zeros((1, 1), F32)
        valid = jnp.zeros((1, 1), F32)
        position = iota((1, SLOT), 1)
        for b in range(IMG):
            spatial = jnp.where((position > 0) & (position < length_of(groups, b)), 1.0, 0.0)
            kept += jnp.sum(spatial * keep[b : b + 1, :].astype(F32), keepdims=True)
            valid += jnp.sum(spatial, keepdims=True)
        row = iota((8, 128), 0)
        held[0] = jnp.where(row == 0, kept, jnp.where(row == 1, valid, 0.0))

    def step(s):
        if s == 0:
            begin()
        else:
            total = held[s - 1]
            for slot, copy in enumerate(copies(s - 1)):
                copy.wait()
                total = total + landed[first[s - 1] + slot]
            held[s] = total
        if s < len(stages):
            for copy in copies(s):
                copy.start()
        else:
            total = held[s]
            row = iota((8, 128), 0)
            excess = total[0:1, :] / total[1:2, :] - KEEP_TARGET
            loss = RATIO_WEIGHT * total[1:2, :] * excess * excess
            out[...] = jnp.where(row == 2, 2.0 * RATIO_WEIGHT * excess, jnp.where(row == 3, loss, total))

    return [functools.partial(step, s) for s in range(len(stages) + 1)]


def layer(sizes, *operands):
    pieces, starts, rows = pieces_of(sizes)
    copies = max(sum(p.copies for p in pieces), 1)
    fits = rows <= 17408
    small = max(sum(sizes[a] - 1 for a in AXES), 1)
    vmem = pl.BlockSpec(memory_space=pltpu.VMEM)
    hbm = pl.BlockSpec(memory_space=pltpu.HBM)
    shape = jax.ShapeDtypeStruct
    return pl.pallas_call(
        functools.partial(layer_kernel, sizes, pieces, starts),
        grid=(1,),
        out_shape=(
            shape((IMG, SLOT, D), BF16),
            shape((IMG, SLOT, D), BF16),
            pltpu.VMEM((GRAD_ROWS, 128), F32) if fits else shape((GRAD_ROWS, 128), F32),
            shape((8, 128), F32),
        ),
        in_specs=[
            hbm, hbm, hbm, hbm, hbm,
            pl.BlockSpec((1024,), lambda i: (NPARAM // 1024,)),
        ],
        out_specs=[hbm, hbm, pl.BlockSpec(memory_space=pl.ANY), vmem],
        scratch_shapes=[
            pltpu.VMEM((D, 3 * D), BF16),
            pltpu.VMEM((D, D), BF16),
            pltpu.VMEM((D, MLP), BF16),
            pltpu.VMEM((MLP, D), BF16),
            pltpu.VMEM((D, D), BF16),
            pltpu.VMEM((D, 256), BF16),
            pltpu.VMEM((256, 128), BF16),
            pltpu.VMEM((128, 128), BF16),
            pltpu.VMEM((16, MLP), F32),
            pltpu.VMEM((8, 3 * D), F32),
            pltpu.VMEM((IMG, PAIRS, WIDE, 128), BF16),
            pltpu.VMEM((IMG, PAIRS, ROWS, 128), BF16),
            pltpu.VMEM((IMG, PAIRS, ROWS, 128), BF16),
            pltpu.VMEM((IMG, PAIRS, WIDE, 128), BF16),
            pltpu.VMEM((IMG, PAIRS, 3, 8, 256), F32),
            pltpu.VMEM((PAIRS, 128, ROWS), BF16),
            pltpu.VMEM((IMG, D, WIDE), BF16),
            pltpu.VMEM((ALL, D), BF16),
            pltpu.VMEM((ALL, D), F32),
            pltpu.VMEM((16, D), F32),
            pltpu.VMEM((8, MLP), F32),
            pltpu.VMEM((rows, 128), F32),
            pltpu.VMEM((rows, 128), F32),
            pltpu.SemaphoreType.DMA((4, copies)),
            pltpu.SemaphoreType.REGULAR((max(sum(len(p.stages) for p in pieces), 1),)),
            pltpu.VMEM((4, 8, 128), F32),
            pltpu.VMEM((small, 8, 128), F32),
            pltpu.SemaphoreType.DMA((2, small)),
            pltpu.SemaphoreType.DMA((3,)),
            pltpu.SMEM((IMG,), jnp.int32),
            pltpu.VMEM((IMG, SLOT, D), BF16),
            pltpu.VMEM((IMG, SLOT, D), BF16),
            pltpu.VMEM((IMG, SLOT), jnp.int32),
            pltpu.SemaphoreType.DMA((4,)),
            pltpu.VMEM((IMG, SLOT, D), BF16),
            pltpu.VMEM((IMG, SLOT, D), BF16),
            pltpu.SemaphoreType.DMA((2,)),
        ],
        compiler_params=pltpu.CompilerParams(
            collective_id=0, has_side_effects=True, vmem_limit_bytes=(95 if fits else 116) << 19
        ),
        name="layer",
    )(*operands)


UPDATE_ROWS = 4032


def update_kernel(
    grads, after, counts, mixed_in, gradient_in, params, momentum, average,
    new_params, new_momentum, new_average, mixed, input_gradient, loss, block, joined,
):
    i = pl.program_id(0)
    n = UPDATE_ROWS
    mixed[...] = mixed_in[...]
    input_gradient[...] = gradient_in[...]
    loss[0, 0] = counts[3, 0]
    joined[0:n, :] = grads[...]
    joined[n : n + 8, :] = after[...]
    here = joined[0:n, :]
    row = iota((n, 128), 0) + i * n
    lane = iota((n, 128), 1)
    moved = pltpu.roll(jnp.where(lane < 64, joined[1 : n + 1, :], here), 64, 1)
    flat = jnp.where(row < ROW_QKV - 1, here, moved)
    joined[0:n, :] = flat

    @pl.when(i == pl.num_programs(0) - 1)
    def _():
        first = 15708 - (NPARAM // (n * 128)) * n
        lane = iota((40, 128), 1)
        one = grads[first + 1 : first + 41, :]
        two = grads[first + 2 : first + 42, :]
        tail = pltpu.roll(jnp.where(lane < 30, two, one), 98, 1)
        keep_old = (iota((40, 128), 0) == 0) & (lane < 98)
        joined[first : first + 40, :] = jnp.where(keep_old, joined[first : first + 40, :], tail)
        block[...] = grads[first + 2 : first + 38, :].reshape(4608)

    g = joined[0:n, :].reshape(n * 128)
    moment = MOMENTUM_DECAY * momentum[...] + g
    value = params[...] - LEARN_RATE * (g + MOMENTUM_DECAY * moment)
    new_momentum[...] = moment
    new_params[...] = value
    new_average[...] = AVERAGE_DECAY * average[...] + (1.0 - AVERAGE_DECAY) * value


def update(grads, counts, mixed, input_gradient, params, momentum, average):
    n = UPDATE_ROWS
    flat = pl.BlockSpec((n * 128,), lambda i: (i,))
    image = pl.BlockSpec((1, SLOT, D), lambda i: (jnp.minimum(i, IMG - 1), 0, 0))
    out = jax.ShapeDtypeStruct((NPARAM,), F32)
    return pl.pallas_call(
        update_kernel,
        grid=(pl.cdiv(NPARAM, n * 128),),
        out_shape=(
            out, out, out,
            jax.ShapeDtypeStruct(mixed.shape, BF16),
            jax.ShapeDtypeStruct(mixed.shape, BF16),
            jax.ShapeDtypeStruct((1, 1), F32),
            jax.ShapeDtypeStruct((4608,), F32),
        ),
        in_specs=[
            pl.BlockSpec((n, 128), lambda i: (i, 0)),
            pl.BlockSpec((8, 128), lambda i: ((i + 1) * (n // 8), 0)),
            pl.BlockSpec((8, 128), lambda i: (0, 0)),
            image,
            image,
            flat,
            flat,
            flat,
        ],
        out_specs=[
            flat, flat, flat, image, image,
            pl.BlockSpec(memory_space=pltpu.SMEM),
            pl.BlockSpec((4608,), lambda i: (0,)),
        ],
        scratch_shapes=[pltpu.VMEM((n + 8, 128), F32)],
        compiler_params=pltpu.CompilerParams(vmem_limit_bytes=28 << 20),
        name="update",
    )(
        grads, grads,
        *(pltpu.with_memory_space_constraint(x, pltpu.HBM) for x in (counts, mixed, input_gradient)),
        params,
        *(pltpu.with_memory_space_constraint(x, pltpu.HBM) for x in (momentum, average)),
    )


GRAD_ROWS = -(-(NPARAM // 128 + 40) // UPDATE_ROWS) * UPDATE_ROWS + 8


def solution(mesh):
    sizes = dict(mesh.shape)

    def per_device(tokens, cotangent, groups, keep_mask, params, momentum, average):
        mixed, input_gradient, grads, counts = layer(sizes, groups, tokens, cotangent, keep_mask, params, params)
        new_params, new_momentum, new_average, mixed, input_gradient, loss, block = update(
            grads, counts, mixed, input_gradient, params, momentum, average
        )
        return (mixed, input_gradient, loss.reshape(()), new_params, new_momentum, new_average, block)

    split = P(("gx", "gy", "gz"))
    return jax.shard_map(
        per_device,
        mesh=mesh,
        in_specs=(split, split, split, split, P(), P(), P()),
        out_specs=(split, split, P(), P(), P(), P(), P()),
        check_vma=False,
    )
```
